512 devices in a mesh: gx: 16 (over z, y_hi), gy: 32 (over x, y_lo, core).
Axes of the slice: x: 4, y: 8 (y_hi: 2, y_lo: 4; y = y_hi * 4 + y_lo), z: 8, core: 2. Of those that a mesh axis runs over, the one named last changes fastest.
Arguments:
- voxel_material: int32 [1, 4096, 4096], P(None, 'gx', 'gy'), may hold values 0 or 1
- wetted_indicator: int32 [1, 4096, 4096], P(None, 'gx', 'gy'), may hold values 0 or 1
- starting_deficit_map: float32 [1, 4096, 4096], P(None, 'gx', 'gy'), may hold values from -6 to 6
- applied_thermal_slope: float32 [1, 2], replicated, may hold values from -4 to 4
Outputs:
- phase: float32 [1, 4096, 4096], P(None, 'gx', 'gy')
- heat: float32 [1, 4096, 4096], P(None, 'gx', 'gy')
- gradient: float32 [2, 1, 4096, 4096], P(None, None, 'gx', 'gy')
The draws below stay inside these ranges and needn't reach their ends.
All inputs are finite; a program needn't handle non-finite values. No bound on the sum of `voxel_material` or of `wetted_indicator` on one device may be relied on, other than what follows from the above.
Results may differ from the reference program's by a relative error of at most 0.0001.
Values sent between devices are 32-bit elements; how exact they have to be, the bound alone decides.
No kernel may reach another device: no remote copies, remote signals or barrier semaphores. Data moves between devices by JAX's collectives and lax.ppermute only.
A program may use at most 64 MiB of HBM per device.

```python
import jax
import jax.numpy as jnp

SHEET_TOTAL = 1
GRID_ALONG_X = 4096
GRID_ALONG_Y = 4096


def place_ends(result, rng, low, largest):
    longest = result.shape.index(max(result.shape))
    spots = []
    for shift in (0, 1):
        where = [jax.random.randint(jax.random.fold_in(rng, axis), (), 0, length) for axis, length in enumerate(result.shape)]
        where[longest] = (where[longest] + shift) % result.shape[longest]
        spots.append(tuple(where))
    return result.at[spots[0]].set(low).at[spots[1]].set(largest)


def shard_levels(stream_key, shape, pieces, low, largest):
    def one(dim, shards_of):
        heights = jax.random.uniform(jax.random.fold_in(jax.random.fold_in(stream_key, 6), dim), (shards_of,), jnp.float32, low / len(pieces), largest / len(pieces))
        return jnp.repeat(jnp.exp(heights), shape[dim] // shards_of).reshape((-1,) + (1,) * (len(shape) - dim - 1))

    factor_of = one(*pieces[0])
    for cut in pieces[1:]:
        factor_of = factor_of * one(*cut)
    return factor_of


def scatter_about(stream_key, shape, scale, bound, split=(), kind=jnp.bfloat16):
    loudness = shard_levels(stream_key, shape, split, -0.22, 0.18) if split else 1.0
    array = jax.random.normal(stream_key, shape, jnp.float32) * scale * loudness
    return jnp.minimum(jnp.maximum(array, -bound), bound).astype(kind)


def setup_inputs(seed: int = 0) -> dict:
    arg_keys = jax.random.split(jax.random.key(seed), 5)
    return {
        "voxel_material": place_ends((jax.random.randint(arg_keys[0], (SHEET_TOTAL, GRID_ALONG_X, GRID_ALONG_Y), 0, 4) < 3).astype(jnp.int32), jax.random.fold_in(arg_keys[0], 1), 0, 1),
        "wetted_indicator": place_ends((jax.random.randint(arg_keys[1], (SHEET_TOTAL, GRID_ALONG_X, GRID_ALONG_Y), 0, 3) < 1).astype(jnp.int32), jax.random.fold_in(arg_keys[1], 1), 0, 1),
        "starting_deficit_map": scatter_about(arg_keys[2], (SHEET_TOTAL, GRID_ALONG_X, GRID_ALONG_Y), 1.0, 6.0, ((1, 16), (2, 32)), jnp.float32),
        "applied_thermal_slope": scatter_about(arg_keys[3], (SHEET_TOTAL, 2), 1.0, 4.0, (), jnp.float32),
    }


solid_conduct = 1.7
gas_conduct = 0.026
liquid_conduct = 0.6
reference_conduct = 0.863
step_grad = 0.1
step_well = 0.3
step_drive = 0.2
step_heat = 0.12
latent_heat = 0.5
gradient_gain = 0.5


def laplace_full(field):
    padded = jnp.pad(field, 1)
    inplane = padded[1:-1, 2:, 1:-1] + padded[1:-1, :-2, 1:-1] + padded[1:-1, 1:-1, 2:] + padded[1:-1, 1:-1, :-2]
    across = padded[2:, 1:-1, 1:-1] + padded[:-2, 1:-1, 1:-1]
    return inplane + across - 6.0 * field


def progress_clock_increment(phase, heat, woven_backing_mesh):
    well = 2.0 * phase * (1.0 - phase) * (1.0 - 2.0 * phase)
    growth = 30.0 * phase * phase * (1.0 - phase) * (1.0 - phase)
    new_phase = woven_backing_mesh * (phase + step_grad * laplace_full(phase) - step_well * well + step_drive * heat * growth)
    new_heat = heat + step_heat * laplace_full(heat) - latent_heat * (new_phase - phase)
    return new_phase, new_heat


def wave_numbers(count, scalar_datatype):
    index = jnp.arange(count, dtype=jnp.int32)
    signed = jnp.where(index >= count // 2, index - count, index)
    return signed.astype(scalar_datatype), index == count // 2


def reference(voxel_material, wetted_indicator, starting_deficit_map, applied_thermal_slope):
    scalar_datatype = starting_deficit_map.dtype
    woven_backing_mesh = voxel_material.astype(scalar_datatype)
    previous_liquid_fraction = woven_backing_mesh * wetted_indicator.astype(scalar_datatype)
    coming_liquid_fraction, coming_warmth_values = progress_clock_increment(previous_liquid_fraction, starting_deficit_map, woven_backing_mesh)
    condensate_level2, warmth_level2 = progress_clock_increment(coming_liquid_fraction, coming_warmth_values, woven_backing_mesh)
    warmth_boundary_strip = jnp.pad(coming_warmth_values, ((0, 0), (1, 1), (1, 1)))
    grad_x = gradient_gain * (warmth_boundary_strip[:, 2:, 1:-1] - warmth_boundary_strip[:, :-2, 1:-1])
    grad_y = gradient_gain * (warmth_boundary_strip[:, 1:-1, 2:] - warmth_boundary_strip[:, 1:-1, :-2])
    start_x = applied_thermal_slope[:, 0][:, None, None] + grad_x
    start_y = applied_thermal_slope[:, 1][:, None, None] + grad_y
    conduct = woven_backing_mesh * (gas_conduct + (liquid_conduct - gas_conduct) * condensate_level2) + (1.0 - woven_backing_mesh) * solid_conduct
    contrast = conduct - reference_conduct
    polar_x = contrast * start_x
    polar_y = contrast * start_y
    xwave, xnyquist = wave_numbers(GRID_ALONG_X, scalar_datatype)
    ywave, ynyquist = wave_numbers(GRID_ALONG_Y, scalar_datatype)
    xwave = xwave[:, None]
    ywave = ywave[None, :]
    valid = (~xnyquist)[:, None] & (~ynyquist)[None, :] & ((xwave != 0.0) | (ywave != 0.0))
    denom = reference_conduct * jnp.maximum(xwave * xwave + ywave * ywave, 1.0)
    coef_x = jnp.where(valid, xwave / denom, 0.0)
    coef_y = jnp.where(valid, ywave / denom, 0.0)
    results_x = []
    results_y = []
    for layer in range(SHEET_TOTAL):
        spec_x = jnp.fft.fft2(polar_x[layer])
        spec_y = jnp.fft.fft2(polar_y[layer])
        along = xwave * spec_x + ywave * spec_y
        results_x.append(applied_thermal_slope[layer, 0] - jnp.real(jnp.fft.ifft2(coef_x * along)))
        results_y.append(applied_thermal_slope[layer, 1] - jnp.real(jnp.fft.ifft2(coef_y * along)))
    gradient = jnp.stack([jnp.stack(results_x), jnp.stack(results_y)])
    return condensate_level2, warmth_level2, gradient
```

```python
import functools
import math

import jax
import jax.numpy as jnp
import numpy as np
from jax import lax
from jax.experimental import pallas as pl
from jax.experimental.pallas import tpu as pltpu
from jax.sharding import Mesh
from jax.sharding import PartitionSpec as P

solid_conduct = 1.7
gas_conduct = 0.026
liquid_conduct = 0.6
reference_conduct = 0.863
step_grad = 0.1
step_well = 0.3
step_drive = 0.2
step_heat = 0.12
latent_heat = 0.5
gradient_gain = 0.5
highest = lax.Precision.HIGHEST

TILE_ROWS = 256
TILE_COLS = 128
EDGE = 8
TALL = TILE_ROWS + 2 * EDGE
WIDE = 384
OUTER = 32
SLAB = 16
CHIPS = 256
COLS = 4096
ROWS = 4096
VMEM = pl.BlockSpec(memory_space=pltpu.VMEM)
SMEM = pl.BlockSpec(memory_space=pltpu.SMEM)


def dot(left, right, contract=((1,), (0,))):
    return lax.dot_general(
        left, right, (contract, ((), ())), precision=highest, preferred_element_type=jnp.float32
    )


def call(kernel, outs, *args, smem=()):
    shapes = [jax.ShapeDtypeStruct(shape, jnp.float32) for shape in outs]
    return pl.pallas_call(
        kernel,
        out_shape=shapes,
        in_specs=[SMEM if i in smem else VMEM for i in range(len(args))],
        out_specs=[VMEM] * len(outs),
        compiler_params=pltpu.CompilerParams(vmem_limit_bytes=32 * 1024 * 1024),
    )(*args)


def angles(left, right, length):
    product = np.outer(np.arange(left), np.arange(right)) % length
    return 2.0 * math.pi / length * product


def table(array):
    return jnp.asarray(np.asarray(array, dtype=np.float32))


def column_tables():
    first = angles(OUTER, OUTER, OUTER)
    second = angles(64, 128, 128)
    twist = angles(OUTER, 128, COLS)
    cosine, sine = np.cos(second), np.sin(second)
    forward_first = np.concatenate([np.cos(first), -np.sin(first)], axis=0)
    forward_second = np.block([[cosine, sine], [-sine, cosine]])
    backward_second = np.block([[cosine, sine], [-sine, cosine]])
    backward_first = np.concatenate([np.cos(first), -np.sin(first)], axis=1)
    return forward_first, forward_second, backward_first, backward_second, np.cos(twist), np.sin(twist)


def row_tables():
    first = angles(CHIPS, CHIPS, CHIPS)
    second = angles(SLAB, SLAB, SLAB)
    twist = np.repeat(angles(CHIPS, SLAB, ROWS), 8, axis=1)
    cosine, sine = np.kron(np.cos(second), np.eye(8)), np.kron(np.sin(second), np.eye(8))
    both = np.concatenate([np.cos(first), np.sin(first)], axis=0)
    forward = np.block([[cosine, -sine], [sine, cosine]])
    backward = np.block([[cosine, sine], [-sine, cosine]])
    return both, forward, backward, np.cos(twist), np.sin(twist)


def extend(voxel, wetted, heat, above, below):
    porous = voxel[...].astype(jnp.float32)
    phase = porous * wetted[...].astype(jnp.float32)
    middle = (porous, phase, heat[...])
    return [jnp.concatenate([above[f], middle[f], below[f]], axis=0) for f in range(3)]


def edge_kernel(voxel, wetted, heat, above, below, left, right):
    spare = jnp.zeros((WIDE - TALL, TILE_COLS), jnp.float32)
    for f, field in enumerate(extend(voxel, wetted, heat, above, below)):
        flipped = jnp.concatenate([field, spare], axis=0).T
        left[f] = flipped[:EDGE]
        right[f] = flipped[TILE_COLS - EDGE :]


def progress(phase, heat, porous, phase_lap, heat_lap):
    well = 2.0 * phase * (1.0 - phase) * (1.0 - 2.0 * phase)
    growth = 30.0 * phase * phase * (1.0 - phase) * (1.0 - phase)
    new_phase = porous * (
        phase + step_grad * phase_lap - step_well * well + step_drive * heat * growth
    )
    new_heat = heat + step_heat * heat_lap - latent_heat * (new_phase - phase)
    return new_phase, new_heat


def neighbours(field):
    tall, wide = field.shape
    return (
        pltpu.roll(field, tall - 1, 0),
        pltpu.roll(field, 1, 0),
        pltpu.roll(field, wide - 1, 1),
        pltpu.roll(field, 1, 1),
    )


def laplace(around, field):
    return around[0] + around[1] + around[2] + around[3] - 6.0 * field


def stencil_kernel(
    place, slope, voxel, wetted, heat, above, below, left, right, phase_out, heat_out, polar_out
):
    spare = jnp.zeros((TILE_COLS - 2 * EDGE, WIDE), jnp.float32)
    fields = []
    for f, field in enumerate(extend(voxel, wetted, heat, above, below)):
        side = jnp.concatenate([right[f], spare, left[f]], axis=0).T
        fields.append(jnp.concatenate([field, side[:TALL]], axis=1))
    porous, phase, warmth = fields
    row = lax.broadcasted_iota(jnp.int32, porous.shape, 0) - EDGE + TILE_ROWS * place[0]
    lane = lax.broadcasted_iota(jnp.int32, porous.shape, 1)
    column = jnp.where(lane < 192, lane, lane - 256) + TILE_COLS * place[1]
    inside = (row >= 0) & (row < ROWS) & (column >= 0) & (column < COLS)
    phase_one, heat_one = progress(
        phase, warmth, porous, laplace(neighbours(phase), phase), laplace(neighbours(warmth), warmth)
    )
    heat_one = jnp.where(inside, heat_one, 0.0)

    def centre(field):
        return field[EDGE : EDGE + TILE_ROWS, :TILE_COLS]

    phase_around = [centre(field) for field in neighbours(phase_one)]
    heat_around = [centre(field) for field in neighbours(heat_one)]
    phase_one, heat_one, porous = centre(phase_one), centre(heat_one), centre(porous)
    phase_two, heat_two = progress(
        phase_one, heat_one, porous, laplace(phase_around, phase_one), laplace(heat_around, heat_one)
    )
    phase_out[...] = phase_two
    heat_out[...] = heat_two
    start_x = slope[0, 0] + gradient_gain * (heat_around[0] - heat_around[1])
    start_y = slope[0, 1] + gradient_gain * (heat_around[2] - heat_around[3])
    conduct = (
        porous * (gas_conduct + (liquid_conduct - gas_conduct) * phase_two)
        + (1.0 - porous) * solid_conduct
    )
    contrast = conduct - reference_conduct
    polar_out[:, 0] = (contrast * start_x).reshape(TILE_ROWS // SLAB, SLAB, TILE_COLS)
    polar_out[:, 1] = (contrast * start_y).reshape(TILE_ROWS // SLAB, SLAB, TILE_COLS)


def columns_forward_kernel(data, first, second, twist_cos, twist_sin, out):
    rows = jnp.concatenate([data[pl.ds(s, OUTER, stride=SLAB), :] for s in range(SLAB)], axis=1)
    spread = dot(first[...], rows)
    cosine, sine = twist_cos[...], twist_sin[...]
    real, imag = [], []
    for s in range(SLAB):
        part = slice(s * 128, (s + 1) * 128)
        re, im = spread[:OUTER, part], spread[OUTER:, part]
        real.append(re * cosine + im * sine)
        imag.append(im * cosine - re * sine)
    for g in range(4):
        span = slice(g * 8, (g + 1) * 8)
        re = jnp.concatenate([part[span] for part in real], axis=0)
        im = jnp.concatenate([part[span] for part in imag], axis=0)
        both = jnp.concatenate([re, im], axis=1)
        final = dot(second[...], both, ((1,), (1,)))
        out[pl.ds(2 * g, 64, stride=8), :] = final[:64]
        out[pl.ds(2 * g + 1, 64, stride=8), :] = final[64:]


def columns_backward_kernel(data, first, second, twist_cos, twist_sin, out):
    real, imag = [], []
    for g in range(4):
        span = slice(g * 8, (g + 1) * 8)
        both = jnp.concatenate(
            [data[pl.ds(2 * g, 64, stride=8), :], data[pl.ds(2 * g + 1, 64, stride=8), :]], axis=0
        )
        spread = dot(both, second[...], ((0,), (0,)))
        re = spread[:, :128].reshape(SLAB, 8, 128)
        im = spread[:, 128:].reshape(SLAB, 8, 128)
        cosine, sine = twist_cos[span][None], twist_sin[span][None]
        real.append(re * cosine - im * sine)
        imag.append(im * cosine + re * sine)
    stacked = jnp.concatenate(
        [jnp.concatenate([part[s] for part in real + imag], axis=0) for s in range(SLAB)], axis=1
    )
    final = dot(first[...], stacked)
    for s in range(SLAB):
        out[pl.ds(s, OUTER, stride=SLAB), :] = final[:, s * 128 : (s + 1) * 128]


def wave_numbers(place):
    shape = (CHIPS, 128)
    kp = lax.broadcasted_iota(jnp.int32, shape, 0)
    lane = lax.broadcasted_iota(jnp.int32, shape, 1)
    row_freq = kp + CHIPS * (lane // 8)
    col_freq = 8 * place[2] + lane % 8
    row_wave = jnp.where(row_freq >= ROWS // 2, row_freq - ROWS, row_freq).astype(jnp.float32)
    return row_freq, col_freq, row_wave, col_freq.astype(jnp.float32)


def rows_forward_kernel(place, data, first, second, twist_cos, twist_sin, out):
    real = data[pl.ds(0, CHIPS, stride=2), :]
    imag = data[pl.ds(1, CHIPS, stride=2), :]
    spread = dot(first[...], jnp.concatenate([real, imag], axis=1))
    re = spread[:CHIPS, :128] + spread[CHIPS:, 128:]
    im = spread[:CHIPS, 128:] - spread[CHIPS:, :128]
    cosine, sine = twist_cos[...], twist_sin[...]
    turned = jnp.concatenate([re * cosine + im * sine, im * cosine - re * sine], axis=1)
    final = dot(turned, second[...])
    _, _, row_wave, col_wave = wave_numbers(place)
    wave = jnp.where(place[3] == 0, row_wave, col_wave)
    out[:CHIPS] = wave * final[:, :128]
    out[CHIPS:] = wave * final[:, 128:]


def rows_backward_kernel(place, mine, other, first, second, twist_cos, twist_sin, out):
    row_freq, col_freq, row_wave, col_wave = wave_numbers(place)
    valid = (
        (row_freq != ROWS // 2)
        & (col_freq != COLS // 2)
        & ((row_freq != 0) | (col_freq != 0))
    )
    denom = reference_conduct * jnp.maximum(row_wave * row_wave + col_wave * col_wave, 1.0)
    weight = jnp.where(col_freq == 0, 1.0, 2.0) / (ROWS * COLS)
    wave = jnp.where(place[3] == 0, row_wave, col_wave)
    coef = jnp.where(valid, weight * wave / denom, 0.0)
    along = mine[...] + other[...]
    green = jnp.concatenate([coef * along[:CHIPS], coef * along[CHIPS:]], axis=1)
    spread = dot(green, second[...])
    re, im = spread[:, :128], spread[:, 128:]
    cosine, sine = twist_cos[...], twist_sin[...]
    turned = jnp.concatenate([re * cosine - im * sine, im * cosine + re * sine], axis=1)
    final = dot(first[...], turned)
    out[pl.ds(0, CHIPS, stride=2), :] = final[:CHIPS, :128] - final[CHIPS:, 128:]
    out[pl.ds(1, CHIPS, stride=2), :] = final[:CHIPS, 128:] + final[CHIPS:, :128]


def exchange(array, axes, count):
    blocks = array.reshape((count, array.size // count // 128, 128))
    return lax.all_to_all(blocks, axes, split_axis=0, concat_axis=0, tiled=True)


def shift(block, axes, count, step):
    pairs = [(i, i + step) for i in range(count) if 0 <= i + step < count]
    return lax.ppermute(block, axes, pairs)


def body(voxel_material, wetted_indicator, starting_deficit_map, applied_thermal_slope):
    gx_size = lax.axis_size("gx")
    gt_size = lax.axis_size("gt")
    core_size = lax.axis_size("core")
    gy_size = gt_size * core_size
    gx_index = lax.axis_index("gx")
    gt_index = lax.axis_index("gt")
    core_index = lax.axis_index("core")
    place = jnp.stack(
        [gx_index, gt_index * core_size + core_index, gx_index * gt_size + gt_index, core_index]
    ).astype(jnp.int32)
    voxel, wetted, heat = voxel_material[0], wetted_indicator[0], starting_deficit_map[0]

    def strip(part):
        porous = voxel[part].astype(jnp.float32)
        return jnp.stack([porous, porous * wetted[part].astype(jnp.float32), heat[part]])

    above = shift(strip(slice(TILE_ROWS - EDGE, TILE_ROWS)), "gx", gx_size, 1)
    below = shift(strip(slice(0, EDGE)), "gx", gx_size, -1)
    first_columns, last_columns = call(
        edge_kernel, [(3, EDGE, WIDE)] * 2, voxel, wetted, heat, above, below
    )
    gy = ("gt", "core")
    left = shift(last_columns, gy, gy_size, 1)
    right = shift(first_columns, gy, gy_size, -1)
    phase_two, heat_two, polar = call(
        stencil_kernel,
        [
            (TILE_ROWS, TILE_COLS),
            (TILE_ROWS, TILE_COLS),
            (TILE_ROWS // SLAB, 2, SLAB, TILE_COLS),
        ],
        place, applied_thermal_slope, voxel, wetted, heat, above, below, left, right,
        smem=(0, 1),
    )
    first_to, second_to, first_back, second_back, col_cos, col_sin = map(table, column_tables())
    both, rows_to, rows_back, row_cos, row_sin = map(table, row_tables())
    chips = ("gx", "gt")
    slab = exchange(polar, gy, gy_size).reshape(-1, 128)
    (spec,) = call(
        columns_forward_kernel, [(2 * CHIPS, 128)], slab, first_to, second_to, col_cos, col_sin
    )
    spec = exchange(spec, chips, CHIPS).reshape(-1, 128)
    (mine,) = call(
        rows_forward_kernel, [(2 * CHIPS, 128)], place, spec, both, rows_to, row_cos, row_sin, smem=(0,)
    )
    other = lax.ppermute(mine, "core", [(0, 1), (1, 0)])
    (green,) = call(
        rows_backward_kernel, [(2 * CHIPS, 128)],
        place, mine, other, both, rows_back, row_cos, row_sin, smem=(0,),
    )
    green = exchange(green, chips, CHIPS).reshape(-1, 128)
    (answer,) = call(
        columns_backward_kernel, [(OUTER * SLAB, 128)], green, first_back, second_back, col_cos, col_sin
    )
    answer = exchange(answer, gy, gy_size).reshape(TILE_ROWS // SLAB, 2, SLAB, TILE_COLS)
    answer = jnp.swapaxes(answer, 0, 1).reshape(2, 1, TILE_ROWS, TILE_COLS)
    gradient = applied_thermal_slope[0][:, None, None, None] - answer
    return (phase_two[None], heat_two[None], gradient)


def solution(mesh):
    gx_size, gy_size = mesh.devices.shape
    fine = Mesh(mesh.devices.reshape(gx_size, gy_size // 2, 2), ("gx", "gt", "core"))
    gy = ("gt", "core")
    in_specs = (P(None, "gx", gy), P(None, "gx", gy), P(None, "gx", gy), P())
    out_specs = (P(None, "gx", gy), P(None, "gx", gy), P(None, None, "gx", gy))
    return jax.shard_map(body, mesh=fine, in_specs=in_specs, out_specs=out_specs, check_vma=False)
```

```python
import functools
import math

import jax
import jax.numpy as jnp
import numpy as np
from jax import lax
from jax.experimental import pallas as pl
from jax.experimental.pallas import tpu as pltpu
from jax.sharding import Mesh
from jax.sharding import PartitionSpec as P

solid_conduct = 1.7
gas_conduct = 0.026
liquid_conduct = 0.6
reference_conduct = 0.863
step_grad = 0.1
step_well = 0.3
step_drive = 0.2
step_heat = 0.12
latent_heat = 0.5
gradient_gain = 0.5

TILE_ROWS = 256
TILE_COLS = 128
EDGE = 8
SHIFT = 2
TALL = TILE_ROWS + EDGE
WIDE = 384
OUTER = 32
SLAB = 16
CHIPS = 256
COLS = 4096
ROWS = 4096
CORE_MAJOR = np.arange(OUTER).reshape(-1, 2).T.reshape(-1)
VMEM = pl.BlockSpec(memory_space=pltpu.VMEM)
SMEM = pl.BlockSpec(memory_space=pltpu.SMEM)


def halves(array):
    high = array.astype(jnp.bfloat16)
    return high, (array - high.astype(jnp.float32)).astype(jnp.bfloat16)


def dot(left, right, contract=((1,), (0,))):
    def product(x, y):
        return lax.dot_general(x, y, (contract, ((), ())), preferred_element_type=jnp.float32)

    (left_high, left_low), (right_high, right_low) = halves(left), halves(right)
    return product(left_high, right_high) + (
        product(left_high, right_low) + product(left_low, right_high)
    )


def call(kernel, outs, *args, smem=()):
    shapes = [jax.ShapeDtypeStruct(shape, jnp.float32) for shape in outs]
    spaces = [SMEM if i in smem else VMEM for i in range(len(args))]
    return pl.pallas_call(
        kernel,
        out_shape=shapes,
        in_specs=spaces,
        out_specs=[VMEM] * len(outs),
        compiler_params=pltpu.CompilerParams(vmem_limit_bytes=32 * 1024 * 1024),
    )(*args)


def angles(left, right, length):
    product = np.outer(np.arange(left), np.asarray(right)) % length
    return 2.0 * math.pi / length * product


def table(array):
    return jnp.asarray(np.asarray(array, dtype=np.float32))


def column_tables():
    first = angles(OUTER, range(OUTER), OUTER)
    cosine, sine = np.cos(first), np.sin(first)
    tables = []
    for shift in (SHIFT, 0):
        inner = np.arange(128) - shift
        second = angles(64, inner, 128)
        twist = angles(OUTER, inner, COLS)
        if shift:
            stack = np.concatenate([cosine, -sine], axis=0)
        else:
            stack = np.concatenate([cosine, -sine], axis=1)[CORE_MAJOR]
        mix = np.block([[np.cos(second), np.sin(second)], [-np.sin(second), np.cos(second)]])
        tables.append([table(array) for array in (stack, mix, np.cos(twist), np.sin(twist))])
    return tables


def row_tables():
    first = angles(CHIPS, range(CHIPS), CHIPS)
    both = table(np.concatenate([np.cos(first), np.sin(first)], axis=0))
    tables = []
    for shift, sign in ((SHIFT, -1.0), (0, 1.0)):
        inner = np.arange(SLAB) - shift
        second = angles(SLAB, inner, SLAB)
        twist = np.repeat(angles(CHIPS, inner, ROWS), 8, axis=1)
        cosine, sine = np.kron(np.cos(second), np.eye(8)), sign * np.kron(np.sin(second), np.eye(8))
        if shift:
            cosine, sine = cosine.T, sine.T
        mix = np.block([[cosine, sine], [-sine, cosine]])
        tables.append([both] + [table(array) for array in (mix, np.cos(twist), np.sin(twist))])
    return tables


def prepare_kernel(voxel, wetted, heat, porous, phase, heat_out):
    porous[...] = voxel[...].astype(jnp.float32)
    phase[...] = porous[...] * wetted[...].astype(jnp.float32)
    heat_out[...] = heat[...]


def with_above(above, porous, phase, heat):
    tops = (above[0], above[0] * above[1], above[2])
    return [
        jnp.concatenate([top, field[...]], axis=0) for top, field in zip(tops, (porous, phase, heat))
    ]


def edge_kernel(porous, phase, heat, above, strip):
    spare = jnp.zeros((WIDE - TALL, TILE_COLS), jnp.float32)
    for f, tall in enumerate(with_above(above, porous, phase, heat)):
        strip[f] = jnp.concatenate([tall, spare], axis=0).T[TILE_COLS - EDGE :]


def progress(phase, heat, porous, phase_lap, heat_lap):
    well = 2.0 * phase * (1.0 - phase) * (1.0 - 2.0 * phase)
    growth = 30.0 * phase * phase * (1.0 - phase) * (1.0 - phase)
    new_phase = porous * (
        phase + step_grad * phase_lap - step_well * well + step_drive * heat * growth
    )
    new_heat = heat + step_heat * heat_lap - latent_heat * (new_phase - phase)
    return new_phase, new_heat


def stencil_kernel(place, slope, porous, phase, heat, above, left, fields_out, polar_out):
    spare = jnp.zeros((TILE_COLS - EDGE, WIDE), jnp.float32)
    fields = []
    for f, tall in enumerate(with_above(above, porous, phase, heat)):
        side = jnp.concatenate([spare, left[f]], axis=0).T
        fields.append(jnp.concatenate([tall, side[:TALL]], axis=1))
    porous, phase, heat = fields
    wide = porous.shape[1]
    row = lax.broadcasted_iota(jnp.int32, porous.shape, 0) + TALL * place[0]
    column = lax.broadcasted_iota(jnp.int32, porous.shape, 1) + wide * place[1]
    last_row, first_row = row != EDGE - 1, row != EDGE
    last_column, first_column = column != wide - 1, column != 0

    def neighbours(field):
        return (
            jnp.where(last_row, pltpu.roll(field, TALL - 1, 0), 0.0),
            jnp.where(first_row, pltpu.roll(field, 1, 0), 0.0),
            jnp.where(last_column, pltpu.roll(field, wide - 1, 1), 0.0),
            jnp.where(first_column, pltpu.roll(field, 1, 1), 0.0),
        )

    def laplace(around, field):
        return around[0] + around[1] + around[2] + around[3] - 6.0 * field

    def shifted(field):
        field = pltpu.roll(field, SHIFT, 1)[:, :TILE_COLS]
        return pltpu.roll(field, TALL - EDGE + SHIFT, 0)[:TILE_ROWS]

    phase_lap, heat_lap = laplace(neighbours(phase), phase), laplace(neighbours(heat), heat)
    phase, heat = progress(phase, heat, porous, phase_lap, heat_lap)
    heat_around = neighbours(heat)
    phase_lap, heat_lap = laplace(neighbours(phase), phase), laplace(heat_around, heat)
    phase, heat = progress(phase, heat, porous, phase_lap, heat_lap)
    fields_out[0] = shifted(phase)
    fields_out[1] = shifted(heat)
    start_x = slope[0, 0] + gradient_gain * (heat_around[0] - heat_around[1])
    start_y = slope[0, 1] + gradient_gain * (heat_around[2] - heat_around[3])
    conduct = (
        porous * (gas_conduct + (liquid_conduct - gas_conduct) * phase)
        + (1.0 - porous) * solid_conduct
    )
    contrast = conduct - reference_conduct
    blocks = (TILE_ROWS // SLAB, SLAB, TILE_COLS)
    polar_out[:, 0] = shifted(contrast * start_x).reshape(blocks)
    polar_out[:, 1] = shifted(contrast * start_y).reshape(blocks)


def return_rows_kernel(fields, tail, fixed, strip):
    for f in range(2):
        tall = jnp.concatenate([fields[f], tail[f]], axis=0)
        whole = pltpu.roll(tall, TALL - SHIFT, 0)[:TILE_ROWS]
        fixed[f] = whole
        strip[f] = whole.T[:EDGE]


def return_columns_kernel(fixed, side, phase, heat):
    spare = jnp.zeros((TILE_COLS - EDGE, TILE_ROWS), jnp.float32)
    for f, out in enumerate((phase, heat)):
        wide = jnp.concatenate([fixed[f], jnp.concatenate([side[f], spare], axis=0).T], axis=1)
        out[...] = pltpu.roll(wide, 2 * TILE_COLS - SHIFT, 1)[:, :TILE_COLS]


def columns_forward_kernel(data, first, second, twist_cos, twist_sin, out):
    rows = jnp.concatenate([data[pl.ds(s, OUTER, stride=SLAB), :] for s in range(SLAB)], axis=1)
    spread = dot(first[...], rows)
    cosine, sine = twist_cos[...], twist_sin[...]
    real, imag = [], []
    for s in range(SLAB):
        part = slice(s * 128, (s + 1) * 128)
        re, im = spread[:OUTER, part], spread[OUTER:, part]
        real.append(re * cosine + im * sine)
        imag.append(im * cosine - re * sine)
    for g in range(4):
        span = slice(g * 8, (g + 1) * 8)
        re = jnp.concatenate([part[span] for part in real], axis=0)
        im = jnp.concatenate([part[span] for part in imag], axis=0)
        both = jnp.concatenate([re, im], axis=1)
        final = dot(second[...], both, ((1,), (1,)))
        out[pl.ds(2 * g, 64, stride=8), :] = final[:64]
        out[pl.ds(2 * g + 1, 64, stride=8), :] = final[64:]


def columns_backward_kernel(place, slope, data, first, second, twist_cos, twist_sin, out):
    real, imag = [], []
    for g in range(4):
        span = slice(g * 8, (g + 1) * 8)
        both = jnp.concatenate(
            [data[pl.ds(2 * g, 64, stride=8), :], data[pl.ds(2 * g + 1, 64, stride=8), :]], axis=0
        )
        spread = dot(both, second[...], ((0,), (0,)))
        re = spread[:, :128].reshape(SLAB, 8, 128)
        im = spread[:, 128:].reshape(SLAB, 8, 128)
        cosine, sine = twist_cos[span][None], twist_sin[span][None]
        real.append(re * cosine - im * sine)
        imag.append(im * cosine + re * sine)
    stacked = jnp.concatenate(
        [jnp.concatenate([part[s] for part in real + imag], axis=0) for s in range(SLAB)], axis=1
    )
    mean = jnp.where(place[3] == 0, slope[0, 0], slope[0, 1])
    final = mean - dot(first[...], stacked)
    for s in range(SLAB):
        out[pl.ds(s, OUTER, stride=SLAB), :] = final[:, s * 128 : (s + 1) * 128]


def wave_numbers(place):
    shape = (CHIPS, 128)
    kp = lax.broadcasted_iota(jnp.int32, shape, 0)
    lane = lax.broadcasted_iota(jnp.int32, shape, 1)
    row_freq = kp + CHIPS * (lane // 8)
    col_freq = 8 * place[2] + lane % 8
    row_wave = jnp.where(row_freq >= ROWS // 2, row_freq - ROWS, row_freq).astype(jnp.float32)
    return row_freq, col_freq, row_wave, col_freq.astype(jnp.float32)


def rows_forward_kernel(place, data, first, second, twist_cos, twist_sin, out):
    real = data[pl.ds(0, CHIPS, stride=2), :]
    imag = data[pl.ds(1, CHIPS, stride=2), :]
    spread = dot(first[...], jnp.concatenate([real, imag], axis=1))
    re = spread[:CHIPS, :128] + spread[CHIPS:, 128:]
    im = spread[:CHIPS, 128:] - spread[CHIPS:, :128]
    cosine, sine = twist_cos[...], twist_sin[...]
    turned = jnp.concatenate([re * cosine + im * sine, im * cosine - re * sine], axis=1)
    final = dot(turned, second[...])
    _, _, row_wave, col_wave = wave_numbers(place)
    wave = jnp.where(place[3] == 0, row_wave, col_wave)
    out[:CHIPS] = wave * final[:, :128]
    out[CHIPS:] = wave * final[:, 128:]


def rows_backward_kernel(place, mine, other, first, second, twist_cos, twist_sin, out):
    row_freq, col_freq, row_wave, col_wave = wave_numbers(place)
    valid = (
        (row_freq != ROWS // 2)
        & (col_freq != COLS // 2)
        & ((row_freq != 0) | (col_freq != 0))
    )
    denom = reference_conduct * jnp.maximum(row_wave * row_wave + col_wave * col_wave, 1.0)
    weight = jnp.where(col_freq == 0, 1.0, 2.0) / (ROWS * COLS)
    wave = jnp.where(place[3] == 0, row_wave, col_wave)
    coef = jnp.where(valid, weight * wave / denom, 0.0)
    along = mine[...] + other[...]
    green = jnp.concatenate([coef * along[:CHIPS], coef * along[CHIPS:]], axis=1)
    spread = dot(green, second[...])
    re, im = spread[:, :128], spread[:, 128:]
    cosine, sine = twist_cos[...], twist_sin[...]
    turned = jnp.concatenate([re * cosine - im * sine, im * cosine + re * sine], axis=1)
    final = dot(first[...], turned)
    out[pl.ds(0, CHIPS, stride=2), :] = final[:CHIPS, :128] - final[CHIPS:, 128:]
    out[pl.ds(1, CHIPS, stride=2), :] = final[:CHIPS, 128:] + final[CHIPS:, :128]


def exchange(array, axes, count):
    blocks = array.reshape((count, array.size // count // 128, 128))
    return lax.all_to_all(blocks, axes, split_axis=0, concat_axis=0, tiled=True)


def shift(block, axes, count, step):
    return lax.ppermute(block, axes, [(i, (i + step) % count) for i in range(count)])


def bottom_strip(voxel, wetted, heat):
    bottom = [array[:, TILE_ROWS - EDGE :].astype(jnp.float32) for array in (voxel, wetted, heat)]
    which = lax.broadcasted_iota(jnp.int32, (3, EDGE, TILE_COLS), 0)
    return jnp.where(which == 0, bottom[0], jnp.where(which == 1, bottom[1], bottom[2]))


def body(voxel_material, wetted_indicator, starting_deficit_map, applied_thermal_slope):
    gx_size = lax.axis_size("gx")
    gt_size = lax.axis_size("gt")
    core_size = lax.axis_size("core")
    gy_size = gt_size * core_size
    gx_index = lax.axis_index("gx")
    gt_index = lax.axis_index("gt")
    core_index = lax.axis_index("core")
    gy = ("gt", "core")
    chips = ("gx", "gt")
    place = jnp.stack(
        [gx_index, gt_index * core_size + core_index, gx_index * gt_size + gt_index, core_index]
    ).astype(jnp.int32)
    (col_to, col_back), (row_to, row_back) = column_tables(), row_tables()
    tile = (TILE_ROWS, TILE_COLS)
    voxel, wetted, heat = voxel_material[0], wetted_indicator[0], starting_deficit_map[0]
    porous, phase, heat = call(prepare_kernel, [tile] * 3, voxel, wetted, heat)
    above = shift(bottom_strip(voxel_material, wetted_indicator, starting_deficit_map), "gx", gx_size, 1)
    (strip,) = call(edge_kernel, [(3, EDGE, WIDE)], porous, phase, heat, above)
    left = shift(strip, gy, gy_size, 1)
    fields, polar = call(
        stencil_kernel, [(2,) + tile, (TILE_ROWS // SLAB, 2, SLAB, TILE_COLS)],
        place, applied_thermal_slope, porous, phase, heat, above, left, smem=(0, 1),
    )
    slab = exchange(polar, gy, gy_size).reshape(-1, 128)
    slab = exchange(polar, gy, gy_size).reshape(-1, 128)
    (spec,) = call(columns_forward_kernel, [(2 * CHIPS, 128)], slab, *col_to)
    spec = exchange(spec, chips, CHIPS).reshape(-1, 128)
    (mine,) = call(rows_forward_kernel, [(2 * CHIPS, 128)], place, spec, *row_to, smem=(0,))
    other = lax.ppermute(mine, "core", [(0, 1), (1, 0)])
    (green,) = call(rows_backward_kernel, [(2 * CHIPS, 128)], place, mine, other, *row_back, smem=(0,))
    green, head = lax.optimization_barrier((green, fields[:, :EDGE]))
    tail = shift(head, "gx", gx_size, -1)
    fixed, strip = call(return_rows_kernel, [(2,) + tile, (2, EDGE, TILE_ROWS)], fields, tail)
    green = exchange(green, chips, CHIPS).reshape(-1, 128)
    green, strip = lax.optimization_barrier((green, strip))
    side = shift(strip, gy, gy_size, -1)
    phase_two, heat_two = call(return_columns_kernel, [tile, tile], fixed, side)
    (answer,) = call(
        columns_backward_kernel, [(OUTER * SLAB, 128)],
        place, applied_thermal_slope, green, *col_back, smem=(0, 1),
    )
    gradient = exchange(answer, ("core", "gt"), gy_size).reshape(2, 1, TILE_ROWS, TILE_COLS)
    return (phase_two[None], heat_two[None], gradient)


def solution(mesh):
    gx_size, gy_size = mesh.devices.shape
    fine = Mesh(mesh.devices.reshape(gx_size, gy_size // 2, 2), ("gx", "gt", "core"))
    gy = ("gt", "core")
    in_specs = (P(None, "gx", gy), P(None, "gx", gy), P(None, "gx", gy), P())
    out_specs = (P(None, "gx", gy), P(None, "gx", gy), P(None, None, "gx", gy))
    return jax.shard_map(body, mesh=fine, in_specs=in_specs, out_specs=out_specs, check_vma=False)
```

```python
import functools
import math

import jax
import jax.numpy as jnp
import numpy as np
from jax import lax
from jax.experimental import pallas as pl
from jax.experimental.pallas import tpu as pltpu
from jax.sharding import Mesh
from jax.sharding import PartitionSpec as P

solid_conduct = 1.7
gas_conduct = 0.026
liquid_conduct = 0.6
reference_conduct = 0.863
step_grad = 0.1
step_well = 0.3
step_drive = 0.2
step_heat = 0.12
latent_heat = 0.5
gradient_gain = 0.5

TILE_ROWS = 256
TILE_COLS = 128
EDGE = 8
SHIFT = 2
TALL = TILE_ROWS + EDGE
WIDE = 384
OUTER = 32
SLAB = 16
SPAN = 20
HALF = 64
BLOCK = SLAB + 4
CHIPS = 256
COLS = 4096
ROWS = 4096
CORE_MAJOR = np.arange(OUTER).reshape(-1, 2).T.reshape(-1)
VMEM = pl.BlockSpec(memory_space=pltpu.VMEM)
SMEM = pl.BlockSpec(memory_space=pltpu.SMEM)


def halves(array):
    high = array.astype(jnp.bfloat16)
    return high, (array - high.astype(jnp.float32)).astype(jnp.bfloat16)


def dot(left, right, contract=((1,), (0,))):
    def product(x, y):
        return lax.dot_general(x, y, (contract, ((), ())), preferred_element_type=jnp.float32)

    (left_high, left_low), (right_high, right_low) = left, right
    return product(left_high, right_high) + (
        product(left_high, right_low) + product(left_low, right_high)
    )


def call(kernel, outs, *args, smem=(), scratch=()):
    shapes = [jax.ShapeDtypeStruct(shape, jnp.float32) for shape in outs]
    spaces = [SMEM if i in smem else VMEM for i in range(len(args))]
    return pl.pallas_call(
        kernel,
        out_shape=shapes,
        in_specs=spaces,
        out_specs=[VMEM] * len(outs),
        scratch_shapes=list(scratch),
        compiler_params=pltpu.CompilerParams(vmem_limit_bytes=32 * 1024 * 1024),
    )(*args)


def angles(left, right, length):
    product = np.outer(np.arange(left), np.asarray(right)) % length
    return 2.0 * math.pi / length * product


def table(array):
    return jnp.asarray(np.asarray(array, dtype=np.float32))


def split_table(array):
    array = np.asarray(array, dtype=np.float32)
    high = array.astype(jnp.bfloat16)
    low = (array - high.astype(np.float32)).astype(jnp.bfloat16)
    return jnp.asarray(np.stack([high, low]))


def column_tables():
    first = angles(OUTER, range(OUTER), OUTER)
    cosine, sine = np.cos(first), np.sin(first)
    second = angles(64, range(128), 128)
    twist = angles(OUTER, range(128), COLS)
    mix = np.block([[np.cos(second), np.sin(second)], [-np.sin(second), np.cos(second)]])
    rest = [split_table(mix), table(np.cos(twist)), table(np.sin(twist))]
    slot, s = np.divmod(np.arange(4 * SLAB), SLAB)
    order = np.zeros((128, 128))
    order[np.arange(4 * SLAB), EDGE * s + slot] = 1.0
    stacked = np.concatenate([cosine, -sine], axis=0)
    forward = [split_table(order), split_table(stacked)] + rest
    backward = [split_table(np.concatenate([cosine, -sine], axis=1)[CORE_MAJOR])] + rest
    return forward, backward


def row_tables():
    first = angles(CHIPS, range(CHIPS), CHIPS)
    both = split_table(np.concatenate([np.cos(first), np.sin(first)], axis=0))
    tables = []
    for shift, sign in ((SHIFT, -1.0), (0, 1.0)):
        inner = np.arange(SLAB) - shift
        second = angles(SLAB, inner, SLAB)
        twist = np.repeat(angles(CHIPS, inner, ROWS), 8, axis=1)
        cosine, sine = np.kron(np.cos(second), np.eye(8)), sign * np.kron(np.sin(second), np.eye(8))
        if shift:
            cosine, sine = cosine.T, sine.T
        mix = np.block([[cosine, sine], [-sine, cosine]])
        tables.append([both, split_table(mix), table(np.cos(twist)), table(np.sin(twist))])
    return tables


GX, GY, CHIP, CORE, SLOPE_X, SLOPE_Y, SLOPE = range(7)


def prepare_kernel(place, slope, porous, phase, heat, info, strip):
    values = [place[i].astype(jnp.float32) for i in range(4)] + [slope[0, 0], slope[0, 1]]
    values.append(jnp.where(place[3] == 0, slope[0, 0], slope[0, 1]))
    row = lax.broadcasted_iota(jnp.int32, info.shape, 0)
    filled = jnp.zeros(info.shape, jnp.float32)
    for i, value in enumerate(values):
        filled = jnp.where(row == i, value, filled)
    info[...] = filled
    for f, field in enumerate((porous, phase, heat)):
        strip[f] = field[:EDGE, :]


def known(info, i):
    return info[i : i + 1, :]


def with_above(above, porous, phase, heat):
    tops = (above[0], above[0] * above[1], -above[2])
    return [
        jnp.concatenate([top, field[...]], axis=0) for top, field in zip(tops, (porous, phase, heat))
    ]


def with_both(above, below, porous, phase, heat):
    talls = with_above(above, porous, phase, heat)
    return [jnp.concatenate([tall, below[f]], axis=0) for f, tall in enumerate(talls)]


def edge_kernel(porous, phase, heat, above, below, first, last):
    spare = jnp.zeros((WIDE - TALL - EDGE, TILE_COLS), jnp.float32)
    for f, tall in enumerate(with_both(above, below, porous, phase, heat)):
        flipped = jnp.concatenate([tall, spare], axis=0).T
        first[f] = flipped[:EDGE]
        last[f] = flipped[TILE_COLS - EDGE :]


def progress(phase, heat, porous, phase_lap, heat_lap):
    well = 2.0 * phase * (1.0 - phase) * (1.0 - 2.0 * phase)
    growth = 30.0 * phase * phase * (1.0 - phase) * (1.0 - phase)
    new_phase = porous * (
        phase + step_grad * phase_lap - step_well * well + step_drive * heat * growth
    )
    new_heat = heat + step_heat * heat_lap - latent_heat * (new_phase - phase)
    return new_phase, new_heat


def stencil(porous, phase, heat, neighbours):
    def laplace(around, field):
        return around[0] + around[1] + around[2] + around[3] - 6.0 * field

    phase_lap, heat_lap = laplace(neighbours(phase), phase), laplace(neighbours(heat), heat)
    phase, heat = progress(phase, heat, porous, phase_lap, heat_lap)
    around = neighbours(heat)
    phase_lap, heat_lap = laplace(neighbours(phase), phase), laplace(around, heat)
    phase, heat = progress(phase, heat, porous, phase_lap, heat_lap)
    return phase, heat, around[0] - around[1], around[2] - around[3]


def roll(field, step, axis):
    return pltpu.roll(field, step % field.shape[axis], axis)


def walled(wall, field):
    return field if wall is None else jnp.where(wall, 0.0, field)


def ring_neighbours(walls):
    def neighbours(field):
        moves = ((-1, 0), (1, 0), (-1, 1), (1, 1))
        return [walled(wall, roll(field, *move)) for move, wall in zip(moves, walls)]

    return neighbours


def conductivity_contrast(porous, phase):
    conduct = (
        porous * (gas_conduct + (liquid_conduct - gas_conduct) * phase)
        + (1.0 - porous) * solid_conduct
    )
    return conduct - reference_conduct


def shifted_rows(field):
    return roll(field, SHIFT - EDGE, 0)[:TILE_ROWS]


def row_walls(first, row):
    return first & (row == EDGE - 1), first & (row == EDGE)


def polar_kernel(info, porous, phase, heat, above, out):
    talls = with_above(above, porous, phase, heat)
    row = lax.broadcasted_iota(jnp.int32, talls[0].shape, 0)
    walls = row_walls(known(info, GX) == 0.0, row) + (None, None)
    phase_two, _, along_rows, along_columns = stencil(*talls, ring_neighbours(walls))
    contrast = conductivity_contrast(talls[0], phase_two)
    polars = (
        shifted_rows(contrast * (known(info, SLOPE_X) + gradient_gain * along_rows)),
        shifted_rows(contrast * (known(info, SLOPE_Y) + gradient_gain * along_columns)),
    )
    spare = jnp.zeros((WIDE - TALL, TILE_COLS), jnp.float32)
    sublane = lax.broadcasted_iota(jnp.int32, (EDGE, WIDE), 0)
    lane = lax.broadcasted_iota(jnp.int32, (EDGE, TILE_COLS), 1)
    edges = []
    for tall in talls:
        flipped = jnp.concatenate([tall, spare], axis=0).T
        edges.append(jnp.where(sublane < 4, flipped[:EDGE], flipped[TILE_COLS - EDGE :]))
    for x in range(TILE_ROWS // SLAB):
        first = EDGE - 2 * SHIFT + SLAB * x
        windows = [
            roll(edge, f * SPAN - first, 1)[:, :TILE_COLS] for f, edge in enumerate(edges)
        ]
        packed = jnp.where(
            lane < SPAN, windows[0], jnp.where(lane < 2 * SPAN, windows[1], windows[2])
        )
        packed = jnp.where(lane < HALF, packed, roll(roll(packed, HALF, 1), 4, 0))
        for f in range(2):
            start = (2 * x + f) * BLOCK
            out[start : start + SLAB, :] = polars[f][x * SLAB : (x + 1) * SLAB]
            out[start + SLAB : start + BLOCK, :] = packed[:4]


def fields_kernel(info, porous, phase, heat, above, below, left, right, phase_out, heat_out):
    spare = jnp.zeros((TILE_COLS - 2 * EDGE, WIDE), jnp.float32)
    wides = []
    for f, tall in enumerate(with_both(above, below, porous, phase, heat)):
        side = jnp.concatenate([right[f], spare, left[f]], axis=0).T
        wides.append(jnp.concatenate([tall, side[: TALL + EDGE]], axis=1))
    shape = wides[0].shape
    row = lax.broadcasted_iota(jnp.int32, shape, 0)
    column = lax.broadcasted_iota(jnp.int32, shape, 1)
    gx, gy = (jnp.concatenate([known(info, i)] * 2, axis=1) for i in (GX, GY))
    top, bottom = gx == 0.0, gx == ROWS // TILE_ROWS - 1
    start, end = gy == 0.0, gy == COLS // TILE_COLS - 1
    walls = (
        (top & (row == EDGE - 1)) | (bottom & (row == TALL - 1)),
        (top & (row == EDGE)) | (bottom & (row == TALL)),
        (start & (column == shape[1] - 1)) | (end & (column == TILE_COLS - 1)),
        (start & (column == 0)) | (end & (column == TILE_COLS)),
    )
    phase_two, heat_two, _, _ = stencil(*wides, ring_neighbours(walls))
    phase_out[...] = phase_two[EDGE:TALL, :TILE_COLS]
    heat_out[...] = heat_two[EDGE:TALL, :TILE_COLS]


def edge_polar(info, data):
    raw = jnp.concatenate([data[pl.ds(SLAB + c, OUTER, stride=BLOCK), :] for c in range(4)], axis=0)
    fields = [raw] + [roll(raw, -f * SPAN, 1) for f in (1, 2)]
    lane = lax.broadcasted_iota(jnp.int32, raw.shape, 1)
    row = lane % HALF
    first = known(info, CHIP) == 0.0
    down_wall, up_wall = first & (row == 2 * SHIFT - 1), first & (row == 2 * SHIFT)
    tile = lax.broadcasted_iota(jnp.int32, (OUTER, TILE_COLS), 0)

    def neighbours(field):
        after = walled(tile == OUTER - 1, roll(roll(field[:OUTER], -1, 0), HALF, 1))
        before = walled(tile == 0, roll(roll(field[3 * OUTER :], 1, 0), HALF, 1))
        return (
            walled(down_wall, roll(field, -1, 1)),
            walled(up_wall, roll(field, 1, 1)),
            jnp.concatenate([field[OUTER:], after], axis=0),
            jnp.concatenate([before, field[: 3 * OUTER]], axis=0),
        )

    phase, _, along_rows, along_columns = stencil(*fields, neighbours)
    along = jnp.where(known(info, CORE) == 0.0, along_rows, along_columns)
    polar = conductivity_contrast(raw, phase) * (known(info, SLOPE) + gradient_gain * along)
    return [polar[c * OUTER : (c + 1) * OUTER] for c in range(4)]


def columns_forward_kernel(info, data, order, first, second, twist_cos, twist_sin, out):
    edges = edge_polar(info, data)
    lane = lax.broadcasted_iota(jnp.int32, (OUTER, TILE_COLS), 1)
    packed = jnp.zeros((OUTER, TILE_COLS), jnp.float32)
    for slot, column in enumerate((2, 3, 0, 1)):
        start = SHIFT + (HALF if column >= 2 else 0)
        moved = roll(edges[column], SLAB * slot - start, 1)
        packed = jnp.where(lane // SLAB == slot, moved, packed)
    packed = dot(halves(packed), (order[0], order[1]))
    outer = (lane < SHIFT) | (lane >= TILE_COLS - SHIFT)
    parts = []
    for s in range(SLAB):
        around = roll(packed, -EDGE * s - SHIFT, 1)
        parts.append(jnp.where(outer, around, data[pl.ds(s, OUTER, stride=BLOCK), :]))
    rows = jnp.concatenate(parts, axis=1)
    spread = dot((first[0], first[1]), halves(rows))
    cosine, sine = twist_cos[...], twist_sin[...]
    real, imag = [], []
    for s in range(SLAB):
        part = slice(s * 128, (s + 1) * 128)
        re, im = spread[:OUTER, part], spread[OUTER:, part]
        real.append(re * cosine + im * sine)
        imag.append(im * cosine - re * sine)
    for g in range(4):
        span = slice(g * 8, (g + 1) * 8)
        re = jnp.concatenate([part[span] for part in real], axis=0)
        im = jnp.concatenate([part[span] for part in imag], axis=0)
        both = jnp.concatenate([re, im], axis=1)
        final = dot((second[0], second[1]), halves(both), ((1,), (1,)))
        out[pl.ds(2 * g, 64, stride=8), :] = final[:64]
        out[pl.ds(2 * g + 1, 64, stride=8), :] = final[64:]


def columns_backward_kernel(info, data, first, second, twist_cos, twist_sin, out):
    real, imag = [], []
    for g in range(4):
        span = slice(g * 8, (g + 1) * 8)
        both = jnp.concatenate(
            [data[pl.ds(2 * g, 64, stride=8), :], data[pl.ds(2 * g + 1, 64, stride=8), :]], axis=0
        )
        spread = dot(halves(both.T), (second[0], second[1]))
        re = spread[:, :128].reshape(SLAB, 8, 128)
        im = spread[:, 128:].reshape(SLAB, 8, 128)
        cosine, sine = twist_cos[span][None], twist_sin[span][None]
        real.append(re * cosine - im * sine)
        imag.append(im * cosine + re * sine)
    stacked = jnp.concatenate(
        [jnp.concatenate([part[s] for part in real + imag], axis=0) for s in range(SLAB)], axis=1
    )
    final = dot((first[0], first[1]), halves(stacked))
    for s in range(SLAB):
        part = final[:, s * 128 : (s + 1) * 128]
        out[pl.ds(s, OUTER, stride=SLAB), :] = known(info, SLOPE) - part


def wave_numbers(info):
    shape = (CHIPS, 128)
    lane = lax.broadcasted_iota(jnp.int32, shape, 1)
    row_freq = lax.broadcasted_iota(jnp.int32, shape, 0) + CHIPS * (lane // 8)
    row_wave = jnp.where(row_freq >= ROWS // 2, row_freq - ROWS, row_freq).astype(jnp.float32)
    col_wave = 8.0 * known(info, CHIP) + (lane % 8).astype(jnp.float32)
    wave = jnp.where(known(info, CORE) == 0.0, row_wave, col_wave)
    return row_freq, row_wave, col_wave, wave


def rows_forward_kernel(info, data, first, second, twist_cos, twist_sin, out):
    real = data[pl.ds(0, CHIPS, stride=2), :]
    imag = data[pl.ds(1, CHIPS, stride=2), :]
    spread = dot((first[0], first[1]), halves(jnp.concatenate([real, imag], axis=1)))
    re = spread[:CHIPS, :128] + spread[CHIPS:, 128:]
    im = spread[:CHIPS, 128:] - spread[CHIPS:, :128]
    cosine, sine = twist_cos[...], twist_sin[...]
    turned = jnp.concatenate([re * cosine + im * sine, im * cosine - re * sine], axis=1)
    final = dot(halves(turned), (second[0], second[1]))
    wave = wave_numbers(info)[3]
    out[:CHIPS] = wave * final[:, :128]
    out[CHIPS:] = wave * final[:, 128:]


def rows_backward_kernel(info, mine, other, first, second, twist_cos, twist_sin, out):
    row_freq, row_wave, col_wave, wave = wave_numbers(info)
    valid = (
        (row_freq != ROWS // 2)
        & (col_wave != COLS // 2)
        & ((row_freq != 0) | (col_wave != 0.0))
    )
    denom = reference_conduct * jnp.maximum(row_wave * row_wave + col_wave * col_wave, 1.0)
    weight = jnp.where(col_wave == 0.0, 1.0, 2.0) / (ROWS * COLS)
    coef = jnp.where(valid, weight * wave / denom, 0.0)
    along = mine[...] + other[...]
    green = jnp.concatenate([coef * along[:CHIPS], coef * along[CHIPS:]], axis=1)
    spread = dot(halves(green), (second[0], second[1]))
    re, im = spread[:, :128], spread[:, 128:]
    cosine, sine = twist_cos[...], twist_sin[...]
    turned = jnp.concatenate([re * cosine - im * sine, im * cosine + re * sine], axis=1)
    final = dot((first[0], first[1]), halves(turned))
    out[pl.ds(0, CHIPS, stride=2), :] = final[:CHIPS, :128] - final[CHIPS:, 128:]
    out[pl.ds(1, CHIPS, stride=2), :] = final[:CHIPS, 128:] + final[CHIPS:, :128]


def exchange(array, axes, tile):
    blocks = array.reshape((array.size // tile // 128, tile, 128))
    return lax.all_to_all(blocks, axes, split_axis=0, concat_axis=0, tiled=True)


def shift(block, axes, count, step):
    return lax.ppermute(block, axes, [(i, (i + step) % count) for i in range(count)])


def bottom_strip(voxel, wetted, heat):
    bottom = [array[:, TILE_ROWS - EDGE :] for array in (voxel, wetted, heat)]
    parts = bottom[0].astype(jnp.float32), bottom[1].astype(jnp.float32), -bottom[2]
    which = lax.broadcasted_iota(jnp.int32, (3, EDGE, TILE_COLS), 0)
    return jnp.where(which == 0, parts[0], jnp.where(which == 1, parts[1], parts[2]))


def body(voxel, wetted, heat, slope):
    gx_index, gt_index, core = (lax.axis_index(name) for name in ("gx", "gt", "core"))
    gx_size, gt_size, core_size = (lax.axis_size(name) for name in ("gx", "gt", "core"))
    gy_size = gt_size * core_size
    gy = ("gt", "core")
    chips = ("gx", "gt")
    place = jnp.stack([gx_index, gt_index * core_size + core, gx_index * gt_size + gt_index, core])
    (col_to, col_back), (row_to, row_back) = column_tables(), row_tables()
    tile = (TILE_ROWS, TILE_COLS)
    above = shift(bottom_strip(voxel, wetted, heat), "gx", gx_size, 1)
    porous = voxel[0].astype(jnp.float32)
    phase = porous * wetted[0].astype(jnp.float32)
    heat = heat[0]
    info, top = call(
        prepare_kernel, [(8, 128), (3, EDGE, TILE_COLS)],
        place.astype(jnp.int32), slope, porous, phase, heat, smem=(0, 1),
    )
    (polar,) = call(polar_kernel, [(OUTER * BLOCK, 128)], info, porous, phase, heat, above)
    below = shift(top, "gx", gx_size, -1)
    slab = exchange(polar, gy, 4).reshape(-1, 128)
    slab, below = lax.optimization_barrier((slab, below))
    first, last = call(edge_kernel, [(3, EDGE, WIDE)] * 2, porous, phase, heat, above, below)
    left = shift(last, gy, gy_size, 1)
    (spec,) = call(columns_forward_kernel, [(2 * CHIPS, 128)], info, slab, *col_to)
    spec = exchange(spec, chips, 2).reshape(-1, 128)
    spec, left = lax.optimization_barrier((spec, left))
    (mine,) = call(rows_forward_kernel, [(2 * CHIPS, 128)], info, spec, *row_to)
    other = lax.ppermute(mine, "core", [(0, 1), (1, 0)])
    (green,) = call(rows_backward_kernel, [(2 * CHIPS, 128)], info, mine, other, *row_back)
    green = exchange(green, chips, 2).reshape(-1, 128)
    green, first = lax.optimization_barrier((green, first))
    right = shift(first, gy, gy_size, -1)
    phase_two, heat_two = call(
        fields_kernel, [tile, tile], info, porous, phase, heat, above, below, left, right
    )
    (answer,) = call(columns_backward_kernel, [(OUTER * SLAB, 128)], info, green, *col_back)
    gradient = exchange(answer, ("core", "gt"), 8).reshape(2, 1, TILE_ROWS, TILE_COLS)
    return (phase_two[None], heat_two[None], gradient)


def solution(mesh):
    gx_size, gy_size = mesh.devices.shape
    fine = Mesh(mesh.devices.reshape(gx_size, gy_size // 2, 2), ("gx", "gt", "core"))
    gy = ("gt", "core")
    in_specs = (P(None, "gx", gy), P(None, "gx", gy), P(None, "gx", gy), P())
    out_specs = (P(None, "gx", gy), P(None, "gx", gy), P(None, None, "gx", gy))
    return jax.shard_map(body, mesh=fine, in_specs=in_specs, out_specs=out_specs, check_vma=False)
```

```python
import functools
import math

import jax
import jax.numpy as jnp
import numpy as np
from jax import lax
from jax.experimental import pallas as pl
from jax.experimental.pallas import tpu as pltpu
from jax.sharding import Mesh
from jax.sharding import PartitionSpec as P

solid_conduct = 1.7
gas_conduct = 0.026
liquid_conduct = 0.6
reference_conduct = 0.863
step_grad = 0.1
step_well = 0.3
step_drive = 0.2
step_heat = 0.12
latent_heat = 0.5
gradient_gain = 0.5

TILE_ROWS = 256
TILE_COLS = 128
EDGE = 8
SHIFT = 2
TALL = TILE_ROWS + EDGE
WIDE = 384
OUTER = 32
SLAB = 16
SPAN = 20
HALF = 64
BLOCK = SLAB + 4
CHIPS = 256
COLS = 4096
ROWS = 4096
CORE_MAJOR = np.arange(OUTER).reshape(-1, 2).T.reshape(-1)
VMEM = pl.BlockSpec(memory_space=pltpu.VMEM)
SMEM = pl.BlockSpec(memory_space=pltpu.SMEM)


def halves(array):
    high = array.astype(jnp.bfloat16)
    return high, (array - high.astype(jnp.float32)).astype(jnp.bfloat16)


def dot(left, right, contract=((1,), (0,))):
    def product(x, y):
        return lax.dot_general(x, y, (contract, ((), ())), preferred_element_type=jnp.float32)

    (left_high, left_low), (right_high, right_low) = left, right
    return product(left_high, right_high) + (
        product(left_high, right_low) + product(left_low, right_high)
    )


def call(kernel, outs, *args, smem=(), scratch=()):
    shapes = [jax.ShapeDtypeStruct(shape, jnp.float32) for shape in outs]
    spaces = [SMEM if i in smem else VMEM for i in range(len(args))]
    return pl.pallas_call(
        kernel,
        out_shape=shapes,
        in_specs=spaces,
        out_specs=[VMEM] * len(outs),
        scratch_shapes=list(scratch),
        compiler_params=pltpu.CompilerParams(vmem_limit_bytes=32 * 1024 * 1024),
    )(*args)


def angles(left, right, length):
    product = np.outer(np.arange(left), np.asarray(right)) % length
    return 2.0 * math.pi / length * product


def table(array):
    return jnp.asarray(np.asarray(array, dtype=np.float32))


def split_table(array):
    array = np.asarray(array, dtype=np.float32)
    high = array.astype(jnp.bfloat16)
    low = (array - high.astype(np.float32)).astype(jnp.bfloat16)
    return jnp.asarray(np.stack([high, low]))


def column_tables():
    first = angles(OUTER, range(OUTER), OUTER)
    cosine, sine = np.cos(first), np.sin(first)
    second = angles(64, range(128), 128)
    twist = angles(OUTER, range(128), COLS)
    mix = np.block([[np.cos(second), np.sin(second)], [-np.sin(second), np.cos(second)]])
    rest = [split_table(mix), table(np.cos(twist)), table(np.sin(twist))]
    slot, s = np.divmod(np.arange(4 * SLAB), SLAB)
    order = np.zeros((128, 128))
    order[np.arange(4 * SLAB), EDGE * s + slot] = 1.0
    stacked = np.concatenate([cosine, -sine], axis=0)
    forward = [split_table(order), split_table(stacked)] + rest
    backward = [split_table(np.concatenate([cosine, -sine], axis=1)[CORE_MAJOR])] + rest
    return forward, backward


def row_tables():
    first = angles(CHIPS, range(CHIPS), CHIPS)
    both = split_table(np.concatenate([np.cos(first), np.sin(first)], axis=0))
    tables = []
    for shift, sign in ((SHIFT, -1.0), (0, 1.0)):
        inner = np.arange(SLAB) - shift
        second = angles(SLAB, inner, SLAB)
        twist = np.repeat(angles(CHIPS, inner, ROWS), 8, axis=1)
        cosine, sine = np.kron(np.cos(second), np.eye(8)), sign * np.kron(np.sin(second), np.eye(8))
        if shift:
            cosine, sine = cosine.T, sine.T
        mix = np.block([[cosine, sine], [-sine, cosine]])
        tables.append([both, split_table(mix), table(np.cos(twist)), table(np.sin(twist))])
    return tables


GX, GY, CHIP, CORE, SLOPE_X, SLOPE_Y, SLOPE = range(7)


def prepare_kernel(place, slope, info):
    values = [place[i].astype(jnp.float32) for i in range(4)] + [slope[0, 0], slope[0, 1]]
    values.append(jnp.where(place[3] == 0, slope[0, 0], slope[0, 1]))
    row = lax.broadcasted_iota(jnp.int32, info.shape, 0)
    filled = jnp.zeros(info.shape, jnp.float32)
    for i, value in enumerate(values):
        filled = jnp.where(row == i, value, filled)
    info[...] = filled


def known(info, i):
    return info[i : i + 1, :]


def with_above(above, porous, phase, heat):
    tops = (above[0], above[0] * above[1], -above[2])
    return [
        jnp.concatenate([top, field[...]], axis=0) for top, field in zip(tops, (porous, phase, heat))
    ]


def edge_kernel(porous, phase, heat, above, first, last):
    spare = jnp.zeros((WIDE - TALL, TILE_COLS), jnp.float32)
    for f, tall in enumerate(with_above(above, porous, phase, heat)):
        flipped = jnp.concatenate([tall, spare], axis=0).T
        first[f] = flipped[:EDGE]
        last[f] = flipped[TILE_COLS - EDGE :]


def sides(left, right, f, rows):
    spare = jnp.zeros((TILE_COLS - 2 * EDGE, rows), jnp.float32)
    return jnp.concatenate([right[f, :, :rows], spare, left[f, :, :rows]], axis=0).T


def top_kernel(porous, phase, heat, left, right, out):
    for f, field in enumerate((porous, phase, heat)):
        out[f, :, :TILE_COLS] = field[:EDGE, :]
        out[f, :, TILE_COLS:] = sides(left, right, f, 128)[EDGE : 2 * EDGE]


def progress(phase, heat, porous, phase_lap, heat_lap):
    well = 2.0 * phase * (1.0 - phase) * (1.0 - 2.0 * phase)
    growth = 30.0 * phase * phase * (1.0 - phase) * (1.0 - phase)
    new_phase = porous * (
        phase + step_grad * phase_lap - step_well * well + step_drive * heat * growth
    )
    new_heat = heat + step_heat * heat_lap - latent_heat * (new_phase - phase)
    return new_phase, new_heat


def stencil(porous, phase, heat, neighbours):
    def laplace(around, field):
        return around[0] + around[1] + around[2] + around[3] - 6.0 * field

    phase_lap, heat_lap = laplace(neighbours(phase), phase), laplace(neighbours(heat), heat)
    phase, heat = progress(phase, heat, porous, phase_lap, heat_lap)
    around = neighbours(heat)
    phase_lap, heat_lap = laplace(neighbours(phase), phase), laplace(around, heat)
    phase, heat = progress(phase, heat, porous, phase_lap, heat_lap)
    return phase, heat, around[0] - around[1], around[2] - around[3]


def roll(field, step, axis):
    return pltpu.roll(field, step % field.shape[axis], axis)


def walled(wall, field):
    return field if wall is None else jnp.where(wall, 0.0, field)


def ring_neighbours(walls):
    def neighbours(field):
        moves = ((-1, 0), (1, 0), (-1, 1), (1, 1))
        return [walled(wall, roll(field, *move)) for move, wall in zip(moves, walls)]

    return neighbours


def conductivity_contrast(porous, phase):
    conduct = (
        porous * (gas_conduct + (liquid_conduct - gas_conduct) * phase)
        + (1.0 - porous) * solid_conduct
    )
    return conduct - reference_conduct


def shifted_rows(field):
    return roll(field, SHIFT - EDGE, 0)[:TILE_ROWS]


def row_walls(first, row):
    return first & (row == EDGE - 1), first & (row == EDGE)


def polar_kernel(info, porous, phase, heat, above, out):
    talls = with_above(above, porous, phase, heat)
    row = lax.broadcasted_iota(jnp.int32, talls[0].shape, 0)
    walls = row_walls(known(info, GX) == 0.0, row) + (None, None)
    phase_two, _, along_rows, along_columns = stencil(*talls, ring_neighbours(walls))
    contrast = conductivity_contrast(talls[0], phase_two)
    polars = (
        shifted_rows(contrast * (known(info, SLOPE_X) + gradient_gain * along_rows)),
        shifted_rows(contrast * (known(info, SLOPE_Y) + gradient_gain * along_columns)),
    )
    spare = jnp.zeros((WIDE - TALL, TILE_COLS), jnp.float32)
    sublane = lax.broadcasted_iota(jnp.int32, (EDGE, WIDE), 0)
    lane = lax.broadcasted_iota(jnp.int32, (EDGE, TILE_COLS), 1)
    edges = []
    for tall in talls:
        flipped = jnp.concatenate([tall, spare], axis=0).T
        edges.append(jnp.where(sublane < 4, flipped[:EDGE], flipped[TILE_COLS - EDGE :]))
    for x in range(TILE_ROWS // SLAB):
        first = EDGE - 2 * SHIFT + SLAB * x
        windows = [
            roll(edge, f * SPAN - first, 1)[:, :TILE_COLS] for f, edge in enumerate(edges)
        ]
        packed = jnp.where(
            lane < SPAN, windows[0], jnp.where(lane < 2 * SPAN, windows[1], windows[2])
        )
        packed = jnp.where(lane < HALF, packed, roll(roll(packed, HALF, 1), 4, 0))
        for f in range(2):
            start = (2 * x + f) * BLOCK
            out[start : start + SLAB, :] = polars[f][x * SLAB : (x + 1) * SLAB]
            out[start + SLAB : start + BLOCK, :] = packed[:4]


def fields_kernel(info, porous, phase, heat, above, below, left, right, phase_out, heat_out):
    wides = []
    for f, tall in enumerate(with_above(above, porous, phase, heat)):
        wide = jnp.concatenate([tall, sides(left, right, f, WIDE)[:TALL]], axis=1)
        wides.append(jnp.concatenate([wide, below[f]], axis=0))
    shape = wides[0].shape
    row = lax.broadcasted_iota(jnp.int32, shape, 0)
    column = lax.broadcasted_iota(jnp.int32, shape, 1)
    gx, gy = (jnp.concatenate([known(info, i)] * 2, axis=1) for i in (GX, GY))
    top, bottom = gx == 0.0, gx == ROWS // TILE_ROWS - 1
    start, end = gy == 0.0, gy == COLS // TILE_COLS - 1
    walls = (
        (top & (row == EDGE - 1)) | (bottom & (row == TALL - 1)),
        (top & (row == EDGE)) | (bottom & (row == TALL)),
        (start & (column == shape[1] - 1)) | (end & (column == TILE_COLS - 1)),
        (start & (column == 0)) | (end & (column == TILE_COLS)),
    )
    phase_two, heat_two, _, _ = stencil(*wides, ring_neighbours(walls))
    phase_out[...] = phase_two[EDGE:TALL, :TILE_COLS]
    heat_out[...] = heat_two[EDGE:TALL, :TILE_COLS]


def edge_polar(info, data):
    raw = jnp.concatenate([data[pl.ds(SLAB + c, OUTER, stride=BLOCK), :] for c in range(4)], axis=0)
    fields = [raw] + [roll(raw, -f * SPAN, 1) for f in (1, 2)]
    lane = lax.broadcasted_iota(jnp.int32, raw.shape, 1)
    row = lane % HALF
    first = known(info, CHIP) == 0.0
    down_wall, up_wall = first & (row == 2 * SHIFT - 1), first & (row == 2 * SHIFT)
    tile = lax.broadcasted_iota(jnp.int32, (OUTER, TILE_COLS), 0)

    def neighbours(field):
        after = walled(tile == OUTER - 1, roll(roll(field[:OUTER], -1, 0), HALF, 1))
        before = walled(tile == 0, roll(roll(field[3 * OUTER :], 1, 0), HALF, 1))
        return (
            walled(down_wall, roll(field, -1, 1)),
            walled(up_wall, roll(field, 1, 1)),
            jnp.concatenate([field[OUTER:], after], axis=0),
            jnp.concatenate([before, field[: 3 * OUTER]], axis=0),
        )

    phase, _, along_rows, along_columns = stencil(*fields, neighbours)
    along = jnp.where(known(info, CORE) == 0.0, along_rows, along_columns)
    polar = conductivity_contrast(raw, phase) * (known(info, SLOPE) + gradient_gain * along)
    return [polar[c * OUTER : (c + 1) * OUTER] for c in range(4)]


def columns_forward_kernel(info, data, order, first, second, twist_cos, twist_sin, out):
    edges = edge_polar(info, data)
    lane = lax.broadcasted_iota(jnp.int32, (OUTER, TILE_COLS), 1)
    packed = jnp.zeros((OUTER, TILE_COLS), jnp.float32)
    for slot, column in enumerate((2, 3, 0, 1)):
        start = SHIFT + (HALF if column >= 2 else 0)
        moved = roll(edges[column], SLAB * slot - start, 1)
        packed = jnp.where(lane // SLAB == slot, moved, packed)
    packed = dot(halves(packed), (order[0], order[1]))
    outer = (lane < SHIFT) | (lane >= TILE_COLS - SHIFT)
    parts = []
    for s in range(SLAB):
        around = roll(packed, -EDGE * s - SHIFT, 1)
        parts.append(jnp.where(outer, around, data[pl.ds(s, OUTER, stride=BLOCK), :]))
    rows = jnp.concatenate(parts, axis=1)
    spread = dot((first[0], first[1]), halves(rows))
    cosine, sine = twist_cos[...], twist_sin[...]
    real, imag = [], []
    for s in range(SLAB):
        part = slice(s * 128, (s + 1) * 128)
        re, im = spread[:OUTER, part], spread[OUTER:, part]
        real.append(re * cosine + im * sine)
        imag.append(im * cosine - re * sine)
    for g in range(4):
        span = slice(g * 8, (g + 1) * 8)
        re = jnp.concatenate([part[span] for part in real], axis=0)
        im = jnp.concatenate([part[span] for part in imag], axis=0)
        both = jnp.concatenate([re, im], axis=1)
        final = dot((second[0], second[1]), halves(both), ((1,), (1,)))
        out[pl.ds(2 * g, 64, stride=8), :] = final[:64]
        out[pl.ds(2 * g + 1, 64, stride=8), :] = final[64:]


def columns_backward_kernel(info, data, first, second, twist_cos, twist_sin, out):
    real, imag = [], []
    for g in range(4):
        span = slice(g * 8, (g + 1) * 8)
        both = jnp.concatenate(
            [data[pl.ds(2 * g, 64, stride=8), :], data[pl.ds(2 * g + 1, 64, stride=8), :]], axis=0
        )
        spread = dot(halves(both.T), (second[0], second[1]))
        re = spread[:, :128].reshape(SLAB, 8, 128)
        im = spread[:, 128:].reshape(SLAB, 8, 128)
        cosine, sine = twist_cos[span][None], twist_sin[span][None]
        real.append(re * cosine - im * sine)
        imag.append(im * cosine + re * sine)
    stacked = jnp.concatenate(
        [jnp.concatenate([part[s] for part in real + imag], axis=0) for s in range(SLAB)], axis=1
    )
    final = dot((first[0], first[1]), halves(stacked))
    for s in range(SLAB):
        part = final[:, s * 128 : (s + 1) * 128]
        out[pl.ds(s, OUTER, stride=SLAB), :] = known(info, SLOPE) - part


def wave_numbers(info):
    shape = (CHIPS, 128)
    lane = lax.broadcasted_iota(jnp.int32, shape, 1)
    row_freq = lax.broadcasted_iota(jnp.int32, shape, 0) + CHIPS * (lane // 8)
    row_wave = jnp.where(row_freq >= ROWS // 2, row_freq - ROWS, row_freq).astype(jnp.float32)
    col_wave = 8.0 * known(info, CHIP) + (lane % 8).astype(jnp.float32)
    wave = jnp.where(known(info, CORE) == 0.0, row_wave, col_wave)
    return row_freq, row_wave, col_wave, wave


def rows_forward_kernel(info, data, first, second, twist_cos, twist_sin, out):
    real = data[pl.ds(0, CHIPS, stride=2), :]
    imag = data[pl.ds(1, CHIPS, stride=2), :]
    spread = dot((first[0], first[1]), halves(jnp.concatenate([real, imag], axis=1)))
    re = spread[:CHIPS, :128] + spread[CHIPS:, 128:]
    im = spread[:CHIPS, 128:] - spread[CHIPS:, :128]
    cosine, sine = twist_cos[...], twist_sin[...]
    turned = jnp.concatenate([re * cosine + im * sine, im * cosine - re * sine], axis=1)
    final = dot(halves(turned), (second[0], second[1]))
    wave = wave_numbers(info)[3]
    out[:CHIPS] = wave * final[:, :128]
    out[CHIPS:] = wave * final[:, 128:]


def rows_backward_kernel(info, mine, other, first, second, twist_cos, twist_sin, out):
    row_freq, row_wave, col_wave, wave = wave_numbers(info)
    valid = (
        (row_freq != ROWS // 2)
        & (col_wave != COLS // 2)
        & ((row_freq != 0) | (col_wave != 0.0))
    )
    denom = reference_conduct * jnp.maximum(row_wave * row_wave + col_wave * col_wave, 1.0)
    weight = jnp.where(col_wave == 0.0, 1.0, 2.0) / (ROWS * COLS)
    coef = jnp.where(valid, weight * wave / denom, 0.0)
    along = mine[...] + other[...]
    green = jnp.concatenate([coef * along[:CHIPS], coef * along[CHIPS:]], axis=1)
    spread = dot(halves(green), (second[0], second[1]))
    re, im = spread[:, :128], spread[:, 128:]
    cosine, sine = twist_cos[...], twist_sin[...]
    turned = jnp.concatenate([re * cosine - im * sine, im * cosine + re * sine], axis=1)
    final = dot((first[0], first[1]), halves(turned))
    out[pl.ds(0, CHIPS, stride=2), :] = final[:CHIPS, :128] - final[CHIPS:, 128:]
    out[pl.ds(1, CHIPS, stride=2), :] = final[:CHIPS, 128:] + final[CHIPS:, :128]


def exchange(array, axes, tile):
    blocks = array.reshape((array.size // tile // 128, tile, 128))
    return lax.all_to_all(blocks, axes, split_axis=0, concat_axis=0, tiled=True)


def shift(block, axes, count, step):
    return lax.ppermute(block, axes, [(i, (i + step) % count) for i in range(count)])


def bottom_strip(voxel, wetted, heat):
    bottom = [array[:, TILE_ROWS - EDGE :] for array in (voxel, wetted, heat)]
    parts = bottom[0].astype(jnp.float32), bottom[1].astype(jnp.float32), -bottom[2]
    which = lax.broadcasted_iota(jnp.int32, (3, EDGE, TILE_COLS), 0)
    return jnp.where(which == 0, parts[0], jnp.where(which == 1, parts[1], parts[2]))


def body(voxel, wetted, heat, slope):
    gx_index, gt_index, core = (lax.axis_index(name) for name in ("gx", "gt", "core"))
    gx_size, gt_size, core_size = (lax.axis_size(name) for name in ("gx", "gt", "core"))
    gy_size = gt_size * core_size
    gy = ("gt", "core")
    chips = ("gx", "gt")
    place = jnp.stack([gx_index, gt_index * core_size + core, gx_index * gt_size + gt_index, core])
    (col_to, col_back), (row_to, row_back) = column_tables(), row_tables()
    tile = (TILE_ROWS, TILE_COLS)
    above = shift(bottom_strip(voxel, wetted, heat), "gx", gx_size, 1)
    porous = voxel[0].astype(jnp.float32)
    phase = porous * wetted[0].astype(jnp.float32)
    heat = heat[0]
    (info,) = call(prepare_kernel, [(8, 128)], place.astype(jnp.int32), slope, smem=(0, 1))
    (polar,) = call(polar_kernel, [(OUTER * BLOCK, 128)], info, porous, phase, heat, above)
    slab = exchange(polar, gy, 4).reshape(-1, 128)
    first, last = call(edge_kernel, [(3, EDGE, WIDE)] * 2, porous, phase, heat, above)
    left = shift(last, gy, gy_size, 1)
    right = shift(first, gy, gy_size, -1)
    slab, left, right = lax.optimization_barrier((slab, left, right))
    (spec,) = call(columns_forward_kernel, [(2 * CHIPS, 128)], info, slab, *col_to)
    spec = exchange(spec, chips, 2).reshape(-1, 128)
    (mine,) = call(rows_forward_kernel, [(2 * CHIPS, 128)], info, spec, *row_to)
    other = lax.ppermute(mine, "core", [(0, 1), (1, 0)])
    (green,) = call(rows_backward_kernel, [(2 * CHIPS, 128)], info, mine, other, *row_back)
    green, left, right = lax.optimization_barrier((green, left, right))
    (top,) = call(top_kernel, [(3, EDGE, 2 * TILE_COLS)], porous, phase, heat, left, right)
    below = shift(top, "gx", gx_size, -1)
    green = exchange(green, chips, 2).reshape(-1, 128)
    green, below = lax.optimization_barrier((green, below))
    phase_two, heat_two = call(
        fields_kernel, [tile, tile], info, porous, phase, heat, above, below, left, right
    )
    (answer,) = call(columns_backward_kernel, [(OUTER * SLAB, 128)], info, green, *col_back)
    gradient = exchange(answer, ("core", "gt"), 8).reshape(2, 1, TILE_ROWS, TILE_COLS)
    return (phase_two[None], heat_two[None], gradient)


def solution(mesh):
    gx_size, gy_size = mesh.devices.shape
    fine = Mesh(mesh.devices.reshape(gx_size, gy_size // 2, 2), ("gx", "gt", "core"))
    gy = ("gt", "core")
    in_specs = (P(None, "gx", gy), P(None, "gx", gy), P(None, "gx", gy), P())
    out_specs = (P(None, "gx", gy), P(None, "gx", gy), P(None, None, "gx", gy))
    return jax.shard_map(body, mesh=fine, in_specs=in_specs, out_specs=out_specs, check_vma=False)
```

```python
import functools
import math

import jax
import jax.numpy as jnp
import numpy as np
from jax import lax
from jax.experimental import pallas as pl
from jax.experimental.pallas import tpu as pltpu
from jax.sharding import Mesh
from jax.sharding import PartitionSpec as P

solid_conduct = 1.7
gas_conduct = 0.026
liquid_conduct = 0.6
reference_conduct = 0.863
step_grad = 0.1
step_well = 0.3
step_drive = 0.2
step_heat = 0.12
latent_heat = 0.5
gradient_gain = 0.5

TILE_ROWS = 256
TILE_COLS = 128
EDGE = 8
SHIFT = 2
TALL = TILE_ROWS + EDGE
WIDE = 384
OUTER = 32
SLAB = 16
SPAN = 20
HALF = 64
BLOCK = SLAB + 4
BACK = SLAB + 2
CHIPS = 256
COLS = 4096
ROWS = 4096
CORE_MAJOR = np.arange(OUTER).reshape(-1, 2).T.reshape(-1)
VMEM = pl.BlockSpec(memory_space=pltpu.VMEM)
SMEM = pl.BlockSpec(memory_space=pltpu.SMEM)


def halves(array):
    high = array.astype(jnp.bfloat16)
    return high, (array - high.astype(jnp.float32)).astype(jnp.bfloat16)


def dot(left, right, contract=((1,), (0,))):
    def product(x, y):
        return lax.dot_general(x, y, (contract, ((), ())), preferred_element_type=jnp.float32)

    (left_high, left_low), (right_high, right_low) = left, right
    return product(left_high, right_high) + (
        product(left_high, right_low) + product(left_low, right_high)
    )


def call(kernel, outs, *args, smem=(), scratch=()):
    shapes = [jax.ShapeDtypeStruct(shape, jnp.float32) for shape in outs]
    spaces = [SMEM if i in smem else VMEM for i in range(len(args))]
    return pl.pallas_call(
        kernel,
        out_shape=shapes,
        in_specs=spaces,
        out_specs=[VMEM] * len(outs),
        scratch_shapes=list(scratch),
        compiler_params=pltpu.CompilerParams(vmem_limit_bytes=32 * 1024 * 1024),
    )(*args)


def angles(left, right, length):
    product = np.outer(np.arange(left), np.asarray(right)) % length
    return 2.0 * math.pi / length * product


def table(array):
    return jnp.asarray(np.asarray(array, dtype=np.float32))


def split_table(array):
    array = np.asarray(array, dtype=np.float32)
    high = array.astype(jnp.bfloat16)
    low = (array - high.astype(np.float32)).astype(jnp.bfloat16)
    return jnp.asarray(np.stack([high, low]))


def column_tables():
    first = angles(OUTER, range(OUTER), OUTER)
    cosine, sine = np.cos(first), np.sin(first)
    second = angles(64, range(128), 128)
    twist = angles(OUTER, range(128), COLS)
    mix = np.block([[np.cos(second), np.sin(second)], [-np.sin(second), np.cos(second)]])
    rest = [split_table(mix), table(np.cos(twist)), table(np.sin(twist))]
    slot, s = np.divmod(np.arange(4 * SLAB), SLAB)
    order = np.zeros((128, 128))
    order[np.arange(4 * SLAB), EDGE * s + slot] = 1.0
    stacked = np.concatenate([cosine, -sine], axis=0)
    forward = [split_table(order), split_table(stacked)] + rest
    backward = [split_table(np.concatenate([cosine, -sine], axis=1)[CORE_MAJOR])] + rest
    columns = np.zeros((128, 128))
    columns[np.arange(4 * SLAB), (slot - SHIFT) % TILE_COLS] = 1.0
    return forward, backward, jnp.asarray(columns.astype(jnp.bfloat16))


def row_tables():
    first = angles(CHIPS, range(CHIPS), CHIPS)
    both = split_table(np.concatenate([np.cos(first), np.sin(first)], axis=0))
    tables = []
    for shift, sign in ((SHIFT, -1.0), (0, 1.0)):
        inner = np.arange(SLAB) - shift
        second = angles(SLAB, inner, SLAB)
        twist = np.repeat(angles(CHIPS, inner, ROWS), 8, axis=1)
        cosine, sine = np.kron(np.cos(second), np.eye(8)), sign * np.kron(np.sin(second), np.eye(8))
        if shift:
            cosine, sine = cosine.T, sine.T
        mix = np.block([[cosine, sine], [-sine, cosine]])
        tables.append([both, split_table(mix), table(np.cos(twist)), table(np.sin(twist))])
    return tables


GX, GY, CHIP, CORE, SLOPE_X, SLOPE_Y, SLOPE = range(7)


def prepare_kernel(place, slope, info):
    values = [place[i].astype(jnp.float32) for i in range(4)] + [slope[0, 0], slope[0, 1]]
    values.append(jnp.where(place[3] == 0, slope[0, 0], slope[0, 1]))
    row = lax.broadcasted_iota(jnp.int32, info.shape, 0)
    filled = jnp.zeros(info.shape, jnp.float32)
    for i, value in enumerate(values):
        filled = jnp.where(row == i, value, filled)
    info[...] = filled


def known(info, i):
    return info[i : i + 1, :]


def with_above(above, porous, phase, heat):
    tops = (above[0], above[0] * above[1], -above[2])
    return [
        jnp.concatenate([top, field[...]], axis=0) for top, field in zip(tops, (porous, phase, heat))
    ]


def progress(phase, heat, porous, phase_lap, heat_lap):
    well = 2.0 * phase * (1.0 - phase) * (1.0 - 2.0 * phase)
    growth = 30.0 * phase * phase * (1.0 - phase) * (1.0 - phase)
    new_phase = porous * (
        phase + step_grad * phase_lap - step_well * well + step_drive * heat * growth
    )
    new_heat = heat + step_heat * heat_lap - latent_heat * (new_phase - phase)
    return new_phase, new_heat


def stencil(porous, phase, heat, neighbours):
    def laplace(around, field):
        return around[0] + around[1] + around[2] + around[3] - 6.0 * field

    phase_lap, heat_lap = laplace(neighbours(phase), phase), laplace(neighbours(heat), heat)
    phase, heat = progress(phase, heat, porous, phase_lap, heat_lap)
    around = neighbours(heat)
    phase_lap, heat_lap = laplace(neighbours(phase), phase), laplace(around, heat)
    phase, heat = progress(phase, heat, porous, phase_lap, heat_lap)
    return phase, heat, around[0] - around[1], around[2] - around[3]


def roll(field, step, axis):
    return pltpu.roll(field, step % field.shape[axis], axis)


def walled(wall, field):
    return field if wall is None else jnp.where(wall, 0.0, field)


def ring_neighbours(walls):
    def neighbours(field):
        moves = ((-1, 0), (1, 0), (-1, 1), (1, 1))
        return [walled(wall, roll(field, *move)) for move, wall in zip(moves, walls)]

    return neighbours


def conductivity_contrast(porous, phase):
    conduct = (
        porous * (gas_conduct + (liquid_conduct - gas_conduct) * phase)
        + (1.0 - porous) * solid_conduct
    )
    return conduct - reference_conduct


def shifted_rows(field):
    return roll(field, SHIFT - EDGE, 0)[:TILE_ROWS]


def row_walls(first, row):
    return first & (row == EDGE - 1), first & (row == EDGE)


def polar_kernel(info, porous, phase, heat, above, out, fields):
    talls = with_above(above, porous, phase, heat)
    row = lax.broadcasted_iota(jnp.int32, talls[0].shape, 0)
    walls = row_walls(known(info, GX) == 0.0, row) + (None, None)
    phase_two, heat_two, along_rows, along_columns = stencil(*talls, ring_neighbours(walls))
    fields[0] = shifted_rows(phase_two)
    fields[1] = shifted_rows(heat_two)
    contrast = conductivity_contrast(talls[0], phase_two)
    polars = (
        shifted_rows(contrast * (known(info, SLOPE_X) + gradient_gain * along_rows)),
        shifted_rows(contrast * (known(info, SLOPE_Y) + gradient_gain * along_columns)),
    )
    spare = jnp.zeros((WIDE - TALL, TILE_COLS), jnp.float32)
    sublane = lax.broadcasted_iota(jnp.int32, (EDGE, WIDE), 0)
    lane = lax.broadcasted_iota(jnp.int32, (EDGE, TILE_COLS), 1)
    low = lax.broadcasted_iota(jnp.int32, (EDGE, TILE_COLS), 0) < 4
    edges = []
    for tall in talls:
        flipped = jnp.concatenate([tall, spare], axis=0).T
        edges.append(jnp.where(sublane < 4, flipped[:EDGE], flipped[TILE_COLS - EDGE :]))
    for x in range(TILE_ROWS // SLAB):
        first = EDGE - 2 * SHIFT + SLAB * x
        windows = [
            roll(edge, f * SPAN - first, 1)[:, :TILE_COLS] for f, edge in enumerate(edges)
        ]
        packed = jnp.where(
            lane < SPAN, windows[0], jnp.where(lane < 2 * SPAN, windows[1], windows[2])
        )
        swapped = roll(packed, 4, 0)
        lower, upper = jnp.where(low, packed, swapped), jnp.where(low, swapped, packed)
        both = jnp.where(lane < HALF, lower, roll(upper, HALF, 1))
        rows = slice(x * SLAB, (x + 1) * SLAB)
        start = 2 * x * BLOCK
        out[start : start + SLAB, :] = polars[0][rows]
        rest = roll(jnp.concatenate([both, polars[1][rows]], axis=0), -4, 0)
        out[start + SLAB : start + 2 * BLOCK, :] = rest


def tail_kernel(info, porous, phase, heat, fields, parcel, out):
    ends = [
        jnp.concatenate([field[TILE_ROWS - 2 * EDGE :, :], parcel[f * EDGE : (f + 1) * EDGE, :]])
        for f, field in enumerate((porous, phase, heat))
    ]
    row = lax.broadcasted_iota(jnp.int32, ends[0].shape, 0)
    last = known(info, GX) == ROWS // TILE_ROWS - 1
    walls = (last & (row == 2 * EDGE - 1), last & (row == 2 * EDGE), None, None)
    late = lax.broadcasted_iota(jnp.int32, (EDGE, TILE_COLS), 0) >= EDGE - SHIFT
    for f, end in enumerate(stencil(*ends, ring_neighbours(walls))[:2]):
        whole = roll(fields[f], -SHIFT, 0)
        out[f, : TILE_ROWS - EDGE, :] = whole[: TILE_ROWS - EDGE]
        out[f, TILE_ROWS - EDGE :, :] = jnp.where(
            late, end[EDGE : 2 * EDGE], whole[TILE_ROWS - EDGE :]
        )


def edge_polar(info, data):
    raw = jnp.concatenate([data[pl.ds(SLAB + c, OUTER, stride=BLOCK), :] for c in range(4)], axis=0)
    fields = [raw] + [roll(raw, -f * SPAN, 1) for f in (1, 2)]
    lane = lax.broadcasted_iota(jnp.int32, raw.shape, 1)
    row = lane % HALF
    first = known(info, CHIP) == 0.0
    down_wall, up_wall = first & (row == 2 * SHIFT - 1), first & (row == 2 * SHIFT)
    tile = lax.broadcasted_iota(jnp.int32, (OUTER, TILE_COLS), 0)

    def neighbours(field):
        after = walled(tile == OUTER - 1, roll(roll(field[:OUTER], -1, 0), HALF, 1))
        before = walled(tile == 0, roll(roll(field[3 * OUTER :], 1, 0), HALF, 1))
        return (
            walled(down_wall, roll(field, -1, 1)),
            walled(up_wall, roll(field, 1, 1)),
            jnp.concatenate([field[OUTER:], after], axis=0),
            jnp.concatenate([before, field[: 3 * OUTER]], axis=0),
        )

    phase, heat, along_rows, along_columns = stencil(*fields, neighbours)
    first = known(info, CORE) == 0.0
    along = jnp.where(first, along_rows, along_columns)
    value = jnp.where(first, phase, heat)
    polar = conductivity_contrast(raw, phase) * (known(info, SLOPE) + gradient_gain * along)
    return [[array[c * OUTER : (c + 1) * OUTER] for c in range(4)] for array in (polar, value)]


def pack(columns):
    lane = lax.broadcasted_iota(jnp.int32, (OUTER, TILE_COLS), 1)
    packed = jnp.zeros((OUTER, TILE_COLS), jnp.float32)
    for slot, column in enumerate((2, 3, 0, 1)):
        start = SHIFT + (HALF if column >= 2 else 0)
        moved = roll(columns[column], SLAB * slot - start, 1)
        packed = jnp.where(lane // SLAB == slot, moved, packed)
    return packed


def columns_forward_kernel(
    info, data, porous, phase, heat, order, first, second, twist_cos, twist_sin, out, parcel
):
    polar, value = edge_polar(info, data)
    for f, field in enumerate((porous, phase, heat)):
        parcel[f * EDGE : (f + 1) * EDGE, :] = field[:EDGE, :]
    parcel[3 * EDGE :, :] = pack(value)
    packed = dot(halves(pack(polar)), (order[0], order[1]))
    lane = lax.broadcasted_iota(jnp.int32, (OUTER, TILE_COLS), 1)
    outer = (lane < SHIFT) | (lane >= TILE_COLS - SHIFT)
    parts = []
    for s in range(SLAB):
        around = roll(packed, -EDGE * s - SHIFT, 1)
        parts.append(jnp.where(outer, around, data[pl.ds(s, OUTER, stride=BLOCK), :]))
    rows = jnp.concatenate(parts, axis=1)
    spread = dot((first[0], first[1]), halves(rows))
    cosine, sine = twist_cos[...], twist_sin[...]
    real, imag = [], []
    for s in range(SLAB):
        part = slice(s * 128, (s + 1) * 128)
        re, im = spread[:OUTER, part], spread[OUTER:, part]
        real.append(re * cosine + im * sine)
        imag.append(im * cosine - re * sine)
    for g in range(4):
        span = slice(g * 8, (g + 1) * 8)
        re = jnp.concatenate([part[span] for part in real], axis=0)
        im = jnp.concatenate([part[span] for part in imag], axis=0)
        both = jnp.concatenate([re, im], axis=1)
        final = dot((second[0], second[1]), halves(both), ((1,), (1,)))
        out[pl.ds(2 * g, 64, stride=8), :] = final[:64]
        out[pl.ds(2 * g + 1, 64, stride=8), :] = final[64:]


def columns_backward_kernel(info, data, mine, below, first, second, twist_cos, twist_sin, out):
    real, imag = [], []
    for g in range(4):
        span = slice(g * 8, (g + 1) * 8)
        both = jnp.concatenate(
            [data[pl.ds(2 * g, 64, stride=8), :], data[pl.ds(2 * g + 1, 64, stride=8), :]], axis=0
        )
        spread = dot(halves(both.T), (second[0], second[1]))
        re = spread[:, :128].reshape(SLAB, 8, 128)
        im = spread[:, 128:].reshape(SLAB, 8, 128)
        cosine, sine = twist_cos[span][None], twist_sin[span][None]
        real.append(re * cosine - im * sine)
        imag.append(im * cosine + re * sine)
    stacked = jnp.concatenate(
        [jnp.concatenate([part[s] for part in real + imag], axis=0) for s in range(SLAB)], axis=1
    )
    final = dot((first[0], first[1]), halves(stacked))
    for s in range(SLAB):
        part = final[:, s * 128 : (s + 1) * 128]
        out[pl.ds(s, OUTER, stride=BACK), :] = known(info, SLOPE) - part
    lane = lax.broadcasted_iota(jnp.int32, (SLAB, TILE_COLS), 1)
    slab = known(info, CHIP) - SLAB * known(info, GX)
    late = (slab == 0.0) & (lane % SLAB < SHIFT)
    for core in range(2):
        rows = pl.ds(3 * EDGE + core, SLAB, stride=2)
        start = core * SLAB * BACK + SLAB
        out[pl.ds(start, SLAB, stride=BACK), :] = jnp.where(late, below[rows, :], mine[rows, :])
        out[pl.ds(start + 1, SLAB, stride=BACK), :] = jnp.zeros((SLAB, TILE_COLS), jnp.float32)


def place_kernel(data, fields, columns, phase, heat, gradient):
    lane = lax.broadcasted_iota(jnp.int32, (SLAB, TILE_COLS), 1)
    row = lax.broadcasted_iota(jnp.int32, (SLAB, TILE_COLS), 0)
    own = (lane % SLAB == row) & (lane < 4 * SLAB)
    lane = lax.broadcasted_iota(jnp.int32, (TILE_ROWS, TILE_COLS), 1)
    outer = (lane < SHIFT) | (lane >= TILE_COLS - SHIFT)
    for f, out in enumerate((phase, heat)):
        start = f * SLAB * BACK
        values = data[pl.ds(start + SLAB, SLAB, stride=BACK), :]
        spread = jnp.concatenate(
            [jnp.where(own, values[x : x + 1], 0.0) for x in range(SLAB)], axis=0
        )
        high, rest = halves(spread)
        low = (spread - high.astype(jnp.float32) - rest.astype(jnp.float32)).astype(jnp.bfloat16)
        parts = [
            lax.dot_general(
                part, columns[...], (((1,), (0,)), ((), ())), preferred_element_type=jnp.float32
            )
            for part in (high, rest, low)
        ]
        edge = roll(parts[0] + (parts[1] + parts[2]), -SHIFT, 0)
        out[...] = jnp.where(outer, edge, fields[f])
        for s in range(SLAB):
            gradient[pl.ds(f * TILE_ROWS + s, SLAB, stride=SLAB), :] = data[
                pl.ds(start + s, SLAB, stride=BACK), :
            ]


def wave_numbers(info):
    shape = (CHIPS, 128)
    lane = lax.broadcasted_iota(jnp.int32, shape, 1)
    row_freq = lax.broadcasted_iota(jnp.int32, shape, 0) + CHIPS * (lane // 8)
    row_wave = jnp.where(row_freq >= ROWS // 2, row_freq - ROWS, row_freq).astype(jnp.float32)
    col_wave = 8.0 * known(info, CHIP) + (lane % 8).astype(jnp.float32)
    wave = jnp.where(known(info, CORE) == 0.0, row_wave, col_wave)
    return row_freq, row_wave, col_wave, wave


def rows_forward_kernel(info, data, first, second, twist_cos, twist_sin, out):
    real = data[pl.ds(0, CHIPS, stride=2), :]
    imag = data[pl.ds(1, CHIPS, stride=2), :]
    spread = dot((first[0], first[1]), halves(jnp.concatenate([real, imag], axis=1)))
    re = spread[:CHIPS, :128] + spread[CHIPS:, 128:]
    im = spread[:CHIPS, 128:] - spread[CHIPS:, :128]
    cosine, sine = twist_cos[...], twist_sin[...]
    turned = jnp.concatenate([re * cosine + im * sine, im * cosine - re * sine], axis=1)
    final = dot(halves(turned), (second[0], second[1]))
    wave = wave_numbers(info)[3]
    out[:CHIPS] = wave * final[:, :128]
    out[CHIPS:] = wave * final[:, 128:]


def rows_backward_kernel(info, mine, other, first, second, twist_cos, twist_sin, out):
    row_freq, row_wave, col_wave, wave = wave_numbers(info)
    valid = (
        (row_freq != ROWS // 2)
        & (col_wave != COLS // 2)
        & ((row_freq != 0) | (col_wave != 0.0))
    )
    denom = reference_conduct * jnp.maximum(row_wave * row_wave + col_wave * col_wave, 1.0)
    weight = jnp.where(col_wave == 0.0, 1.0, 2.0) / (ROWS * COLS)
    coef = jnp.where(valid, weight * wave / denom, 0.0)
    along = mine[...] + other[...]
    green = jnp.concatenate([coef * along[:CHIPS], coef * along[CHIPS:]], axis=1)
    spread = dot(halves(green), (second[0], second[1]))
    re, im = spread[:, :128], spread[:, 128:]
    cosine, sine = twist_cos[...], twist_sin[...]
    turned = jnp.concatenate([re * cosine - im * sine, im * cosine + re * sine], axis=1)
    final = dot((first[0], first[1]), halves(turned))
    out[pl.ds(0, CHIPS, stride=2), :] = final[:CHIPS, :128] - final[CHIPS:, 128:]
    out[pl.ds(1, CHIPS, stride=2), :] = final[:CHIPS, 128:] + final[CHIPS:, :128]


def exchange(array, axes, tile):
    blocks = array.reshape((array.size // tile // 128, tile, 128))
    return lax.all_to_all(blocks, axes, split_axis=0, concat_axis=0, tiled=True)


def shift(block, axes, count, step):
    return lax.ppermute(block, axes, [(i, (i + step) % count) for i in range(count)])


def bottom_strip(voxel, wetted, heat):
    bottom = [array[:, TILE_ROWS - EDGE :] for array in (voxel, wetted, heat)]
    parts = bottom[0].astype(jnp.float32), bottom[1].astype(jnp.float32), -bottom[2]
    which = lax.broadcasted_iota(jnp.int32, (3, EDGE, TILE_COLS), 0)
    return jnp.where(which == 0, parts[0], jnp.where(which == 1, parts[1], parts[2]))


def body(voxel, wetted, heat, slope):
    gx_index, gt_index, core = (lax.axis_index(name) for name in ("gx", "gt", "core"))
    gx_size, gt_size, core_size = (lax.axis_size(name) for name in ("gx", "gt", "core"))
    gy_size = gt_size * core_size
    gy = ("gt", "core")
    chips = ("gx", "gt")
    place = jnp.stack([gx_index, gt_index * core_size + core, gx_index * gt_size + gt_index, core])
    (col_to, col_back, columns), (row_to, row_back) = column_tables(), row_tables()
    tile = (TILE_ROWS, TILE_COLS)
    above = shift(bottom_strip(voxel, wetted, heat), "gx", gx_size, 1)
    porous = voxel[0].astype(jnp.float32)
    phase = porous * wetted[0].astype(jnp.float32)
    heat = heat[0]
    (info,) = call(prepare_kernel, [(8, 128)], place.astype(jnp.int32), slope, smem=(0, 1))
    polar, fields = call(
        polar_kernel, [(OUTER * BLOCK, 128), (2,) + tile], info, porous, phase, heat, above
    )
    slab = exchange(polar, gy, 4).reshape(-1, 128)
    spec, parcel = call(
        columns_forward_kernel, [(2 * CHIPS, 128), (3 * EDGE + OUTER, 128)],
        info, slab, porous, phase, heat, *col_to,
    )
    spec = exchange(spec, chips, 2).reshape(-1, 128)
    (mine,) = call(rows_forward_kernel, [(2 * CHIPS, 128)], info, spec, *row_to)
    other = lax.ppermute(mine, "core", [(0, 1), (1, 0)])
    (green,) = call(rows_backward_kernel, [(2 * CHIPS, 128)], info, mine, other, *row_back)
    green, parcel = lax.optimization_barrier((green, parcel))
    below = shift(parcel, "gx", gx_size, -1)
    green = exchange(green, chips, 2).reshape(-1, 128)
    (fields,) = call(tail_kernel, [(2,) + tile], info, porous, phase, heat, fields, below)
    green, below, fields = lax.optimization_barrier((green, below, fields))
    (answer,) = call(
        columns_backward_kernel, [(OUTER * BACK, 128)], info, green, parcel, below, *col_back
    )
    answer = exchange(answer, ("core", "gt"), 2).reshape(-1, 128)
    phase, heat, gradient = call(
        place_kernel, [tile, tile, (2 * TILE_ROWS, TILE_COLS)], answer, fields, columns
    )
    return (phase[None], heat[None], gradient.reshape((2, 1) + tile))


def solution(mesh):
    gx_size, gy_size = mesh.devices.shape
    fine = Mesh(mesh.devices.reshape(gx_size, gy_size // 2, 2), ("gx", "gt", "core"))
    gy = ("gt", "core")
    in_specs = (P(None, "gx", gy), P(None, "gx", gy), P(None, "gx", gy), P())
    out_specs = (P(None, "gx", gy), P(None, "gx", gy), P(None, None, "gx", gy))
    return jax.shard_map(body, mesh=fine, in_specs=in_specs, out_specs=out_specs, check_vma=False)
```

```python
import functools
import math

import jax
import jax.numpy as jnp
import numpy as np
from jax import lax
from jax.experimental import pallas as pl
from jax.experimental.pallas import tpu as pltpu
from jax.sharding import Mesh
from jax.sharding import PartitionSpec as P

solid_conduct = 1.7
gas_conduct = 0.026
liquid_conduct = 0.6
reference_conduct = 0.863
step_grad = 0.1
step_well = 0.3
step_drive = 0.2
step_heat = 0.12
latent_heat = 0.5
gradient_gain = 0.5

TILE_ROWS = 256
TILE_COLS = 128
EDGE = 8
SHIFT = 2
TALL = TILE_ROWS + EDGE
WIDE = 384
OUTER = 32
SLAB = 16
SPAN = 20
HALF = 64
BLOCK = SLAB + 4
BACK = SLAB + 1
CHIPS = 256
COLS = 4096
ROWS = 4096
CORE_MAJOR = np.arange(OUTER).reshape(-1, 2).T.reshape(-1)
VMEM = pl.BlockSpec(memory_space=pltpu.VMEM)
SMEM = pl.BlockSpec(memory_space=pltpu.SMEM)


def halves(array):
    high = array.astype(jnp.bfloat16)
    return high, (array - high.astype(jnp.float32)).astype(jnp.bfloat16)


def dot(left, right, contract=((1,), (0,))):
    def product(x, y):
        return lax.dot_general(x, y, (contract, ((), ())), preferred_element_type=jnp.float32)

    (left_high, left_low), (right_high, right_low) = left, right
    return product(left_high, right_high) + (
        product(left_high, right_low) + product(left_low, right_high)
    )


def call(kernel, outs, *args, smem=(), scratch=()):
    shapes = [jax.ShapeDtypeStruct(shape, jnp.float32) for shape in outs]
    spaces = [SMEM if i in smem else VMEM for i in range(len(args))]
    return pl.pallas_call(
        kernel,
        out_shape=shapes,
        in_specs=spaces,
        out_specs=[VMEM] * len(outs),
        scratch_shapes=list(scratch),
        compiler_params=pltpu.CompilerParams(vmem_limit_bytes=32 * 1024 * 1024),
    )(*args)


def angles(left, right, length):
    product = np.outer(np.arange(left), np.asarray(right)) % length
    return 2.0 * math.pi / length * product


def table(array):
    return jnp.asarray(np.asarray(array, dtype=np.float32))


def split_table(array):
    array = np.asarray(array, dtype=np.float32)
    high = array.astype(jnp.bfloat16)
    low = (array - high.astype(np.float32)).astype(jnp.bfloat16)
    return jnp.asarray(np.stack([high, low]))


def column_tables():
    first = angles(OUTER, range(OUTER), OUTER)
    cosine, sine = np.cos(first), np.sin(first)
    second = angles(64, range(128), 128)
    twist = angles(OUTER, range(128), COLS)
    mix = np.block([[np.cos(second), np.sin(second)], [-np.sin(second), np.cos(second)]])
    slot, s = np.divmod(np.arange(4 * SLAB), SLAB)
    order = np.zeros((128, 128))
    order[np.arange(4 * SLAB), EDGE * s + slot] = 1.0
    every = np.zeros((128 + 2 * OUTER + OUTER, 256))
    every[:128] = mix
    every[128 : 128 + 2 * OUTER, :OUTER] = np.concatenate([cosine, -sine], axis=0)
    every[128 + 2 * OUTER :, : 2 * OUTER] = np.concatenate([cosine, -sine], axis=1)[CORE_MAJOR]
    shared = [split_table(every), table(np.cos(twist)), table(np.sin(twist))]
    columns = np.zeros((128, 128))
    columns[np.arange(4 * SLAB), (slot - SHIFT) % TILE_COLS] = 1.0
    return shared, split_table(order), jnp.asarray(columns.astype(jnp.bfloat16))


def row_tables():
    first = angles(CHIPS, range(CHIPS), CHIPS)
    both = split_table(np.concatenate([np.cos(first), np.sin(first)], axis=0))
    tables = []
    for shift, sign in ((SHIFT, -1.0), (0, 1.0)):
        inner = np.arange(SLAB) - shift
        second = angles(SLAB, inner, SLAB)
        twist = np.repeat(angles(CHIPS, inner, ROWS), 8, axis=1)
        cosine, sine = np.kron(np.cos(second), np.eye(8)), sign * np.kron(np.sin(second), np.eye(8))
        if shift:
            cosine, sine = cosine.T, sine.T
        mix = np.block([[cosine, sine], [-sine, cosine]])
        tables.append([both, split_table(mix), table(np.cos(twist)), table(np.sin(twist))])
    return tables


GX, GY, CHIP, CORE, SLOPE_X, SLOPE_Y, SLOPE = range(7)


def prepare_kernel(place, slope, info):
    values = [place[i].astype(jnp.float32) for i in range(4)] + [slope[0, 0], slope[0, 1]]
    values.append(jnp.where(place[3] == 0, slope[0, 0], slope[0, 1]))
    row = lax.broadcasted_iota(jnp.int32, info.shape, 0)
    filled = jnp.zeros(info.shape, jnp.float32)
    for i, value in enumerate(values):
        filled = jnp.where(row == i, value, filled)
    info[...] = filled


def known(info, i):
    return info[i : i + 1, :]


def with_above(above, porous, phase, heat):
    tops = (above[0], above[0] * above[1], -above[2])
    return [
        jnp.concatenate([top, field[...]], axis=0) for top, field in zip(tops, (porous, phase, heat))
    ]


def progress(phase, heat, porous, phase_lap, heat_lap):
    well = 2.0 * phase * (1.0 - phase) * (1.0 - 2.0 * phase)
    growth = 30.0 * phase * phase * (1.0 - phase) * (1.0 - phase)
    new_phase = porous * (
        phase + step_grad * phase_lap - step_well * well + step_drive * heat * growth
    )
    new_heat = heat + step_heat * heat_lap - latent_heat * (new_phase - phase)
    return new_phase, new_heat


def stencil(porous, phase, heat, neighbours):
    def laplace(around, field):
        return around[0] + around[1] + around[2] + around[3] - 6.0 * field

    phase_lap, heat_lap = laplace(neighbours(phase), phase), laplace(neighbours(heat), heat)
    phase, heat = progress(phase, heat, porous, phase_lap, heat_lap)
    around = neighbours(heat)
    phase_lap, heat_lap = laplace(neighbours(phase), phase), laplace(around, heat)
    phase, heat = progress(phase, heat, porous, phase_lap, heat_lap)
    return phase, heat, around[0] - around[1], around[2] - around[3]


def roll(field, step, axis):
    return pltpu.roll(field, step % field.shape[axis], axis)


def walled(wall, field):
    return field if wall is None else jnp.where(wall, 0.0, field)


def ring_neighbours(walls):
    def neighbours(field):
        moves = ((-1, 0), (1, 0), (-1, 1), (1, 1))
        return [walled(wall, roll(field, *move)) for move, wall in zip(moves, walls)]

    return neighbours


def conductivity_contrast(porous, phase):
    conduct = (
        porous * (gas_conduct + (liquid_conduct - gas_conduct) * phase)
        + (1.0 - porous) * solid_conduct
    )
    return conduct - reference_conduct


def shifted_rows(field):
    return roll(field, SHIFT - EDGE, 0)[:TILE_ROWS]


def row_walls(first, row):
    return first & (row == EDGE - 1), first & (row == EDGE)


def polar_kernel(info, porous, phase, heat, above, out, fields):
    talls = with_above(above, porous, phase, heat)
    row = lax.broadcasted_iota(jnp.int32, talls[0].shape, 0)
    walls = row_walls(known(info, GX) == 0.0, row) + (None, None)
    phase_two, heat_two, along_rows, along_columns = stencil(*talls, ring_neighbours(walls))
    fields[0] = shifted_rows(phase_two)
    fields[1] = shifted_rows(heat_two)
    contrast = conductivity_contrast(talls[0], phase_two)
    polars = (
        shifted_rows(contrast * (known(info, SLOPE_X) + gradient_gain * along_rows)),
        shifted_rows(contrast * (known(info, SLOPE_Y) + gradient_gain * along_columns)),
    )
    spare = jnp.zeros((WIDE - TALL, TILE_COLS), jnp.float32)
    sublane = lax.broadcasted_iota(jnp.int32, (EDGE, WIDE), 0)
    lane = lax.broadcasted_iota(jnp.int32, (EDGE, TILE_COLS), 1)
    low = lax.broadcasted_iota(jnp.int32, (EDGE, TILE_COLS), 0) < 4
    edges = []
    for tall in talls:
        flipped = jnp.concatenate([tall, spare], axis=0).T
        edges.append(jnp.where(sublane < 4, flipped[:EDGE], flipped[TILE_COLS - EDGE :]))
    for x in range(TILE_ROWS // SLAB):
        first = EDGE - 2 * SHIFT + SLAB * x
        windows = [
            roll(edge, f * SPAN - first, 1)[:, :TILE_COLS] for f, edge in enumerate(edges)
        ]
        packed = jnp.where(
            lane < SPAN, windows[0], jnp.where(lane < 2 * SPAN, windows[1], windows[2])
        )
        swapped = roll(packed, 4, 0)
        lower, upper = jnp.where(low, packed, swapped), jnp.where(low, swapped, packed)
        both = jnp.where(lane < HALF, lower, roll(upper, HALF, 1))
        rows = slice(x * SLAB, (x + 1) * SLAB)
        start = 2 * x * BLOCK
        out[start : start + SLAB, :] = polars[0][rows]
        rest = roll(jnp.concatenate([both, polars[1][rows]], axis=0), -4, 0)
        out[start + SLAB : start + 2 * BLOCK, :] = rest


def tail_kernel(info, porous, phase, heat, fields, parcel, out):
    ends = [
        jnp.concatenate([field[TILE_ROWS - 2 * EDGE :, :], parcel[f * EDGE : (f + 1) * EDGE, :]])
        for f, field in enumerate((porous, phase, heat))
    ]
    row = lax.broadcasted_iota(jnp.int32, ends[0].shape, 0)
    last = known(info, GX) == ROWS // TILE_ROWS - 1
    walls = (last & (row == 2 * EDGE - 1), last & (row == 2 * EDGE), None, None)
    late = lax.broadcasted_iota(jnp.int32, (EDGE, TILE_COLS), 0) >= EDGE - SHIFT
    for f, end in enumerate(stencil(*ends, ring_neighbours(walls))[:2]):
        whole = roll(fields[f], -SHIFT, 0)
        out[f, : TILE_ROWS - EDGE, :] = whole[: TILE_ROWS - EDGE]
        out[f, TILE_ROWS - EDGE :, :] = jnp.where(
            late, end[EDGE : 2 * EDGE], whole[TILE_ROWS - EDGE :]
        )


def edge_polar(info, data):
    raw = jnp.concatenate([data[pl.ds(SLAB + c, OUTER, stride=BLOCK), :] for c in range(4)], axis=0)
    fields = [raw] + [roll(raw, -f * SPAN, 1) for f in (1, 2)]
    lane = lax.broadcasted_iota(jnp.int32, raw.shape, 1)
    row = lane % HALF
    first = known(info, CHIP) == 0.0
    down_wall, up_wall = first & (row == 2 * SHIFT - 1), first & (row == 2 * SHIFT)
    tile = lax.broadcasted_iota(jnp.int32, (OUTER, TILE_COLS), 0)

    def neighbours(field):
        after = walled(tile == OUTER - 1, roll(roll(field[:OUTER], -1, 0), HALF, 1))
        before = walled(tile == 0, roll(roll(field[3 * OUTER :], 1, 0), HALF, 1))
        return (
            walled(down_wall, roll(field, -1, 1)),
            walled(up_wall, roll(field, 1, 1)),
            jnp.concatenate([field[OUTER:], after], axis=0),
            jnp.concatenate([before, field[: 3 * OUTER]], axis=0),
        )

    phase, heat, along_rows, along_columns = stencil(*fields, neighbours)
    first = known(info, CORE) == 0.0
    along = jnp.where(first, along_rows, along_columns)
    value = jnp.where(first, phase, heat)
    polar = conductivity_contrast(raw, phase) * (known(info, SLOPE) + gradient_gain * along)
    return [[array[c * OUTER : (c + 1) * OUTER] for c in range(4)] for array in (polar, value)]


def pack(columns):
    lane = lax.broadcasted_iota(jnp.int32, (OUTER, TILE_COLS), 1)
    packed = jnp.zeros((OUTER, TILE_COLS), jnp.float32)
    for slot, column in enumerate((2, 3, 0, 1)):
        start = SHIFT + (HALF if column >= 2 else 0)
        moved = roll(columns[column], SLAB * slot - start, 1)
        packed = jnp.where(lane // SLAB == slot, moved, packed)
    return packed


def columns_forward_kernel(
    info, data, porous, phase, heat, order, every, twist_cos, twist_sin, out, parcel
):
    polar, value = edge_polar(info, data)
    for f, field in enumerate((porous, phase, heat)):
        parcel[f * EDGE : (f + 1) * EDGE, :] = field[:EDGE, :]
    parcel[3 * EDGE :, :] = pack(value)
    packed = dot(halves(pack(polar)), (order[0], order[1]))
    lane = lax.broadcasted_iota(jnp.int32, (OUTER, TILE_COLS), 1)
    outer = (lane < SHIFT) | (lane >= TILE_COLS - SHIFT)
    parts = []
    for s in range(SLAB):
        around = roll(packed, -EDGE * s - SHIFT, 1)
        parts.append(jnp.where(outer, around, data[pl.ds(s, OUTER, stride=BLOCK), :]))
    rows = jnp.concatenate(parts, axis=1)
    first = slice(128, 128 + 2 * OUTER)
    spread = dot((every[0, first, :OUTER], every[1, first, :OUTER]), halves(rows))
    cosine, sine = twist_cos[...], twist_sin[...]
    real, imag = [], []
    for s in range(SLAB):
        part = slice(s * 128, (s + 1) * 128)
        re, im = spread[:OUTER, part], spread[OUTER:, part]
        real.append(re * cosine + im * sine)
        imag.append(im * cosine - re * sine)
    for g in range(4):
        span = slice(g * 8, (g + 1) * 8)
        re = jnp.concatenate([part[span] for part in real], axis=0)
        im = jnp.concatenate([part[span] for part in imag], axis=0)
        both = jnp.concatenate([re, im], axis=1)
        final = dot((every[0, :128], every[1, :128]), halves(both), ((1,), (1,)))
        out[pl.ds(2 * g, 64, stride=8), :] = final[:64]
        out[pl.ds(2 * g + 1, 64, stride=8), :] = final[64:]


def columns_backward_kernel(info, data, mine, below, every, twist_cos, twist_sin, out):
    real, imag = [], []
    for g in range(4):
        span = slice(g * 8, (g + 1) * 8)
        both = jnp.concatenate(
            [data[pl.ds(2 * g, 64, stride=8), :], data[pl.ds(2 * g + 1, 64, stride=8), :]], axis=0
        )
        spread = dot(halves(both.T), (every[0, :128], every[1, :128]))
        re = spread[:, :128].reshape(SLAB, 8, 128)
        im = spread[:, 128:].reshape(SLAB, 8, 128)
        cosine, sine = twist_cos[span][None], twist_sin[span][None]
        real.append(re * cosine - im * sine)
        imag.append(im * cosine + re * sine)
    stacked = jnp.concatenate(
        [jnp.concatenate([part[s] for part in real + imag], axis=0) for s in range(SLAB)], axis=1
    )
    first = slice(128 + 2 * OUTER, 128 + 3 * OUTER)
    final = dot((every[0, first, : 2 * OUTER], every[1, first, : 2 * OUTER]), halves(stacked))
    for s in range(SLAB):
        part = final[:, s * 128 : (s + 1) * 128]
        out[pl.ds(s, OUTER, stride=BACK), :] = known(info, SLOPE) - part
    lane = lax.broadcasted_iota(jnp.int32, (SLAB, TILE_COLS), 1)
    slab = known(info, CHIP) - SLAB * known(info, GX)
    late = (slab == 0.0) & (lane % SLAB < SHIFT)
    for core in range(2):
        rows = pl.ds(3 * EDGE + core, SLAB, stride=2)
        start = core * SLAB * BACK + SLAB
        out[pl.ds(start, SLAB, stride=BACK), :] = jnp.where(late, below[rows, :], mine[rows, :])


def place_kernel(data, fields, columns, phase, heat, gradient):
    lane = lax.broadcasted_iota(jnp.int32, (SLAB, TILE_COLS), 1)
    row = lax.broadcasted_iota(jnp.int32, (SLAB, TILE_COLS), 0)
    own = (lane % SLAB == row) & (lane < 4 * SLAB)
    lane = lax.broadcasted_iota(jnp.int32, (TILE_ROWS, TILE_COLS), 1)
    outer = (lane < SHIFT) | (lane >= TILE_COLS - SHIFT)
    for f, out in enumerate((phase, heat)):
        start = f * SLAB * BACK
        values = data[pl.ds(start + SLAB, SLAB, stride=BACK), :]
        spread = jnp.concatenate(
            [jnp.where(own, values[x : x + 1], 0.0) for x in range(SLAB)], axis=0
        )
        high, rest = halves(spread)
        low = (spread - high.astype(jnp.float32) - rest.astype(jnp.float32)).astype(jnp.bfloat16)
        parts = [
            lax.dot_general(
                part, columns[...], (((1,), (0,)), ((), ())), preferred_element_type=jnp.float32
            )
            for part in (high, rest, low)
        ]
        edge = roll(parts[0] + (parts[1] + parts[2]), -SHIFT, 0)
        out[...] = jnp.where(outer, edge, fields[f])
        for s in range(SLAB):
            gradient[pl.ds(f * TILE_ROWS + s, SLAB, stride=SLAB), :] = data[
                pl.ds(start + s, SLAB, stride=BACK), :
            ]


def wave_numbers(info):
    shape = (CHIPS, 128)
    lane = lax.broadcasted_iota(jnp.int32, shape, 1)
    row_freq = lax.broadcasted_iota(jnp.int32, shape, 0) + CHIPS * (lane // 8)
    row_wave = jnp.where(row_freq >= ROWS // 2, row_freq - ROWS, row_freq).astype(jnp.float32)
    col_wave = 8.0 * known(info, CHIP) + (lane % 8).astype(jnp.float32)
    wave = jnp.where(known(info, CORE) == 0.0, row_wave, col_wave)
    return row_freq, row_wave, col_wave, wave


def rows_forward_kernel(info, data, first, second, twist_cos, twist_sin, out):
    real = data[pl.ds(0, CHIPS, stride=2), :]
    imag = data[pl.ds(1, CHIPS, stride=2), :]
    spread = dot((first[0], first[1]), halves(jnp.concatenate([real, imag], axis=1)))
    re = spread[:CHIPS, :128] + spread[CHIPS:, 128:]
    im = spread[:CHIPS, 128:] - spread[CHIPS:, :128]
    cosine, sine = twist_cos[...], twist_sin[...]
    turned = jnp.concatenate([re * cosine + im * sine, im * cosine - re * sine], axis=1)
    final = dot(halves(turned), (second[0], second[1]))
    wave = wave_numbers(info)[3]
    out[:CHIPS] = wave * final[:, :128]
    out[CHIPS:] = wave * final[:, 128:]


def rows_backward_kernel(info, mine, other, first, second, twist_cos, twist_sin, out):
    row_freq, row_wave, col_wave, wave = wave_numbers(info)
    valid = (
        (row_freq != ROWS // 2)
        & (col_wave != COLS // 2)
        & ((row_freq != 0) | (col_wave != 0.0))
    )
    denom = reference_conduct * jnp.maximum(row_wave * row_wave + col_wave * col_wave, 1.0)
    weight = jnp.where(col_wave == 0.0, 1.0, 2.0) / (ROWS * COLS)
    coef = jnp.where(valid, weight * wave / denom, 0.0)
    along = mine[...] + other[...]
    green = jnp.concatenate([coef * along[:CHIPS], coef * along[CHIPS:]], axis=1)
    spread = dot(halves(green), (second[0], second[1]))
    re, im = spread[:, :128], spread[:, 128:]
    cosine, sine = twist_cos[...], twist_sin[...]
    turned = jnp.concatenate([re * cosine - im * sine, im * cosine + re * sine], axis=1)
    final = dot((first[0], first[1]), halves(turned))
    out[pl.ds(0, CHIPS, stride=2), :] = final[:CHIPS, :128] - final[CHIPS:, 128:]
    out[pl.ds(1, CHIPS, stride=2), :] = final[:CHIPS, 128:] + final[CHIPS:, :128]


def exchange(array, axes, tile):
    blocks = array.reshape((array.size // tile // 128, tile, 128))
    return lax.all_to_all(blocks, axes, split_axis=0, concat_axis=0, tiled=True)


def shift(block, axes, count, step):
    return lax.ppermute(block, axes, [(i, (i + step) % count) for i in range(count)])


def bottom_strip(voxel, wetted, heat):
    bottom = [array[:, TILE_ROWS - EDGE :] for array in (voxel, wetted, heat)]
    parts = bottom[0].astype(jnp.float32), bottom[1].astype(jnp.float32), -bottom[2]
    which = lax.broadcasted_iota(jnp.int32, (3, EDGE, TILE_COLS), 0)
    return jnp.where(which == 0, parts[0], jnp.where(which == 1, parts[1], parts[2]))


def body(voxel, wetted, heat, slope):
    gx_index, gt_index, core = (lax.axis_index(name) for name in ("gx", "gt", "core"))
    gx_size, gt_size, core_size = (lax.axis_size(name) for name in ("gx", "gt", "core"))
    gy_size = gt_size * core_size
    gy = ("gt", "core")
    chips = ("gx", "gt")
    place = jnp.stack([gx_index, gt_index * core_size + core, gx_index * gt_size + gt_index, core])
    (shared, order, columns), (row_to, row_back) = column_tables(), row_tables()
    tile = (TILE_ROWS, TILE_COLS)
    above = shift(bottom_strip(voxel, wetted, heat), "gx", gx_size, 1)
    porous = voxel[0].astype(jnp.float32)
    phase = porous * wetted[0].astype(jnp.float32)
    heat = heat[0]
    (info,) = call(prepare_kernel, [(8, 128)], place.astype(jnp.int32), slope, smem=(0, 1))
    polar, fields = call(
        polar_kernel, [(OUTER * BLOCK, 128), (2,) + tile], info, porous, phase, heat, above
    )
    slab = exchange(polar, gy, 4).reshape(-1, 128)
    spec, parcel = call(
        columns_forward_kernel, [(2 * CHIPS, 128), (3 * EDGE + OUTER, 128)],
        info, slab, porous, phase, heat, order, *shared,
    )
    spec = exchange(spec, chips, 2).reshape(-1, 128)
    (mine,) = call(rows_forward_kernel, [(2 * CHIPS, 128)], info, spec, *row_to)
    other = lax.ppermute(mine, "core", [(0, 1), (1, 0)])
    (green,) = call(rows_backward_kernel, [(2 * CHIPS, 128)], info, mine, other, *row_back)
    green, parcel = lax.optimization_barrier((green, parcel))
    below = shift(parcel, "gx", gx_size, -1)
    green = exchange(green, chips, 2).reshape(-1, 128)
    (fields,) = call(tail_kernel, [(2,) + tile], info, porous, phase, heat, fields, below)
    green, below, fields = lax.optimization_barrier((green, below, fields))
    (answer,) = call(
        columns_backward_kernel, [(OUTER * BACK, 128)], info, green, parcel, below, *shared
    )
    answer = exchange(answer, ("core", "gt"), 1).reshape(-1, 128)
    phase, heat, gradient = call(
        place_kernel, [tile, tile, (2 * TILE_ROWS, TILE_COLS)], answer, fields, columns
    )
    return (phase[None], heat[None], gradient.reshape((2, 1) + tile))


def solution(mesh):
    gx_size, gy_size = mesh.devices.shape
    fine = Mesh(mesh.devices.reshape(gx_size, gy_size // 2, 2), ("gx", "gt", "core"))
    gy = ("gt", "core")
    in_specs = (P(None, "gx", gy), P(None, "gx", gy), P(None, "gx", gy), P())
    out_specs = (P(None, "gx", gy), P(None, "gx", gy), P(None, None, "gx", gy))
    return jax.shard_map(body, mesh=fine, in_specs=in_specs, out_specs=out_specs, check_vma=False)
```

```python
import functools
import math

import jax
import jax.numpy as jnp
import numpy as np
from jax import lax
from jax.experimental import pallas as pl
from jax.experimental.pallas import tpu as pltpu
from jax.sharding import Mesh
from jax.sharding import PartitionSpec as P

solid_conduct = 1.7
gas_conduct = 0.026
liquid_conduct = 0.6
reference_conduct = 0.863
step_grad = 0.1
step_well = 0.3
step_drive = 0.2
step_heat = 0.12
latent_heat = 0.5
gradient_gain = 0.5

TILE_ROWS = 256
TILE_COLS = 128
EDGE = 8
SHIFT = 2
TALL = TILE_ROWS + EDGE
WIDE = 384
OUTER = 32
SLAB = 16
SPAN = 20
HALF = 64
BLOCK = SLAB + 4
BACK = SLAB + 1
CHIPS = 256
COLS = 4096
ROWS = 4096
CORE_MAJOR = np.arange(OUTER).reshape(-1, 2).T.reshape(-1)
SIZES = {"z": 8, "y_hi": 2, "x": 4, "y_lo": 4, "core": 2}
GX_AXES, GY_AXES = ("z", "y_hi"), ("x", "y_lo", "core")
CHIP_AXES = ("y_lo", "x", "y_hi", "z")
CHIP_ORDER = np.arange(CHIPS).reshape(8, 2, 4, 4).transpose(3, 2, 1, 0).reshape(-1)
VMEM = pl.BlockSpec(memory_space=pltpu.VMEM)
SMEM = pl.BlockSpec(memory_space=pltpu.SMEM)


def halves(array):
    high = array.astype(jnp.bfloat16)
    return high, (array - high.astype(jnp.float32)).astype(jnp.bfloat16)


def dot(left, right, contract=((1,), (0,))):
    def product(x, y):
        return lax.dot_general(x, y, (contract, ((), ())), preferred_element_type=jnp.float32)

    (left_high, left_low), (right_high, right_low) = left, right
    return product(left_high, right_high) + (
        product(left_high, right_low) + product(left_low, right_high)
    )


def call(kernel, outs, *args, smem=(), scratch=()):
    shapes = [jax.ShapeDtypeStruct(shape, jnp.float32) for shape in outs]
    spaces = [SMEM if i in smem else VMEM for i in range(len(args))]
    return pl.pallas_call(
        kernel,
        out_shape=shapes,
        in_specs=spaces,
        out_specs=[VMEM] * len(outs),
        scratch_shapes=list(scratch),
        compiler_params=pltpu.CompilerParams(vmem_limit_bytes=32 * 1024 * 1024),
    )(*args)


def angles(left, right, length):
    product = np.outer(np.arange(left), np.asarray(right)) % length
    return 2.0 * math.pi / length * product


def table(array):
    return jnp.asarray(np.asarray(array, dtype=np.float32))


def split_table(array):
    array = np.asarray(array, dtype=np.float32)
    high = array.astype(jnp.bfloat16)
    low = (array - high.astype(np.float32)).astype(jnp.bfloat16)
    return jnp.asarray(np.stack([high, low]))


def column_tables():
    first = angles(OUTER, range(OUTER), OUTER)
    cosine, sine = np.cos(first), np.sin(first)
    second = angles(64, range(128), 128)
    twist = angles(OUTER, range(128), COLS)
    mix = np.block([[np.cos(second), np.sin(second)], [-np.sin(second), np.cos(second)]])
    slot, s = np.divmod(np.arange(4 * SLAB), SLAB)
    order = np.zeros((128, 128))
    order[np.arange(4 * SLAB), EDGE * s + slot] = 1.0
    every = np.zeros((128 + 2 * OUTER + OUTER, 256))
    every[:128] = mix
    every[128 : 128 + 2 * OUTER, :OUTER] = np.concatenate([cosine, -sine], axis=0)
    every[128 + 2 * OUTER :, : 2 * OUTER] = np.concatenate([cosine, -sine], axis=1)[CORE_MAJOR]
    shared = [split_table(every), table(np.cos(twist)), table(np.sin(twist))]
    columns = np.zeros((128, 128))
    columns[np.arange(4 * SLAB), (slot - SHIFT) % TILE_COLS] = 1.0
    return shared, split_table(order), jnp.asarray(columns.astype(jnp.bfloat16))


def row_tables():
    first = angles(CHIPS, range(CHIPS), CHIPS)
    cosine, sine = np.cos(first)[:, CHIP_ORDER], np.sin(first)[:, CHIP_ORDER]
    starts = (np.concatenate([cosine, sine], axis=0), np.concatenate([cosine.T, sine.T], axis=0))
    tables = []
    for shift, sign, start in ((SHIFT, -1.0, starts[0]), (0, 1.0, starts[1])):
        inner = np.arange(SLAB) - shift
        second = angles(SLAB, inner, SLAB)
        twist = np.repeat(angles(CHIPS, inner, ROWS), 8, axis=1)
        cosine, sine = np.kron(np.cos(second), np.eye(8)), sign * np.kron(np.sin(second), np.eye(8))
        if shift:
            cosine, sine = cosine.T, sine.T
        mix = np.block([[cosine, sine], [-sine, cosine]])
        rest = [split_table(mix), table(np.cos(twist)), table(np.sin(twist))]
        tables.append([split_table(start)] + rest)
    return tables


GX, GY, CHIP, CORE, PLACE, SLOPE_X, SLOPE_Y, SLOPE = range(8)


def prepare_kernel(place, slope, info):
    values = [place[i].astype(jnp.float32) for i in range(5)] + [slope[0, 0], slope[0, 1]]
    values.append(jnp.where(place[3] == 0, slope[0, 0], slope[0, 1]))
    row = lax.broadcasted_iota(jnp.int32, info.shape, 0)
    filled = jnp.zeros(info.shape, jnp.float32)
    for i, value in enumerate(values):
        filled = jnp.where(row == i, value, filled)
    info[...] = filled


def known(info, i):
    return info[i : i + 1, :]


def with_above(above, porous, phase, heat):
    tops = (above[0], above[0] * above[1], -above[2])
    return [
        jnp.concatenate([top, field[...]], axis=0) for top, field in zip(tops, (porous, phase, heat))
    ]


def progress(phase, heat, porous, phase_lap, heat_lap):
    well = 2.0 * phase * (1.0 - phase) * (1.0 - 2.0 * phase)
    growth = 30.0 * phase * phase * (1.0 - phase) * (1.0 - phase)
    new_phase = porous * (
        phase + step_grad * phase_lap - step_well * well + step_drive * heat * growth
    )
    new_heat = heat + step_heat * heat_lap - latent_heat * (new_phase - phase)
    return new_phase, new_heat


def stencil(porous, phase, heat, neighbours):
    def laplace(around, field):
        return around[0] + around[1] + around[2] + around[3] - 6.0 * field

    phase_lap, heat_lap = laplace(neighbours(phase), phase), laplace(neighbours(heat), heat)
    phase, heat = progress(phase, heat, porous, phase_lap, heat_lap)
    around = neighbours(heat)
    phase_lap, heat_lap = laplace(neighbours(phase), phase), laplace(around, heat)
    phase, heat = progress(phase, heat, porous, phase_lap, heat_lap)
    return phase, heat, around[0] - around[1], around[2] - around[3]


def roll(field, step, axis):
    return pltpu.roll(field, step % field.shape[axis], axis)


def walled(wall, field):
    return field if wall is None else jnp.where(wall, 0.0, field)


def ring_neighbours(walls):
    def neighbours(field):
        moves = ((-1, 0), (1, 0), (-1, 1), (1, 1))
        return [walled(wall, roll(field, *move)) for move, wall in zip(moves, walls)]

    return neighbours


def conductivity_contrast(porous, phase):
    conduct = (
        porous * (gas_conduct + (liquid_conduct - gas_conduct) * phase)
        + (1.0 - porous) * solid_conduct
    )
    return conduct - reference_conduct


def shifted_rows(field):
    return roll(field, SHIFT - EDGE, 0)[:TILE_ROWS]


def row_walls(first, row):
    return first & (row == EDGE - 1), first & (row == EDGE)


def polar_kernel(info, porous, phase, heat, above, out, fields):
    talls = with_above(above, porous, phase, heat)
    row = lax.broadcasted_iota(jnp.int32, talls[0].shape, 0)
    walls = row_walls(known(info, GX) == 0.0, row) + (None, None)
    phase_two, heat_two, along_rows, along_columns = stencil(*talls, ring_neighbours(walls))
    fields[0] = shifted_rows(phase_two)
    fields[1] = shifted_rows(heat_two)
    contrast = conductivity_contrast(talls[0], phase_two)
    polars = (
        shifted_rows(contrast * (known(info, SLOPE_X) + gradient_gain * along_rows)),
        shifted_rows(contrast * (known(info, SLOPE_Y) + gradient_gain * along_columns)),
    )
    spare = jnp.zeros((WIDE - TALL, TILE_COLS), jnp.float32)
    sublane = lax.broadcasted_iota(jnp.int32, (EDGE, WIDE), 0)
    lane = lax.broadcasted_iota(jnp.int32, (EDGE, TILE_COLS), 1)
    low = lax.broadcasted_iota(jnp.int32, (EDGE, TILE_COLS), 0) < 4
    edges = []
    for tall in talls:
        flipped = jnp.concatenate([tall, spare], axis=0).T
        edges.append(jnp.where(sublane < 4, flipped[:EDGE], flipped[TILE_COLS - EDGE :]))
    for x in range(TILE_ROWS // SLAB):
        first = EDGE - 2 * SHIFT + SLAB * x
        windows = [
            roll(edge, f * SPAN - first, 1)[:, :TILE_COLS] for f, edge in enumerate(edges)
        ]
        packed = jnp.where(
            lane < SPAN, windows[0], jnp.where(lane < 2 * SPAN, windows[1], windows[2])
        )
        swapped = roll(packed, 4, 0)
        lower, upper = jnp.where(low, packed, swapped), jnp.where(low, swapped, packed)
        both = jnp.where(lane < HALF, lower, roll(upper, HALF, 1))
        rows = slice(x * SLAB, (x + 1) * SLAB)
        start = 2 * x * BLOCK
        out[start : start + SLAB, :] = polars[0][rows]
        rest = roll(jnp.concatenate([both, polars[1][rows]], axis=0), -4, 0)
        out[start + SLAB : start + 2 * BLOCK, :] = rest


def tail_kernel(info, porous, phase, heat, fields, parcel, out):
    ends = [
        jnp.concatenate([field[TILE_ROWS - 2 * EDGE :, :], parcel[f * EDGE : (f + 1) * EDGE, :]])
        for f, field in enumerate((porous, phase, heat))
    ]
    row = lax.broadcasted_iota(jnp.int32, ends[0].shape, 0)
    last = known(info, GX) == ROWS // TILE_ROWS - 1
    walls = (last & (row == 2 * EDGE - 1), last & (row == 2 * EDGE), None, None)
    late = lax.broadcasted_iota(jnp.int32, (EDGE, TILE_COLS), 0) >= EDGE - SHIFT
    for f, end in enumerate(stencil(*ends, ring_neighbours(walls))[:2]):
        whole = roll(fields[f], -SHIFT, 0)
        out[f, : TILE_ROWS - EDGE, :] = whole[: TILE_ROWS - EDGE]
        out[f, TILE_ROWS - EDGE :, :] = jnp.where(
            late, end[EDGE : 2 * EDGE], whole[TILE_ROWS - EDGE :]
        )


def edge_polar(info, data):
    raw = jnp.concatenate([data[pl.ds(SLAB + c, OUTER, stride=BLOCK), :] for c in range(4)], axis=0)
    fields = [raw] + [roll(raw, -f * SPAN, 1) for f in (1, 2)]
    lane = lax.broadcasted_iota(jnp.int32, raw.shape, 1)
    row = lane % HALF
    first = known(info, CHIP) == 0.0
    down_wall, up_wall = first & (row == 2 * SHIFT - 1), first & (row == 2 * SHIFT)
    tile = lax.broadcasted_iota(jnp.int32, (OUTER, TILE_COLS), 0)

    def neighbours(field):
        after = walled(tile == OUTER - 1, roll(roll(field[:OUTER], -1, 0), HALF, 1))
        before = walled(tile == 0, roll(roll(field[3 * OUTER :], 1, 0), HALF, 1))
        return (
            walled(down_wall, roll(field, -1, 1)),
            walled(up_wall, roll(field, 1, 1)),
            jnp.concatenate([field[OUTER:], after], axis=0),
            jnp.concatenate([before, field[: 3 * OUTER]], axis=0),
        )

    phase, heat, along_rows, along_columns = stencil(*fields, neighbours)
    first = known(info, CORE) == 0.0
    along = jnp.where(first, along_rows, along_columns)
    value = jnp.where(first, phase, heat)
    polar = conductivity_contrast(raw, phase) * (known(info, SLOPE) + gradient_gain * along)
    return [[array[c * OUTER : (c + 1) * OUTER] for c in range(4)] for array in (polar, value)]


def pack(columns):
    lane = lax.broadcasted_iota(jnp.int32, (OUTER, TILE_COLS), 1)
    packed = jnp.zeros((OUTER, TILE_COLS), jnp.float32)
    for slot, column in enumerate((2, 3, 0, 1)):
        start = SHIFT + (HALF if column >= 2 else 0)
        moved = roll(columns[column], SLAB * slot - start, 1)
        packed = jnp.where(lane // SLAB == slot, moved, packed)
    return packed


def columns_forward_kernel(
    info, data, porous, phase, heat, order, every, twist_cos, twist_sin, out, parcel
):
    polar, value = edge_polar(info, data)
    for f, field in enumerate((porous, phase, heat)):
        parcel[f * EDGE : (f + 1) * EDGE, :] = field[:EDGE, :]
    parcel[3 * EDGE :, :] = pack(value)
    packed = dot(halves(pack(polar)), (order[0], order[1]))
    lane = lax.broadcasted_iota(jnp.int32, (OUTER, TILE_COLS), 1)
    outer = (lane < SHIFT) | (lane >= TILE_COLS - SHIFT)
    parts = []
    for s in range(SLAB):
        around = roll(packed, -EDGE * s - SHIFT, 1)
        parts.append(jnp.where(outer, around, data[pl.ds(s, OUTER, stride=BLOCK), :]))
    rows = jnp.concatenate(parts, axis=1)
    first = slice(128, 128 + 2 * OUTER)
    spread = dot((every[0, first, :OUTER], every[1, first, :OUTER]), halves(rows))
    cosine, sine = twist_cos[...], twist_sin[...]
    real, imag = [], []
    for s in range(SLAB):
        part = slice(s * 128, (s + 1) * 128)
        re, im = spread[:OUTER, part], spread[OUTER:, part]
        real.append(re * cosine + im * sine)
        imag.append(im * cosine - re * sine)
    for g in range(4):
        span = slice(g * 8, (g + 1) * 8)
        re = jnp.concatenate([part[span] for part in real], axis=0)
        im = jnp.concatenate([part[span] for part in imag], axis=0)
        both = jnp.concatenate([re, im], axis=1)
        final = dot((every[0, :128], every[1, :128]), halves(both), ((1,), (1,)))
        out[pl.ds(2 * g, 64, stride=8), :] = final[:64]
        out[pl.ds(2 * g + 1, 64, stride=8), :] = final[64:]


def columns_backward_kernel(info, data, mine, below, every, twist_cos, twist_sin, out):
    real, imag = [], []
    for g in range(4):
        span = slice(g * 8, (g + 1) * 8)
        both = jnp.concatenate(
            [data[pl.ds(2 * g, 64, stride=8), :], data[pl.ds(2 * g + 1, 64, stride=8), :]], axis=0
        )
        spread = dot(halves(both.T), (every[0, :128], every[1, :128]))
        re = spread[:, :128].reshape(SLAB, 8, 128)
        im = spread[:, 128:].reshape(SLAB, 8, 128)
        cosine, sine = twist_cos[span][None], twist_sin[span][None]
        real.append(re * cosine - im * sine)
        imag.append(im * cosine + re * sine)
    stacked = jnp.concatenate(
        [jnp.concatenate([part[s] for part in real + imag], axis=0) for s in range(SLAB)], axis=1
    )
    first = slice(128 + 2 * OUTER, 128 + 3 * OUTER)
    final = dot((every[0, first, : 2 * OUTER], every[1, first, : 2 * OUTER]), halves(stacked))
    for s in range(SLAB):
        part = final[:, s * 128 : (s + 1) * 128]
        out[pl.ds(s, OUTER, stride=BACK), :] = known(info, SLOPE) - part
    lane = lax.broadcasted_iota(jnp.int32, (SLAB, TILE_COLS), 1)
    late = (known(info, PLACE) == 0.0) & (lane % SLAB < SHIFT)
    for core in range(2):
        rows = pl.ds(3 * EDGE + core, SLAB, stride=2)
        start = core * SLAB * BACK + SLAB
        out[pl.ds(start, SLAB, stride=BACK), :] = jnp.where(late, below[rows, :], mine[rows, :])


def place_kernel(data, fields, columns, phase, heat, gradient):
    lane = lax.broadcasted_iota(jnp.int32, (SLAB, TILE_COLS), 1)
    row = lax.broadcasted_iota(jnp.int32, (SLAB, TILE_COLS), 0)
    own = (lane % SLAB == row) & (lane < 4 * SLAB)
    lane = lax.broadcasted_iota(jnp.int32, (TILE_ROWS, TILE_COLS), 1)
    outer = (lane < SHIFT) | (lane >= TILE_COLS - SHIFT)
    for f, out in enumerate((phase, heat)):
        start = f * SLAB * BACK
        values = data[pl.ds(start + SLAB, SLAB, stride=BACK), :]
        spread = jnp.concatenate(
            [jnp.where(own, values[x : x + 1], 0.0) for x in range(SLAB)], axis=0
        )
        high, rest = halves(spread)
        low = (spread - high.astype(jnp.float32) - rest.astype(jnp.float32)).astype(jnp.bfloat16)
        parts = [
            lax.dot_general(
                part, columns[...], (((1,), (0,)), ((), ())), preferred_element_type=jnp.float32
            )
            for part in (high, rest, low)
        ]
        edge = roll(parts[0] + (parts[1] + parts[2]), -SHIFT, 0)
        out[...] = jnp.where(outer, edge, fields[f])
        for s in range(SLAB):
            gradient[pl.ds(f * TILE_ROWS + s, SLAB, stride=SLAB), :] = data[
                pl.ds(start + s, SLAB, stride=BACK), :
            ]


def wave_numbers(info):
    shape = (CHIPS, 128)
    lane = lax.broadcasted_iota(jnp.int32, shape, 1)
    row_freq = lax.broadcasted_iota(jnp.int32, shape, 0) + CHIPS * (lane // 8)
    row_wave = jnp.where(row_freq >= ROWS // 2, row_freq - ROWS, row_freq).astype(jnp.float32)
    col_wave = 8.0 * known(info, CHIP) + (lane % 8).astype(jnp.float32)
    wave = jnp.where(known(info, CORE) == 0.0, row_wave, col_wave)
    return row_freq, row_wave, col_wave, wave


def rows_forward_kernel(info, data, first, second, twist_cos, twist_sin, out):
    real = data[pl.ds(0, CHIPS, stride=2), :]
    imag = data[pl.ds(1, CHIPS, stride=2), :]
    spread = dot((first[0], first[1]), halves(jnp.concatenate([real, imag], axis=1)))
    re = spread[:CHIPS, :128] + spread[CHIPS:, 128:]
    im = spread[:CHIPS, 128:] - spread[CHIPS:, :128]
    cosine, sine = twist_cos[...], twist_sin[...]
    turned = jnp.concatenate([re * cosine + im * sine, im * cosine - re * sine], axis=1)
    final = dot(halves(turned), (second[0], second[1]))
    wave = wave_numbers(info)[3]
    out[:CHIPS] = wave * final[:, :128]
    out[CHIPS:] = wave * final[:, 128:]


def rows_backward_kernel(info, mine, other, first, second, twist_cos, twist_sin, out):
    row_freq, row_wave, col_wave, wave = wave_numbers(info)
    valid = (
        (row_freq != ROWS // 2)
        & (col_wave != COLS // 2)
        & ((row_freq != 0) | (col_wave != 0.0))
    )
    denom = reference_conduct * jnp.maximum(row_wave * row_wave + col_wave * col_wave, 1.0)
    weight = jnp.where(col_wave == 0.0, 1.0, 2.0) / (ROWS * COLS)
    coef = jnp.where(valid, weight * wave / denom, 0.0)
    along = mine[...] + other[...]
    green = jnp.concatenate([coef * along[:CHIPS], coef * along[CHIPS:]], axis=1)
    spread = dot(halves(green), (second[0], second[1]))
    re, im = spread[:, :128], spread[:, 128:]
    cosine, sine = twist_cos[...], twist_sin[...]
    turned = jnp.concatenate([re * cosine - im * sine, im * cosine + re * sine], axis=1)
    final = dot((first[0], first[1]), halves(turned))
    out[pl.ds(0, CHIPS, stride=2), :] = final[:CHIPS, :128] - final[CHIPS:, 128:]
    out[pl.ds(1, CHIPS, stride=2), :] = final[:CHIPS, 128:] + final[CHIPS:, :128]


def exchange(array, axes, tile):
    blocks = array.reshape((array.size // tile // 128, tile, 128))
    return lax.all_to_all(blocks, axes, split_axis=0, concat_axis=0, tiled=True)


def shift(block, axes, count, step):
    return lax.ppermute(block, axes, [(i, (i + step) % count) for i in range(count)])


def bottom_strip(voxel, wetted, heat):
    bottom = [array[:, TILE_ROWS - EDGE :] for array in (voxel, wetted, heat)]
    parts = bottom[0].astype(jnp.float32), bottom[1].astype(jnp.float32), -bottom[2]
    which = lax.broadcasted_iota(jnp.int32, (3, EDGE, TILE_COLS), 0)
    return jnp.where(which == 0, parts[0], jnp.where(which == 1, parts[1], parts[2]))


def body(voxel, wetted, heat, slope):
    gx_size, gy_size = ROWS // TILE_ROWS, COLS // TILE_COLS
    indices = (GX_AXES, GY_AXES, CHIP_AXES, "core", ("x", "y_lo"))
    place = jnp.stack([lax.axis_index(axes) for axes in indices])
    (shared, order, columns), (row_to, row_back) = column_tables(), row_tables()
    tile = (TILE_ROWS, TILE_COLS)
    above = shift(bottom_strip(voxel, wetted, heat), GX_AXES, gx_size, 1)
    porous = voxel[0].astype(jnp.float32)
    phase = porous * wetted[0].astype(jnp.float32)
    heat = heat[0]
    (info,) = call(prepare_kernel, [(8, 128)], place.astype(jnp.int32), slope, smem=(0, 1))
    polar, fields = call(
        polar_kernel, [(OUTER * BLOCK, 128), (2,) + tile], info, porous, phase, heat, above
    )
    slab = exchange(polar, GY_AXES, 4).reshape(-1, 128)
    spec, parcel = call(
        columns_forward_kernel, [(2 * CHIPS, 128), (3 * EDGE + OUTER, 128)],
        info, slab, porous, phase, heat, order, *shared,
    )
    spec = exchange(spec, CHIP_AXES, 2).reshape(-1, 128)
    (mine,) = call(rows_forward_kernel, [(2 * CHIPS, 128)], info, spec, *row_to)
    other = lax.ppermute(mine, "core", [(0, 1), (1, 0)])
    (green,) = call(rows_backward_kernel, [(2 * CHIPS, 128)], info, mine, other, *row_back)
    green, parcel = lax.optimization_barrier((green, parcel))
    below = shift(parcel, GX_AXES, gx_size, -1)
    green = exchange(green, CHIP_AXES, 2).reshape(-1, 128)
    (fields,) = call(tail_kernel, [(2,) + tile], info, porous, phase, heat, fields, below)
    green, below, fields = lax.optimization_barrier((green, below, fields))
    (answer,) = call(
        columns_backward_kernel, [(OUTER * BACK, 128)], info, green, parcel, below, *shared
    )
    answer = exchange(answer, ("core", "x", "y_lo"), 1).reshape(-1, 128)
    phase, heat, gradient = call(
        place_kernel, [tile, tile, (2 * TILE_ROWS, TILE_COLS)], answer, fields, columns
    )
    return (phase[None], heat[None], gradient.reshape((2, 1) + tile))


def solution(mesh):
    fine = Mesh(mesh.devices.reshape(tuple(SIZES.values())), tuple(SIZES))
    in_specs = (P(None, GX_AXES, GY_AXES),) * 3 + (P(),)
    out_specs = (P(None, GX_AXES, GY_AXES),) * 2 + (P(None, None, GX_AXES, GY_AXES),)
    return jax.shard_map(body, mesh=fine, in_specs=in_specs, out_specs=out_specs, check_vma=False)
```

```python
import functools
import math

import jax
import jax.numpy as jnp
import numpy as np
from jax import lax
from jax.experimental import pallas as pl
from jax.experimental.pallas import tpu as pltpu
from jax.sharding import Mesh
from jax.sharding import PartitionSpec as P

solid_conduct = 1.7
gas_conduct = 0.026
liquid_conduct = 0.6
reference_conduct = 0.863
step_grad = 0.1
step_well = 0.3
step_drive = 0.2
step_heat = 0.12
latent_heat = 0.5
gradient_gain = 0.5

TILE_ROWS = 256
TILE_COLS = 128
EDGE = 8
SHIFT = 2
TALL = TILE_ROWS + EDGE
WIDE = 384
OUTER = 32
SLAB = 16
SPAN = 20
HALF = 64
BLOCK = SLAB + 4
BACK = SLAB + 1
CHIPS = 256
COLS = 4096
ROWS = 4096
CORE_MAJOR = np.arange(OUTER).reshape(-1, 2).T.reshape(-1)
SIZES = {"z": 8, "y_hi": 2, "x": 4, "y_lo": 4, "core": 2}
GX_AXES, GY_AXES = ("z", "y_hi"), ("x", "y_lo", "core")
CHIP_AXES = ("y_lo", "x", "y_hi", "z")
CHIP_ORDER = np.arange(CHIPS).reshape(8, 2, 4, 4).transpose(3, 2, 1, 0).reshape(-1)
VMEM = pl.BlockSpec(memory_space=pltpu.VMEM)
SMEM = pl.BlockSpec(memory_space=pltpu.SMEM)


def halves(array):
    high = array.astype(jnp.bfloat16)
    return high, (array - high.astype(jnp.float32)).astype(jnp.bfloat16)


def dot(left, right, contract=((1,), (0,))):
    def product(x, y):
        return lax.dot_general(x, y, (contract, ((), ())), preferred_element_type=jnp.float32)

    (left_high, left_low), (right_high, right_low) = left, right
    return product(left_high, right_high) + (
        product(left_high, right_low) + product(left_low, right_high)
    )


def call(kernel, outs, *args, smem=(), scratch=(), aliases=()):
    shapes = [jax.ShapeDtypeStruct(shape, jnp.float32) for shape in outs]
    spaces = [SMEM if i in smem else VMEM for i in range(len(args))]
    return pl.pallas_call(
        kernel,
        out_shape=shapes,
        in_specs=spaces,
        out_specs=[VMEM] * len(outs),
        scratch_shapes=list(scratch),
        input_output_aliases=dict(aliases),
        compiler_params=pltpu.CompilerParams(vmem_limit_bytes=32 * 1024 * 1024),
    )(*args)


def angles(left, right, length):
    product = np.outer(np.arange(left), np.asarray(right)) % length
    return 2.0 * math.pi / length * product


def table(array):
    return jnp.asarray(np.asarray(array, dtype=np.float32))


def split_table(array):
    array = np.asarray(array, dtype=np.float32)
    high = array.astype(jnp.bfloat16)
    low = (array - high.astype(np.float32)).astype(jnp.bfloat16)
    return jnp.asarray(np.stack([high, low]))


def column_tables():
    first = angles(OUTER, range(OUTER), OUTER)
    cosine, sine = np.cos(first), np.sin(first)
    second = angles(64, range(128), 128)
    twist = angles(OUTER, range(128), COLS)
    mix = np.block([[np.cos(second), np.sin(second)], [-np.sin(second), np.cos(second)]])
    slot, s = np.divmod(np.arange(4 * SLAB), SLAB)
    order = np.zeros((128, 128))
    order[np.arange(4 * SLAB), EDGE * s + slot] = 1.0
    every = np.zeros((128 + 2 * OUTER + OUTER, 256))
    every[:128] = mix
    every[128 : 128 + 2 * OUTER, :OUTER] = np.concatenate([cosine, -sine], axis=0)
    every[128 + 2 * OUTER :, : 2 * OUTER] = np.concatenate([cosine, -sine], axis=1)[CORE_MAJOR]
    shared = [split_table(every), table(np.cos(twist)), table(np.sin(twist))]
    columns = np.zeros((128, 128))
    columns[np.arange(4 * SLAB), (slot - SHIFT) % TILE_COLS] = 1.0
    return shared, split_table(order), jnp.asarray(columns.astype(jnp.bfloat16))


def row_tables():
    first = angles(CHIPS, range(CHIPS), CHIPS)
    cosine, sine = np.cos(first)[:, CHIP_ORDER], np.sin(first)[:, CHIP_ORDER]
    starts = (np.concatenate([cosine, sine], axis=0), np.concatenate([cosine.T, sine.T], axis=0))
    tables = []
    for shift, sign, start in ((SHIFT, -1.0, starts[0]), (0, 1.0, starts[1])):
        inner = np.arange(SLAB) - shift
        second = angles(SLAB, inner, SLAB)
        twist = np.repeat(angles(CHIPS, inner, ROWS), 8, axis=1)
        cosine, sine = np.kron(np.cos(second), np.eye(8)), sign * np.kron(np.sin(second), np.eye(8))
        if shift:
            cosine, sine = cosine.T, sine.T
        mix = np.block([[cosine, sine], [-sine, cosine]])
        rest = [split_table(mix), table(np.cos(twist)), table(np.sin(twist))]
        tables.append([split_table(start)] + rest)
    return tables


GX, GY, CHIP, CORE, PLACE, SLOPE_X, SLOPE_Y, SLOPE = range(8)


def prepare_kernel(place, slope, info):
    values = [place[i].astype(jnp.float32) for i in range(5)] + [slope[0, 0], slope[0, 1]]
    values.append(jnp.where(place[3] == 0, slope[0, 0], slope[0, 1]))
    row = lax.broadcasted_iota(jnp.int32, info.shape, 0)
    filled = jnp.zeros(info.shape, jnp.float32)
    for i, value in enumerate(values):
        filled = jnp.where(row == i, value, filled)
    info[...] = filled


def known(info, i):
    return info[i : i + 1, :]


def with_above(above, porous, phase, heat):
    tops = (above[0], above[0] * above[1], -above[2])
    return [
        jnp.concatenate([top, field[...]], axis=0) for top, field in zip(tops, (porous, phase, heat))
    ]


def progress(phase, heat, porous, phase_lap, heat_lap):
    well = 2.0 * phase * (1.0 - phase) * (1.0 - 2.0 * phase)
    growth = 30.0 * phase * phase * (1.0 - phase) * (1.0 - phase)
    new_phase = porous * (
        phase + step_grad * phase_lap - step_well * well + step_drive * heat * growth
    )
    new_heat = heat + step_heat * heat_lap - latent_heat * (new_phase - phase)
    return new_phase, new_heat


def stencil(porous, phase, heat, neighbours):
    def laplace(around, field):
        return around[0] + around[1] + around[2] + around[3] - 6.0 * field

    phase_lap, heat_lap = laplace(neighbours(phase), phase), laplace(neighbours(heat), heat)
    phase, heat = progress(phase, heat, porous, phase_lap, heat_lap)
    around = neighbours(heat)
    phase_lap, heat_lap = laplace(neighbours(phase), phase), laplace(around, heat)
    phase, heat = progress(phase, heat, porous, phase_lap, heat_lap)
    return phase, heat, around[0] - around[1], around[2] - around[3]


def roll(field, step, axis):
    return pltpu.roll(field, step % field.shape[axis], axis)


def walled(wall, field):
    return field if wall is None else jnp.where(wall, 0.0, field)


def ring_neighbours(walls):
    def neighbours(field):
        moves = ((-1, 0), (1, 0), (-1, 1), (1, 1))
        return [walled(wall, roll(field, *move)) for move, wall in zip(moves, walls)]

    return neighbours


def conductivity_contrast(porous, phase):
    conduct = (
        porous * (gas_conduct + (liquid_conduct - gas_conduct) * phase)
        + (1.0 - porous) * solid_conduct
    )
    return conduct - reference_conduct


def shifted_rows(field):
    return roll(field, SHIFT - EDGE, 0)[: field.shape[0] - EDGE]


def row_walls(first, row):
    return first & (row == EDGE - 1), first & (row == EDGE)


def polar_blocks(info, talls, slabs, rows, out, fields):
    row = lax.broadcasted_iota(jnp.int32, talls[0].shape, 0)
    walls = row_walls(known(info, GX) == 0.0, row) + (None, None)
    phase_two, heat_two, along_rows, along_columns = stencil(*talls, ring_neighbours(walls))
    fields[0, :rows] = shifted_rows(phase_two)[:rows]
    fields[1, :rows] = shifted_rows(heat_two)[:rows]
    contrast = conductivity_contrast(talls[0], phase_two)
    polars = (
        shifted_rows(contrast * (known(info, SLOPE_X) + gradient_gain * along_rows)),
        shifted_rows(contrast * (known(info, SLOPE_Y) + gradient_gain * along_columns)),
    )
    tall = talls[0].shape[0]
    wide = WIDE if tall == TALL else TILE_COLS
    spare = jnp.zeros((wide - tall, TILE_COLS), jnp.float32)
    sublane = lax.broadcasted_iota(jnp.int32, (EDGE, wide), 0)
    lane = lax.broadcasted_iota(jnp.int32, (EDGE, TILE_COLS), 1)
    low = lax.broadcasted_iota(jnp.int32, (EDGE, TILE_COLS), 0) < 4
    edges = []
    for tall in talls:
        flipped = jnp.concatenate([tall, spare], axis=0).T
        edges.append(jnp.where(sublane < 4, flipped[:EDGE], flipped[TILE_COLS - EDGE :]))
    for x in slabs:
        first = EDGE - 2 * SHIFT + SLAB * x
        windows = [
            roll(edge, f * SPAN - first, 1)[:, :TILE_COLS] for f, edge in enumerate(edges)
        ]
        packed = jnp.where(
            lane < SPAN, windows[0], jnp.where(lane < 2 * SPAN, windows[1], windows[2])
        )
        swapped = roll(packed, 4, 0)
        lower, upper = jnp.where(low, packed, swapped), jnp.where(low, swapped, packed)
        both = jnp.where(lane < HALF, lower, roll(upper, HALF, 1))
        rows = slice(x * SLAB, (x + 1) * SLAB)
        start = 2 * x * BLOCK
        out[start : start + SLAB, :] = polars[0][rows]
        rest = roll(jnp.concatenate([both, polars[1][rows]], axis=0), -4, 0)
        out[start + SLAB : start + 2 * BLOCK, :] = rest


def polar_kernel(info, porous, phase, heat, out, fields):
    nothing = jnp.zeros((3, EDGE, TILE_COLS), jnp.float32)
    talls = with_above(nothing, porous, phase, heat)
    polar_blocks(info, talls, range(1, TILE_ROWS // SLAB), TILE_ROWS, out, fields)


def first_slab_kernel(info, porous, phase, heat, above, blocks, rows, out, fields):
    del blocks, rows
    talls = [tall[: 4 * EDGE] for tall in with_above(above, porous, phase, heat)]
    polar_blocks(info, talls, range(1), EDGE, out, fields)


def tail_kernel(info, porous, phase, heat, fields, parcel, out):
    ends = [
        jnp.concatenate([field[TILE_ROWS - 2 * EDGE :, :], parcel[f * EDGE : (f + 1) * EDGE, :]])
        for f, field in enumerate((porous, phase, heat))
    ]
    row = lax.broadcasted_iota(jnp.int32, ends[0].shape, 0)
    last = known(info, GX) == ROWS // TILE_ROWS - 1
    walls = (last & (row == 2 * EDGE - 1), last & (row == 2 * EDGE), None, None)
    late = lax.broadcasted_iota(jnp.int32, (EDGE, TILE_COLS), 0) >= EDGE - SHIFT
    for f, end in enumerate(stencil(*ends, ring_neighbours(walls))[:2]):
        whole = roll(fields[f], -SHIFT, 0)
        out[f, : TILE_ROWS - EDGE, :] = whole[: TILE_ROWS - EDGE]
        out[f, TILE_ROWS - EDGE :, :] = jnp.where(
            late, end[EDGE : 2 * EDGE], whole[TILE_ROWS - EDGE :]
        )


def edge_polar(info, data):
    raw = jnp.concatenate([data[pl.ds(SLAB + c, OUTER, stride=BLOCK), :] for c in range(4)], axis=0)
    fields = [raw] + [roll(raw, -f * SPAN, 1) for f in (1, 2)]
    lane = lax.broadcasted_iota(jnp.int32, raw.shape, 1)
    row = lane % HALF
    first = known(info, CHIP) == 0.0
    down_wall, up_wall = first & (row == 2 * SHIFT - 1), first & (row == 2 * SHIFT)
    tile = lax.broadcasted_iota(jnp.int32, (OUTER, TILE_COLS), 0)

    def neighbours(field):
        after = walled(tile == OUTER - 1, roll(roll(field[:OUTER], -1, 0), HALF, 1))
        before = walled(tile == 0, roll(roll(field[3 * OUTER :], 1, 0), HALF, 1))
        return (
            walled(down_wall, roll(field, -1, 1)),
            walled(up_wall, roll(field, 1, 1)),
            jnp.concatenate([field[OUTER:], after], axis=0),
            jnp.concatenate([before, field[: 3 * OUTER]], axis=0),
        )

    phase, heat, along_rows, along_columns = stencil(*fields, neighbours)
    first = known(info, CORE) == 0.0
    along = jnp.where(first, along_rows, along_columns)
    value = jnp.where(first, phase, heat)
    polar = conductivity_contrast(raw, phase) * (known(info, SLOPE) + gradient_gain * along)
    return [[array[c * OUTER : (c + 1) * OUTER] for c in range(4)] for array in (polar, value)]


def pack(columns):
    lane = lax.broadcasted_iota(jnp.int32, (OUTER, TILE_COLS), 1)
    packed = jnp.zeros((OUTER, TILE_COLS), jnp.float32)
    for slot, column in enumerate((2, 3, 0, 1)):
        start = SHIFT + (HALF if column >= 2 else 0)
        moved = roll(columns[column], SLAB * slot - start, 1)
        packed = jnp.where(lane // SLAB == slot, moved, packed)
    return packed


def columns_forward_kernel(
    info, data, porous, phase, heat, order, every, twist_cos, twist_sin, out, parcel
):
    polar, value = edge_polar(info, data)
    for f, field in enumerate((porous, phase, heat)):
        parcel[f * EDGE : (f + 1) * EDGE, :] = field[:EDGE, :]
    parcel[3 * EDGE :, :] = pack(value)
    packed = dot(halves(pack(polar)), (order[0], order[1]))
    lane = lax.broadcasted_iota(jnp.int32, (OUTER, TILE_COLS), 1)
    outer = (lane < SHIFT) | (lane >= TILE_COLS - SHIFT)
    parts = []
    for s in range(SLAB):
        around = roll(packed, -EDGE * s - SHIFT, 1)
        parts.append(jnp.where(outer, around, data[pl.ds(s, OUTER, stride=BLOCK), :]))
    rows = jnp.concatenate(parts, axis=1)
    first = slice(128, 128 + 2 * OUTER)
    spread = dot((every[0, first, :OUTER], every[1, first, :OUTER]), halves(rows))
    cosine, sine = twist_cos[...], twist_sin[...]
    real, imag = [], []
    for s in range(SLAB):
        part = slice(s * 128, (s + 1) * 128)
        re, im = spread[:OUTER, part], spread[OUTER:, part]
        real.append(re * cosine + im * sine)
        imag.append(im * cosine - re * sine)
    for g in range(4):
        span = slice(g * 8, (g + 1) * 8)
        re = jnp.concatenate([part[span] for part in real], axis=0)
        im = jnp.concatenate([part[span] for part in imag], axis=0)
        both = jnp.concatenate([re, im], axis=1)
        final = dot((every[0, :128], every[1, :128]), halves(both), ((1,), (1,)))
        out[pl.ds(2 * g, 64, stride=8), :] = final[:64]
        out[pl.ds(2 * g + 1, 64, stride=8), :] = final[64:]


def columns_backward_kernel(info, data, mine, below, every, twist_cos, twist_sin, out):
    real, imag = [], []
    for g in range(4):
        span = slice(g * 8, (g + 1) * 8)
        both = jnp.concatenate(
            [data[pl.ds(2 * g, 64, stride=8), :], data[pl.ds(2 * g + 1, 64, stride=8), :]], axis=0
        )
        spread = dot(halves(both.T), (every[0, :128], every[1, :128]))
        re = spread[:, :128].reshape(SLAB, 8, 128)
        im = spread[:, 128:].reshape(SLAB, 8, 128)
        cosine, sine = twist_cos[span][None], twist_sin[span][None]
        real.append(re * cosine - im * sine)
        imag.append(im * cosine + re * sine)
    stacked = jnp.concatenate(
        [jnp.concatenate([part[s] for part in real + imag], axis=0) for s in range(SLAB)], axis=1
    )
    first = slice(128 + 2 * OUTER, 128 + 3 * OUTER)
    final = dot((every[0, first, : 2 * OUTER], every[1, first, : 2 * OUTER]), halves(stacked))
    for s in range(SLAB):
        part = final[:, s * 128 : (s + 1) * 128]
        out[pl.ds(s, OUTER, stride=BACK), :] = known(info, SLOPE) - part
    lane = lax.broadcasted_iota(jnp.int32, (SLAB, TILE_COLS), 1)
    late = (known(info, PLACE) == 0.0) & (lane % SLAB < SHIFT)
    for core in range(2):
        rows = pl.ds(3 * EDGE + core, SLAB, stride=2)
        start = core * SLAB * BACK + SLAB
        out[pl.ds(start, SLAB, stride=BACK), :] = jnp.where(late, below[rows, :], mine[rows, :])


def place_kernel(data, fields, columns, phase, heat, gradient):
    lane = lax.broadcasted_iota(jnp.int32, (SLAB, TILE_COLS), 1)
    row = lax.broadcasted_iota(jnp.int32, (SLAB, TILE_COLS), 0)
    own = (lane % SLAB == row) & (lane < 4 * SLAB)
    lane = lax.broadcasted_iota(jnp.int32, (TILE_ROWS, TILE_COLS), 1)
    outer = (lane < SHIFT) | (lane >= TILE_COLS - SHIFT)
    for f, out in enumerate((phase, heat)):
        start = f * SLAB * BACK
        values = data[pl.ds(start + SLAB, SLAB, stride=BACK), :]
        spread = jnp.concatenate(
            [jnp.where(own, values[x : x + 1], 0.0) for x in range(SLAB)], axis=0
        )
        high, rest = halves(spread)
        low = (spread - high.astype(jnp.float32) - rest.astype(jnp.float32)).astype(jnp.bfloat16)
        parts = [
            lax.dot_general(
                part, columns[...], (((1,), (0,)), ((), ())), preferred_element_type=jnp.float32
            )
            for part in (high, rest, low)
        ]
        edge = roll(parts[0] + (parts[1] + parts[2]), -SHIFT, 0)
        out[...] = jnp.where(outer, edge, fields[f])
        for s in range(SLAB):
            gradient[pl.ds(f * TILE_ROWS + s, SLAB, stride=SLAB), :] = data[
                pl.ds(start + s, SLAB, stride=BACK), :
            ]


def wave_numbers(info):
    shape = (CHIPS, 128)
    lane = lax.broadcasted_iota(jnp.int32, shape, 1)
    row_freq = lax.broadcasted_iota(jnp.int32, shape, 0) + CHIPS * (lane // 8)
    row_wave = jnp.where(row_freq >= ROWS // 2, row_freq - ROWS, row_freq).astype(jnp.float32)
    col_wave = 8.0 * known(info, CHIP) + (lane % 8).astype(jnp.float32)
    wave = jnp.where(known(info, CORE) == 0.0, row_wave, col_wave)
    return row_freq, row_wave, col_wave, wave


def rows_forward_kernel(info, data, first, second, twist_cos, twist_sin, out):
    real = data[pl.ds(0, CHIPS, stride=2), :]
    imag = data[pl.ds(1, CHIPS, stride=2), :]
    spread = dot((first[0], first[1]), halves(jnp.concatenate([real, imag], axis=1)))
    re = spread[:CHIPS, :128] + spread[CHIPS:, 128:]
    im = spread[:CHIPS, 128:] - spread[CHIPS:, :128]
    cosine, sine = twist_cos[...], twist_sin[...]
    turned = jnp.concatenate([re * cosine + im * sine, im * cosine - re * sine], axis=1)
    final = dot(halves(turned), (second[0], second[1]))
    wave = wave_numbers(info)[3]
    out[:CHIPS] = wave * final[:, :128]
    out[CHIPS:] = wave * final[:, 128:]


def rows_backward_kernel(info, mine, other, first, second, twist_cos, twist_sin, out):
    row_freq, row_wave, col_wave, wave = wave_numbers(info)
    valid = (
        (row_freq != ROWS // 2)
        & (col_wave != COLS // 2)
        & ((row_freq != 0) | (col_wave != 0.0))
    )
    denom = reference_conduct * jnp.maximum(row_wave * row_wave + col_wave * col_wave, 1.0)
    weight = jnp.where(col_wave == 0.0, 1.0, 2.0) / (ROWS * COLS)
    coef = jnp.where(valid, weight * wave / denom, 0.0)
    along = mine[...] + other[...]
    green = jnp.concatenate([coef * along[:CHIPS], coef * along[CHIPS:]], axis=1)
    spread = dot(halves(green), (second[0], second[1]))
    re, im = spread[:, :128], spread[:, 128:]
    cosine, sine = twist_cos[...], twist_sin[...]
    turned = jnp.concatenate([re * cosine - im * sine, im * cosine + re * sine], axis=1)
    final = dot((first[0], first[1]), halves(turned))
    out[pl.ds(0, CHIPS, stride=2), :] = final[:CHIPS, :128] - final[CHIPS:, 128:]
    out[pl.ds(1, CHIPS, stride=2), :] = final[:CHIPS, 128:] + final[CHIPS:, :128]


def exchange(array, axes, tile):
    blocks = array.reshape((array.size // tile // 128, tile, 128))
    return lax.all_to_all(blocks, axes, split_axis=0, concat_axis=0, tiled=True)


def shift(block, axes, count, step):
    return lax.ppermute(block, axes, [(i, (i + step) % count) for i in range(count)])


def bottom_strip(voxel, wetted, heat):
    bottom = [array[:, TILE_ROWS - EDGE :] for array in (voxel, wetted, heat)]
    parts = bottom[0].astype(jnp.float32), bottom[1].astype(jnp.float32), -bottom[2]
    which = lax.broadcasted_iota(jnp.int32, (3, EDGE, TILE_COLS), 0)
    return jnp.where(which == 0, parts[0], jnp.where(which == 1, parts[1], parts[2]))


def body(voxel, wetted, heat, slope):
    gx_size, gy_size = ROWS // TILE_ROWS, COLS // TILE_COLS
    indices = (GX_AXES, GY_AXES, CHIP_AXES, "core", ("x", "y_lo"))
    place = jnp.stack([lax.axis_index(axes) for axes in indices])
    (shared, order, columns), (row_to, row_back) = column_tables(), row_tables()
    tile = (TILE_ROWS, TILE_COLS)
    above = shift(bottom_strip(voxel, wetted, heat), GX_AXES, gx_size, 1)
    porous = voxel[0].astype(jnp.float32)
    phase = porous * wetted[0].astype(jnp.float32)
    heat = heat[0]
    (info,) = call(prepare_kernel, [(8, 128)], place.astype(jnp.int32), slope, smem=(0, 1))
    shapes = [(OUTER * BLOCK, 128), (2,) + tile]
    polar, fields = call(polar_kernel, shapes, info, porous, phase, heat)
    polar, fields = call(
        first_slab_kernel, shapes, info, porous, phase, heat, above, polar, fields,
        aliases=((5, 0), (6, 1)),
    )
    slab = exchange(polar, GY_AXES, 4).reshape(-1, 128)
    spec, parcel = call(
        columns_forward_kernel, [(2 * CHIPS, 128), (3 * EDGE + OUTER, 128)],
        info, slab, porous, phase, heat, order, *shared,
    )
    spec = exchange(spec, CHIP_AXES, 2).reshape(-1, 128)
    (mine,) = call(rows_forward_kernel, [(2 * CHIPS, 128)], info, spec, *row_to)
    other = lax.ppermute(mine, "core", [(0, 1), (1, 0)])
    (green,) = call(rows_backward_kernel, [(2 * CHIPS, 128)], info, mine, other, *row_back)
    green, parcel = lax.optimization_barrier((green, parcel))
    below = shift(parcel, GX_AXES, gx_size, -1)
    green = exchange(green, CHIP_AXES, 2).reshape(-1, 128)
    (fields,) = call(tail_kernel, [(2,) + tile], info, porous, phase, heat, fields, below)
    green, below, fields = lax.optimization_barrier((green, below, fields))
    (answer,) = call(
        columns_backward_kernel, [(OUTER * BACK, 128)], info, green, parcel, below, *shared
    )
    answer = exchange(answer, ("core", "x", "y_lo"), 1).reshape(-1, 128)
    phase, heat, gradient = call(
        place_kernel, [tile, tile, (2 * TILE_ROWS, TILE_COLS)], answer, fields, columns
    )
    return (phase[None], heat[None], gradient.reshape((2, 1) + tile))


def solution(mesh):
    fine = Mesh(mesh.devices.reshape(tuple(SIZES.values())), tuple(SIZES))
    in_specs = (P(None, GX_AXES, GY_AXES),) * 3 + (P(),)
    out_specs = (P(None, GX_AXES, GY_AXES),) * 2 + (P(None, None, GX_AXES, GY_AXES),)
    return jax.shard_map(body, mesh=fine, in_specs=in_specs, out_specs=out_specs, check_vma=False)
```

```python
import functools
import math

import jax
import jax.numpy as jnp
import numpy as np
from jax import lax
from jax.experimental import pallas as pl
from jax.experimental.pallas import tpu as pltpu
from jax.sharding import Mesh
from jax.sharding import PartitionSpec as P

solid_conduct = 1.7
gas_conduct = 0.026
liquid_conduct = 0.6
reference_conduct = 0.863
step_grad = 0.1
step_well = 0.3
step_drive = 0.2
step_heat = 0.12
latent_heat = 0.5
gradient_gain = 0.5

TILE_ROWS = 256
TILE_COLS = 128
EDGE = 8
SHIFT = 2
TALL = TILE_ROWS + EDGE
WIDE = 384
OUTER = 32
SLAB = 16
SPAN = 20
HALF = 64
BLOCK = SLAB + 4
BACK = SLAB + 1
CHIPS = 256
COLS = 4096
ROWS = 4096
CORE_MAJOR = np.arange(OUTER).reshape(-1, 2).T.reshape(-1)
SIZES = {"z": 8, "y_hi": 2, "x": 4, "y_lo": 4, "core": 2}
GX_AXES, GY_AXES = ("z", "y_hi"), ("x", "y_lo", "core")
CHIP_AXES = ("y_lo", "x", "y_hi", "z")
CHIP_ORDER = np.arange(CHIPS).reshape(8, 2, 4, 4).transpose(3, 2, 1, 0).reshape(-1)
VMEM = pl.BlockSpec(memory_space=pltpu.VMEM)
SMEM = pl.BlockSpec(memory_space=pltpu.SMEM)


def halves(array):
    high = array.astype(jnp.bfloat16)
    return high, (array - high.astype(jnp.float32)).astype(jnp.bfloat16)


def dot(left, right, contract=((1,), (0,))):
    def product(x, y):
        return lax.dot_general(x, y, (contract, ((), ())), preferred_element_type=jnp.float32)

    (left_high, left_low), (right_high, right_low) = left, right
    return product(left_high, right_high) + (
        product(left_high, right_low) + product(left_low, right_high)
    )


def call(kernel, outs, *args, smem=(), scratch=()):
    shapes = [jax.ShapeDtypeStruct(shape, jnp.float32) for shape in outs]
    spaces = [SMEM if i in smem else VMEM for i in range(len(args))]
    return pl.pallas_call(
        kernel,
        out_shape=shapes,
        in_specs=spaces,
        out_specs=[VMEM] * len(outs),
        scratch_shapes=list(scratch),
        compiler_params=pltpu.CompilerParams(vmem_limit_bytes=32 * 1024 * 1024),
    )(*args)


def angles(left, right, length):
    product = np.outer(np.arange(left), np.asarray(right)) % length
    return 2.0 * math.pi / length * product


def table(array):
    return jnp.asarray(np.asarray(array, dtype=np.float32))


def split_table(array):
    array = np.asarray(array, dtype=np.float32)
    high = array.astype(jnp.bfloat16)
    low = (array - high.astype(np.float32)).astype(jnp.bfloat16)
    return jnp.asarray(np.stack([high, low]))


def column_tables():
    first = angles(OUTER, range(OUTER), OUTER)
    cosine, sine = np.cos(first), np.sin(first)
    second = angles(64, range(128), 128)
    twist = angles(OUTER, range(128), COLS)
    mix = np.block([[np.cos(second), np.sin(second)], [-np.sin(second), np.cos(second)]])
    slot, s = np.divmod(np.arange(4 * SLAB), SLAB)
    order = np.zeros((128, 128))
    order[np.arange(4 * SLAB), EDGE * s + slot] = 1.0
    every = np.zeros((128 + 2 * OUTER + OUTER, 256))
    every[:128] = mix
    every[128 : 128 + 2 * OUTER, :OUTER] = np.concatenate([cosine, -sine], axis=0)
    every[128 + 2 * OUTER :, : 2 * OUTER] = np.concatenate([cosine, -sine], axis=1)[CORE_MAJOR]
    shared = [split_table(every), table(np.cos(twist)), table(np.sin(twist))]
    columns = np.zeros((128, 128))
    columns[np.arange(4 * SLAB), (slot - SHIFT) % TILE_COLS] = 1.0
    return shared, split_table(order), jnp.asarray(columns.astype(jnp.bfloat16))


def row_tables():
    first = angles(CHIPS, range(CHIPS), CHIPS)
    cosine, sine = np.cos(first)[:, CHIP_ORDER], np.sin(first)[:, CHIP_ORDER]
    starts = (np.concatenate([cosine, sine], axis=0), np.concatenate([cosine.T, sine.T], axis=0))
    tables = []
    for shift, sign, start in ((SHIFT, -1.0, starts[0]), (0, 1.0, starts[1])):
        inner = np.arange(SLAB) - shift
        second = angles(SLAB, inner, SLAB)
        twist = np.repeat(angles(CHIPS, inner, ROWS), 8, axis=1)
        cosine, sine = np.kron(np.cos(second), np.eye(8)), sign * np.kron(np.sin(second), np.eye(8))
        if shift:
            cosine, sine = cosine.T, sine.T
        mix = np.block([[cosine, sine], [-sine, cosine]])
        rest = [split_table(mix), table(np.cos(twist)), table(np.sin(twist))]
        tables.append([split_table(start)] + rest)
    return tables


GX, GY, CHIP, CORE, PLACE, SLOPE_X, SLOPE_Y, SLOPE = range(8)


def prepare_kernel(place, slope, info):
    values = [place[i].astype(jnp.float32) for i in range(5)] + [slope[0, 0], slope[0, 1]]
    values.append(jnp.where(place[3] == 0, slope[0, 0], slope[0, 1]))
    row = lax.broadcasted_iota(jnp.int32, info.shape, 0)
    filled = jnp.zeros(info.shape, jnp.float32)
    for i, value in enumerate(values):
        filled = jnp.where(row == i, value, filled)
    info[...] = filled


def known(info, i):
    return info[i : i + 1, :]


def with_above(above, porous, phase, heat):
    tops = (above[0], above[0] * above[1], -above[2])
    return [
        jnp.concatenate([top, field[...]], axis=0) for top, field in zip(tops, (porous, phase, heat))
    ]


def progress(phase, heat, porous, phase_lap, heat_lap):
    well = 2.0 * phase * (1.0 - phase) * (1.0 - 2.0 * phase)
    growth = 30.0 * phase * phase * (1.0 - phase) * (1.0 - phase)
    new_phase = porous * (
        phase + step_grad * phase_lap - step_well * well + step_drive * heat * growth
    )
    new_heat = heat + step_heat * heat_lap - latent_heat * (new_phase - phase)
    return new_phase, new_heat


def stencil(porous, phase, heat, neighbours):
    def laplace(around, field):
        return around[0] + around[1] + around[2] + around[3] - 6.0 * field

    phase_lap, heat_lap = laplace(neighbours(phase), phase), laplace(neighbours(heat), heat)
    phase, heat = progress(phase, heat, porous, phase_lap, heat_lap)
    around = neighbours(heat)
    phase_lap, heat_lap = laplace(neighbours(phase), phase), laplace(around, heat)
    phase, heat = progress(phase, heat, porous, phase_lap, heat_lap)
    return phase, heat, around[0] - around[1], around[2] - around[3]


def roll(field, step, axis):
    return pltpu.roll(field, step % field.shape[axis], axis)


def walled(wall, field):
    return field if wall is None else jnp.where(wall, 0.0, field)


def ring_neighbours(walls):
    def neighbours(field):
        moves = ((-1, 0), (1, 0), (-1, 1), (1, 1))
        return [walled(wall, roll(field, *move)) for move, wall in zip(moves, walls)]

    return neighbours


def conductivity_contrast(porous, phase):
    conduct = (
        porous * (gas_conduct + (liquid_conduct - gas_conduct) * phase)
        + (1.0 - porous) * solid_conduct
    )
    return conduct - reference_conduct


def shifted_rows(field):
    return roll(field, SHIFT - EDGE, 0)[: field.shape[0] - EDGE]


def row_walls(first, row):
    return first & (row == EDGE - 1), first & (row == EDGE)


def polar_blocks(info, talls, slabs, rows, out, fields):
    row = lax.broadcasted_iota(jnp.int32, talls[0].shape, 0)
    walls = row_walls(known(info, GX) == 0.0, row) + (None, None)
    phase_two, heat_two, along_rows, along_columns = stencil(*talls, ring_neighbours(walls))
    fields[0, :rows] = shifted_rows(phase_two)[:rows]
    fields[1, :rows] = shifted_rows(heat_two)[:rows]
    contrast = conductivity_contrast(talls[0], phase_two)
    polars = (
        shifted_rows(contrast * (known(info, SLOPE_X) + gradient_gain * along_rows)),
        shifted_rows(contrast * (known(info, SLOPE_Y) + gradient_gain * along_columns)),
    )
    tall = talls[0].shape[0]
    wide = WIDE if tall == TALL else TILE_COLS
    spare = jnp.zeros((wide - tall, TILE_COLS), jnp.float32)
    sublane = lax.broadcasted_iota(jnp.int32, (EDGE, wide), 0)
    lane = lax.broadcasted_iota(jnp.int32, (EDGE, TILE_COLS), 1)
    low = lax.broadcasted_iota(jnp.int32, (EDGE, TILE_COLS), 0) < 4
    edges = []
    for tall in talls:
        flipped = jnp.concatenate([tall, spare], axis=0).T
        edges.append(jnp.where(sublane < 4, flipped[:EDGE], flipped[TILE_COLS - EDGE :]))
    for x in slabs:
        first = EDGE - 2 * SHIFT + SLAB * x
        windows = [
            roll(edge, f * SPAN - first, 1)[:, :TILE_COLS] for f, edge in enumerate(edges)
        ]
        packed = jnp.where(
            lane < SPAN, windows[0], jnp.where(lane < 2 * SPAN, windows[1], windows[2])
        )
        swapped = roll(packed, 4, 0)
        lower, upper = jnp.where(low, packed, swapped), jnp.where(low, swapped, packed)
        both = jnp.where(lane < HALF, lower, roll(upper, HALF, 1))
        rows = slice(x * SLAB, (x + 1) * SLAB)
        start = 2 * x * BLOCK
        out[start : start + SLAB, :] = polars[0][rows]
        rest = roll(jnp.concatenate([both, polars[1][rows]], axis=0), -4, 0)
        out[start + SLAB : start + 2 * BLOCK, :] = rest


def polar_kernel(info, porous, phase, heat, out, fields):
    nothing = jnp.zeros((3, EDGE, TILE_COLS), jnp.float32)
    talls = with_above(nothing, porous, phase, heat)
    polar_blocks(info, talls, range(1, TILE_ROWS // SLAB), TILE_ROWS, out, fields)


def first_slab_kernel(info, porous, phase, heat, above, blocks, rows, out, fields):
    done = 2 * BLOCK
    out[done:, :] = blocks[done:, :]
    fields[:, EDGE:] = rows[:, EDGE:]
    talls = [tall[: 4 * EDGE] for tall in with_above(above, porous, phase, heat)]
    polar_blocks(info, talls, range(1), EDGE, out, fields)


def tail_kernel(info, porous, phase, heat, fields, parcel, out):
    ends = [
        jnp.concatenate([field[TILE_ROWS - 2 * EDGE :, :], parcel[f * EDGE : (f + 1) * EDGE, :]])
        for f, field in enumerate((porous, phase, heat))
    ]
    row = lax.broadcasted_iota(jnp.int32, ends[0].shape, 0)
    last = known(info, GX) == ROWS // TILE_ROWS - 1
    walls = (last & (row == 2 * EDGE - 1), last & (row == 2 * EDGE), None, None)
    late = lax.broadcasted_iota(jnp.int32, (EDGE, TILE_COLS), 0) >= EDGE - SHIFT
    for f, end in enumerate(stencil(*ends, ring_neighbours(walls))[:2]):
        whole = roll(fields[f], -SHIFT, 0)
        out[f, : TILE_ROWS - EDGE, :] = whole[: TILE_ROWS - EDGE]
        out[f, TILE_ROWS - EDGE :, :] = jnp.where(
            late, end[EDGE : 2 * EDGE], whole[TILE_ROWS - EDGE :]
        )


def edge_polar(info, data):
    raw = jnp.concatenate([data[pl.ds(SLAB + c, OUTER, stride=BLOCK), :] for c in range(4)], axis=0)
    fields = [raw] + [roll(raw, -f * SPAN, 1) for f in (1, 2)]
    lane = lax.broadcasted_iota(jnp.int32, raw.shape, 1)
    row = lane % HALF
    first = known(info, CHIP) == 0.0
    down_wall, up_wall = first & (row == 2 * SHIFT - 1), first & (row == 2 * SHIFT)
    tile = lax.broadcasted_iota(jnp.int32, (OUTER, TILE_COLS), 0)

    def neighbours(field):
        after = walled(tile == OUTER - 1, roll(roll(field[:OUTER], -1, 0), HALF, 1))
        before = walled(tile == 0, roll(roll(field[3 * OUTER :], 1, 0), HALF, 1))
        return (
            walled(down_wall, roll(field, -1, 1)),
            walled(up_wall, roll(field, 1, 1)),
            jnp.concatenate([field[OUTER:], after], axis=0),
            jnp.concatenate([before, field[: 3 * OUTER]], axis=0),
        )

    phase, heat, along_rows, along_columns = stencil(*fields, neighbours)
    first = known(info, CORE) == 0.0
    along = jnp.where(first, along_rows, along_columns)
    value = jnp.where(first, phase, heat)
    polar = conductivity_contrast(raw, phase) * (known(info, SLOPE) + gradient_gain * along)
    return [[array[c * OUTER : (c + 1) * OUTER] for c in range(4)] for array in (polar, value)]


def pack(columns):
    lane = lax.broadcasted_iota(jnp.int32, (OUTER, TILE_COLS), 1)
    packed = jnp.zeros((OUTER, TILE_COLS), jnp.float32)
    for slot, column in enumerate((2, 3, 0, 1)):
        start = SHIFT + (HALF if column >= 2 else 0)
        moved = roll(columns[column], SLAB * slot - start, 1)
        packed = jnp.where(lane // SLAB == slot, moved, packed)
    return packed


def columns_forward_kernel(
    info, data, porous, phase, heat, order, every, twist_cos, twist_sin, out, parcel
):
    polar, value = edge_polar(info, data)
    for f, field in enumerate((porous, phase, heat)):
        parcel[f * EDGE : (f + 1) * EDGE, :] = field[:EDGE, :]
    parcel[3 * EDGE :, :] = pack(value)
    packed = dot(halves(pack(polar)), (order[0], order[1]))
    lane = lax.broadcasted_iota(jnp.int32, (OUTER, TILE_COLS), 1)
    outer = (lane < SHIFT) | (lane >= TILE_COLS - SHIFT)
    parts = []
    for s in range(SLAB):
        around = roll(packed, -EDGE * s - SHIFT, 1)
        parts.append(jnp.where(outer, around, data[pl.ds(s, OUTER, stride=BLOCK), :]))
    rows = jnp.concatenate(parts, axis=1)
    first = slice(128, 128 + 2 * OUTER)
    spread = dot((every[0, first, :OUTER], every[1, first, :OUTER]), halves(rows))
    cosine, sine = twist_cos[...], twist_sin[...]
    real, imag = [], []
    for s in range(SLAB):
        part = slice(s * 128, (s + 1) * 128)
        re, im = spread[:OUTER, part], spread[OUTER:, part]
        real.append(re * cosine + im * sine)
        imag.append(im * cosine - re * sine)
    for g in range(4):
        span = slice(g * 8, (g + 1) * 8)
        re = jnp.concatenate([part[span] for part in real], axis=0)
        im = jnp.concatenate([part[span] for part in imag], axis=0)
        both = jnp.concatenate([re, im], axis=1)
        final = dot((every[0, :128], every[1, :128]), halves(both), ((1,), (1,)))
        out[pl.ds(2 * g, 64, stride=8), :] = final[:64]
        out[pl.ds(2 * g + 1, 64, stride=8), :] = final[64:]


def columns_backward_kernel(info, data, mine, below, every, twist_cos, twist_sin, out):
    real, imag = [], []
    for g in range(4):
        span = slice(g * 8, (g + 1) * 8)
        both = jnp.concatenate(
            [data[pl.ds(2 * g, 64, stride=8), :], data[pl.ds(2 * g + 1, 64, stride=8), :]], axis=0
        )
        spread = dot(halves(both.T), (every[0, :128], every[1, :128]))
        re = spread[:, :128].reshape(SLAB, 8, 128)
        im = spread[:, 128:].reshape(SLAB, 8, 128)
        cosine, sine = twist_cos[span][None], twist_sin[span][None]
        real.append(re * cosine - im * sine)
        imag.append(im * cosine + re * sine)
    stacked = jnp.concatenate(
        [jnp.concatenate([part[s] for part in real + imag], axis=0) for s in range(SLAB)], axis=1
    )
    first = slice(128 + 2 * OUTER, 128 + 3 * OUTER)
    final = dot((every[0, first, : 2 * OUTER], every[1, first, : 2 * OUTER]), halves(stacked))
    for s in range(SLAB):
        part = final[:, s * 128 : (s + 1) * 128]
        out[pl.ds(s, OUTER, stride=BACK), :] = known(info, SLOPE) - part
    lane = lax.broadcasted_iota(jnp.int32, (SLAB, TILE_COLS), 1)
    late = (known(info, PLACE) == 0.0) & (lane % SLAB < SHIFT)
    for core in range(2):
        rows = pl.ds(3 * EDGE + core, SLAB, stride=2)
        start = core * SLAB * BACK + SLAB
        out[pl.ds(start, SLAB, stride=BACK), :] = jnp.where(late, below[rows, :], mine[rows, :])


def place_kernel(data, fields, columns, phase, heat, gradient):
    lane = lax.broadcasted_iota(jnp.int32, (SLAB, TILE_COLS), 1)
    row = lax.broadcasted_iota(jnp.int32, (SLAB, TILE_COLS), 0)
    own = (lane % SLAB == row) & (lane < 4 * SLAB)
    lane = lax.broadcasted_iota(jnp.int32, (TILE_ROWS, TILE_COLS), 1)
    outer = (lane < SHIFT) | (lane >= TILE_COLS - SHIFT)
    for f, out in enumerate((phase, heat)):
        start = f * SLAB * BACK
        values = data[pl.ds(start + SLAB, SLAB, stride=BACK), :]
        spread = jnp.concatenate(
            [jnp.where(own, values[x : x + 1], 0.0) for x in range(SLAB)], axis=0
        )
        high, rest = halves(spread)
        low = (spread - high.astype(jnp.float32) - rest.astype(jnp.float32)).astype(jnp.bfloat16)
        parts = [
            lax.dot_general(
                part, columns[...], (((1,), (0,)), ((), ())), preferred_element_type=jnp.float32
            )
            for part in (high, rest, low)
        ]
        edge = roll(parts[0] + (parts[1] + parts[2]), -SHIFT, 0)
        out[...] = jnp.where(outer, edge, fields[f])
        for s in range(SLAB):
            gradient[pl.ds(f * TILE_ROWS + s, SLAB, stride=SLAB), :] = data[
                pl.ds(start + s, SLAB, stride=BACK), :
            ]


def wave_numbers(info):
    shape = (CHIPS, 128)
    lane = lax.broadcasted_iota(jnp.int32, shape, 1)
    row_freq = lax.broadcasted_iota(jnp.int32, shape, 0) + CHIPS * (lane // 8)
    row_wave = jnp.where(row_freq >= ROWS // 2, row_freq - ROWS, row_freq).astype(jnp.float32)
    col_wave = 8.0 * known(info, CHIP) + (lane % 8).astype(jnp.float32)
    wave = jnp.where(known(info, CORE) == 0.0, row_wave, col_wave)
    return row_freq, row_wave, col_wave, wave


def rows_forward_kernel(info, data, first, second, twist_cos, twist_sin, out):
    real = data[pl.ds(0, CHIPS, stride=2), :]
    imag = data[pl.ds(1, CHIPS, stride=2), :]
    spread = dot((first[0], first[1]), halves(jnp.concatenate([real, imag], axis=1)))
    re = spread[:CHIPS, :128] + spread[CHIPS:, 128:]
    im = spread[:CHIPS, 128:] - spread[CHIPS:, :128]
    cosine, sine = twist_cos[...], twist_sin[...]
    turned = jnp.concatenate([re * cosine + im * sine, im * cosine - re * sine], axis=1)
    final = dot(halves(turned), (second[0], second[1]))
    wave = wave_numbers(info)[3]
    out[:CHIPS] = wave * final[:, :128]
    out[CHIPS:] = wave * final[:, 128:]


def rows_backward_kernel(info, mine, other, first, second, twist_cos, twist_sin, out):
    row_freq, row_wave, col_wave, wave = wave_numbers(info)
    valid = (
        (row_freq != ROWS // 2)
        & (col_wave != COLS // 2)
        & ((row_freq != 0) | (col_wave != 0.0))
    )
    denom = reference_conduct * jnp.maximum(row_wave * row_wave + col_wave * col_wave, 1.0)
    weight = jnp.where(col_wave == 0.0, 1.0, 2.0) / (ROWS * COLS)
    coef = jnp.where(valid, weight * wave / denom, 0.0)
    along = mine[...] + other[...]
    green = jnp.concatenate([coef * along[:CHIPS], coef * along[CHIPS:]], axis=1)
    spread = dot(halves(green), (second[0], second[1]))
    re, im = spread[:, :128], spread[:, 128:]
    cosine, sine = twist_cos[...], twist_sin[...]
    turned = jnp.concatenate([re * cosine - im * sine, im * cosine + re * sine], axis=1)
    final = dot((first[0], first[1]), halves(turned))
    out[pl.ds(0, CHIPS, stride=2), :] = final[:CHIPS, :128] - final[CHIPS:, 128:]
    out[pl.ds(1, CHIPS, stride=2), :] = final[:CHIPS, 128:] + final[CHIPS:, :128]


def exchange(array, axes, tile):
    blocks = array.reshape((array.size // tile // 128, tile, 128))
    return lax.all_to_all(blocks, axes, split_axis=0, concat_axis=0, tiled=True)


def shift(block, axes, count, step):
    return lax.ppermute(block, axes, [(i, (i + step) % count) for i in range(count)])


def bottom_strip(voxel, wetted, heat):
    bottom = [array[:, TILE_ROWS - EDGE :] for array in (voxel, wetted, heat)]
    parts = bottom[0].astype(jnp.float32), bottom[1].astype(jnp.float32), -bottom[2]
    which = lax.broadcasted_iota(jnp.int32, (3, EDGE, TILE_COLS), 0)
    return jnp.where(which == 0, parts[0], jnp.where(which == 1, parts[1], parts[2]))


def body(voxel, wetted, heat, slope):
    gx_size, gy_size = ROWS // TILE_ROWS, COLS // TILE_COLS
    indices = (GX_AXES, GY_AXES, CHIP_AXES, "core", ("x", "y_lo"))
    place = jnp.stack([lax.axis_index(axes) for axes in indices])
    (shared, order, columns), (row_to, row_back) = column_tables(), row_tables()
    tile = (TILE_ROWS, TILE_COLS)
    above = shift(bottom_strip(voxel, wetted, heat), GX_AXES, gx_size, 1)
    porous = voxel[0].astype(jnp.float32)
    phase = porous * wetted[0].astype(jnp.float32)
    heat = heat[0]
    (info,) = call(prepare_kernel, [(8, 128)], place.astype(jnp.int32), slope, smem=(0, 1))
    shapes = [(OUTER * BLOCK, 128), (2,) + tile]
    polar, fields = call(polar_kernel, shapes, info, porous, phase, heat)
    polar, fields = call(
        first_slab_kernel, shapes, info, porous, phase, heat, above, polar, fields
    )
    slab = exchange(polar, GY_AXES, 4).reshape(-1, 128)
    spec, parcel = call(
        columns_forward_kernel, [(2 * CHIPS, 128), (3 * EDGE + OUTER, 128)],
        info, slab, porous, phase, heat, order, *shared,
    )
    spec = exchange(spec, CHIP_AXES, 2).reshape(-1, 128)
    (mine,) = call(rows_forward_kernel, [(2 * CHIPS, 128)], info, spec, *row_to)
    other = lax.ppermute(mine, "core", [(0, 1), (1, 0)])
    (green,) = call(rows_backward_kernel, [(2 * CHIPS, 128)], info, mine, other, *row_back)
    green, parcel = lax.optimization_barrier((green, parcel))
    below = shift(parcel, GX_AXES, gx_size, -1)
    green = exchange(green, CHIP_AXES, 2).reshape(-1, 128)
    (fields,) = call(tail_kernel, [(2,) + tile], info, porous, phase, heat, fields, below)
    green, below, fields = lax.optimization_barrier((green, below, fields))
    (answer,) = call(
        columns_backward_kernel, [(OUTER * BACK, 128)], info, green, parcel, below, *shared
    )
    answer = exchange(answer, ("core", "x", "y_lo"), 1).reshape(-1, 128)
    phase, heat, gradient = call(
        place_kernel, [tile, tile, (2 * TILE_ROWS, TILE_COLS)], answer, fields, columns
    )
    return (phase[None], heat[None], gradient.reshape((2, 1) + tile))


def solution(mesh):
    fine = Mesh(mesh.devices.reshape(tuple(SIZES.values())), tuple(SIZES))
    in_specs = (P(None, GX_AXES, GY_AXES),) * 3 + (P(),)
    out_specs = (P(None, GX_AXES, GY_AXES),) * 2 + (P(None, None, GX_AXES, GY_AXES),)
    return jax.shard_map(body, mesh=fine, in_specs=in_specs, out_specs=out_specs, check_vma=False)
```

```python
import functools
import math

import jax
import jax.numpy as jnp
import numpy as np
from jax import lax
from jax.experimental import pallas as pl
from jax.experimental.pallas import tpu as pltpu
from jax.sharding import Mesh
from jax.sharding import PartitionSpec as P

solid_conduct = 1.7
gas_conduct = 0.026
liquid_conduct = 0.6
reference_conduct = 0.863
step_grad = 0.1
step_well = 0.3
step_drive = 0.2
step_heat = 0.12
latent_heat = 0.5
gradient_gain = 0.5

TILE_ROWS = 256
TILE_COLS = 128
EDGE = 8
SHIFT = 2
TALL = TILE_ROWS + EDGE
WIDE = 384
OUTER = 32
SLAB = 16
SPAN = 20
HALF = 64
BLOCK = SLAB + 4
BACK = SLAB + 1
CHIPS = 256
COLS = 4096
ROWS = 4096
CORE_MAJOR = np.arange(OUTER).reshape(-1, 2).T.reshape(-1)
SIZES = {"z": 8, "y_hi": 2, "x": 4, "y_lo": 4, "core": 2}
GX_AXES, GY_AXES = ("z", "y_hi"), ("x", "y_lo", "core")
CHIP_AXES = ("y_lo", "x", "y_hi", "z")
CHIP_ORDER = np.arange(CHIPS).reshape(8, 2, 4, 4).transpose(3, 2, 1, 0).reshape(-1)
VMEM = pl.BlockSpec(memory_space=pltpu.VMEM)
SMEM = pl.BlockSpec(memory_space=pltpu.SMEM)


def halves(array):
    high = array.astype(jnp.bfloat16)
    return high, (array - high.astype(jnp.float32)).astype(jnp.bfloat16)


def dot(left, right, contract=((1,), (0,))):
    def product(x, y):
        return lax.dot_general(x, y, (contract, ((), ())), preferred_element_type=jnp.float32)

    (left_high, left_low), (right_high, right_low) = left, right
    return product(left_high, right_high) + (
        product(left_high, right_low) + product(left_low, right_high)
    )


def call(kernel, outs, *args, smem=(), scratch=()):
    shapes = [jax.ShapeDtypeStruct(shape, jnp.float32) for shape in outs]
    spaces = [SMEM if i in smem else VMEM for i in range(len(args))]
    return pl.pallas_call(
        kernel,
        out_shape=shapes,
        in_specs=spaces,
        out_specs=[VMEM] * len(outs),
        scratch_shapes=list(scratch),
        compiler_params=pltpu.CompilerParams(vmem_limit_bytes=32 * 1024 * 1024),
    )(*args)


def angles(left, right, length):
    product = np.outer(np.arange(left), np.asarray(right)) % length
    return 2.0 * math.pi / length * product


def table(array):
    return jnp.asarray(np.asarray(array, dtype=np.float32))


def split_table(array):
    array = np.asarray(array, dtype=np.float32)
    high = array.astype(jnp.bfloat16)
    low = (array - high.astype(np.float32)).astype(jnp.bfloat16)
    return jnp.asarray(np.stack([high, low]))


def column_tables():
    first = angles(OUTER, range(OUTER), OUTER)
    cosine, sine = np.cos(first), np.sin(first)
    second = angles(64, range(128), 128)
    twist = angles(OUTER, range(128), COLS)
    mix = np.block([[np.cos(second), np.sin(second)], [-np.sin(second), np.cos(second)]])
    slot, s = np.divmod(np.arange(4 * SLAB), SLAB)
    order = np.zeros((128, 128))
    order[np.arange(4 * SLAB), EDGE * s + slot] = 1.0
    every = np.zeros((128 + 2 * OUTER + OUTER, 256))
    every[:128] = mix
    every[128 : 128 + 2 * OUTER, :OUTER] = np.concatenate([cosine, -sine], axis=0)
    every[128 + 2 * OUTER :, : 2 * OUTER] = np.concatenate([cosine, -sine], axis=1)[CORE_MAJOR]
    shared = [split_table(every), table(np.cos(twist)), table(np.sin(twist))]
    columns = np.zeros((128, 128))
    columns[np.arange(4 * SLAB), (slot - SHIFT) % TILE_COLS] = 1.0
    return shared, split_table(order), jnp.asarray(columns.astype(jnp.bfloat16))


def row_tables():
    first = angles(CHIPS, range(CHIPS), CHIPS)
    cosine, sine = np.cos(first)[:, CHIP_ORDER], np.sin(first)[:, CHIP_ORDER]
    starts = (np.concatenate([cosine, sine], axis=0), np.concatenate([cosine.T, sine.T], axis=0))
    tables = []
    for shift, sign, start in ((SHIFT, -1.0, starts[0]), (0, 1.0, starts[1])):
        inner = np.arange(SLAB) - shift
        second = angles(SLAB, inner, SLAB)
        twist = np.repeat(angles(CHIPS, inner, ROWS), 8, axis=1)
        cosine, sine = np.kron(np.cos(second), np.eye(8)), sign * np.kron(np.sin(second), np.eye(8))
        if shift:
            cosine, sine = cosine.T, sine.T
        mix = np.block([[cosine, sine], [-sine, cosine]])
        rest = [split_table(mix), table(np.cos(twist)), table(np.sin(twist))]
        tables.append([split_table(start)] + rest)
    return tables


GX, GY, CHIP, CORE, PLACE, SLOPE_X, SLOPE_Y, SLOPE = range(8)


def prepare_kernel(place, slope, info):
    values = [place[i].astype(jnp.float32) for i in range(5)] + [slope[0, 0], slope[0, 1]]
    values.append(jnp.where(place[3] == 0, slope[0, 0], slope[0, 1]))
    row = lax.broadcasted_iota(jnp.int32, info.shape, 0)
    filled = jnp.zeros(info.shape, jnp.float32)
    for i, value in enumerate(values):
        filled = jnp.where(row == i, value, filled)
    info[...] = filled


def known(info, i):
    return info[i : i + 1, :]


def with_above(above, porous, phase, heat):
    tops = (above[0], above[0] * above[1], -above[2])
    return [
        jnp.concatenate([top, field[...]], axis=0) for top, field in zip(tops, (porous, phase, heat))
    ]


def progress(phase, heat, porous, phase_lap, heat_lap):
    well = 2.0 * phase * (1.0 - phase) * (1.0 - 2.0 * phase)
    growth = 30.0 * phase * phase * (1.0 - phase) * (1.0 - phase)
    new_phase = porous * (
        phase + step_grad * phase_lap - step_well * well + step_drive * heat * growth
    )
    new_heat = heat + step_heat * heat_lap - latent_heat * (new_phase - phase)
    return new_phase, new_heat


def stencil(porous, phase, heat, neighbours):
    def laplace(around, field):
        return around[0] + around[1] + around[2] + around[3] - 6.0 * field

    phase_lap, heat_lap = laplace(neighbours(phase), phase), laplace(neighbours(heat), heat)
    phase, heat = progress(phase, heat, porous, phase_lap, heat_lap)
    around = neighbours(heat)
    phase_lap, heat_lap = laplace(neighbours(phase), phase), laplace(around, heat)
    phase, heat = progress(phase, heat, porous, phase_lap, heat_lap)
    return phase, heat, around[0] - around[1], around[2] - around[3]


def roll(field, step, axis):
    return pltpu.roll(field, step % field.shape[axis], axis)


def walled(wall, field):
    return field if wall is None else jnp.where(wall, 0.0, field)


def ring_neighbours(walls):
    def neighbours(field):
        moves = ((-1, 0), (1, 0), (-1, 1), (1, 1))
        return [walled(wall, roll(field, *move)) for move, wall in zip(moves, walls)]

    return neighbours


def conductivity_contrast(porous, phase):
    conduct = (
        porous * (gas_conduct + (liquid_conduct - gas_conduct) * phase)
        + (1.0 - porous) * solid_conduct
    )
    return conduct - reference_conduct


def shifted_rows(field):
    return roll(field, SHIFT - EDGE, 0)[: field.shape[0] - EDGE]


def row_walls(first, row):
    return first & (row == EDGE - 1), first & (row == EDGE)


def polar_blocks(info, talls, slabs, rows, out, fields):
    row = lax.broadcasted_iota(jnp.int32, talls[0].shape, 0)
    walls = row_walls(known(info, GX) == 0.0, row) + (None, None)
    phase_two, heat_two, along_rows, along_columns = stencil(*talls, ring_neighbours(walls))
    fields[0, :rows] = shifted_rows(phase_two)[:rows]
    fields[1, :rows] = shifted_rows(heat_two)[:rows]
    contrast = conductivity_contrast(talls[0], phase_two)
    polars = (
        shifted_rows(contrast * (known(info, SLOPE_X) + gradient_gain * along_rows)),
        shifted_rows(contrast * (known(info, SLOPE_Y) + gradient_gain * along_columns)),
    )
    tall = talls[0].shape[0]
    wide = WIDE if tall == TALL else TILE_COLS
    spare = jnp.zeros((wide - tall, TILE_COLS), jnp.float32)
    sublane = lax.broadcasted_iota(jnp.int32, (EDGE, wide), 0)
    lane = lax.broadcasted_iota(jnp.int32, (EDGE, TILE_COLS), 1)
    low = lax.broadcasted_iota(jnp.int32, (EDGE, TILE_COLS), 0) < 4
    edges = []
    for tall in talls:
        flipped = jnp.concatenate([tall, spare], axis=0).T
        edges.append(jnp.where(sublane < 4, flipped[:EDGE], flipped[TILE_COLS - EDGE :]))
    for x in slabs:
        first = EDGE - 2 * SHIFT + SLAB * x
        windows = [
            roll(edge, f * SPAN - first, 1)[:, :TILE_COLS] for f, edge in enumerate(edges)
        ]
        packed = jnp.where(
            lane < SPAN, windows[0], jnp.where(lane < 2 * SPAN, windows[1], windows[2])
        )
        swapped = roll(packed, 4, 0)
        lower, upper = jnp.where(low, packed, swapped), jnp.where(low, swapped, packed)
        both = jnp.where(lane < HALF, lower, roll(upper, HALF, 1))
        rows = slice(x * SLAB, (x + 1) * SLAB)
        start = 2 * x * BLOCK
        out[start : start + SLAB, :] = polars[0][rows]
        rest = roll(jnp.concatenate([both, polars[1][rows]], axis=0), -4, 0)
        out[start + SLAB : start + 2 * BLOCK, :] = rest


def polar_kernel(info, porous, phase, heat, out, fields):
    nothing = jnp.zeros((3, EDGE, TILE_COLS), jnp.float32)
    talls = with_above(nothing, porous, phase, heat)
    polar_blocks(info, talls, range(1, TILE_ROWS // SLAB), TILE_ROWS, out, fields)


def first_slab_kernel(info, porous, phase, heat, above, blocks, rows, out, fields):
    done = 2 * BLOCK
    out[done:, :] = blocks[done:, :]
    fields[:, EDGE:] = rows[:, EDGE:]
    talls = [tall[: 4 * EDGE] for tall in with_above(above, porous, phase, heat)]
    polar_blocks(info, talls, range(1), EDGE, out, fields)


def tail_kernel(info, porous, phase, heat, fields, parcel, out):
    ends = [
        jnp.concatenate([field[TILE_ROWS - 2 * EDGE :, :], parcel[f * EDGE : (f + 1) * EDGE, :]])
        for f, field in enumerate((porous, phase, heat))
    ]
    row = lax.broadcasted_iota(jnp.int32, ends[0].shape, 0)
    last = known(info, GX) == ROWS // TILE_ROWS - 1
    walls = (last & (row == 2 * EDGE - 1), last & (row == 2 * EDGE), None, None)
    late = lax.broadcasted_iota(jnp.int32, (EDGE, TILE_COLS), 0) >= EDGE - SHIFT
    for f, end in enumerate(stencil(*ends, ring_neighbours(walls))[:2]):
        whole = roll(fields[f], -SHIFT, 0)
        out[f, : TILE_ROWS - EDGE, :] = whole[: TILE_ROWS - EDGE]
        out[f, TILE_ROWS - EDGE :, :] = jnp.where(
            late, end[EDGE : 2 * EDGE], whole[TILE_ROWS - EDGE :]
        )


def edge_polar(info, data):
    raw = jnp.concatenate([data[pl.ds(SLAB + c, OUTER, stride=BLOCK), :] for c in range(4)], axis=0)
    fields = [raw] + [roll(raw, -f * SPAN, 1) for f in (1, 2)]
    lane = lax.broadcasted_iota(jnp.int32, raw.shape, 1)
    row = lane % HALF
    first = known(info, CHIP) == 0.0
    down_wall, up_wall = first & (row == 2 * SHIFT - 1), first & (row == 2 * SHIFT)
    tile = lax.broadcasted_iota(jnp.int32, (OUTER, TILE_COLS), 0)

    def neighbours(field):
        after = walled(tile == OUTER - 1, roll(roll(field[:OUTER], -1, 0), HALF, 1))
        before = walled(tile == 0, roll(roll(field[3 * OUTER :], 1, 0), HALF, 1))
        return (
            walled(down_wall, roll(field, -1, 1)),
            walled(up_wall, roll(field, 1, 1)),
            jnp.concatenate([field[OUTER:], after], axis=0),
            jnp.concatenate([before, field[: 3 * OUTER]], axis=0),
        )

    phase, heat, along_rows, along_columns = stencil(*fields, neighbours)
    first = known(info, CORE) == 0.0
    along = jnp.where(first, along_rows, along_columns)
    value = jnp.where(first, phase, heat)
    polar = conductivity_contrast(raw, phase) * (known(info, SLOPE) + gradient_gain * along)
    return [[array[c * OUTER : (c + 1) * OUTER] for c in range(4)] for array in (polar, value)]


def pack(columns):
    lane = lax.broadcasted_iota(jnp.int32, (OUTER, TILE_COLS), 1)
    packed = jnp.zeros((OUTER, TILE_COLS), jnp.float32)
    for slot, column in enumerate((2, 3, 0, 1)):
        start = SHIFT + (HALF if column >= 2 else 0)
        moved = roll(columns[column], SLAB * slot - start, 1)
        packed = jnp.where(lane // SLAB == slot, moved, packed)
    return packed


def columns_forward_kernel(
    info, data, porous, phase, heat, order, every, twist_cos, twist_sin, out, parcel
):
    polar, value = edge_polar(info, data)
    for f, field in enumerate((porous, phase, heat)):
        parcel[f * EDGE : (f + 1) * EDGE, :] = field[:EDGE, :]
    parcel[3 * EDGE :, :] = pack(value)
    packed = dot(halves(pack(polar)), (order[0], order[1]))
    lane = lax.broadcasted_iota(jnp.int32, (OUTER, TILE_COLS), 1)
    outer = (lane < SHIFT) | (lane >= TILE_COLS - SHIFT)
    parts = []
    for s in range(SLAB):
        parts.append(jnp.where(outer, 0.0, data[pl.ds(s, OUTER, stride=BLOCK), :]))
    rows = jnp.concatenate(parts, axis=1)
    first = slice(128, 128 + 2 * OUTER)
    starts = every[0, first, :OUTER], every[1, first, :OUTER]
    spread = dot(starts, halves(rows))
    edge = dot(starts, halves(packed))
    both_outer = jnp.concatenate([outer, outer], axis=0)
    cosine, sine = twist_cos[...], twist_sin[...]
    real, imag = [], []
    for s in range(SLAB):
        part = slice(s * 128, (s + 1) * 128)
        around = jnp.where(both_outer, roll(edge, -EDGE * s - SHIFT, 1), 0.0)
        whole = spread[:, part] + around
        re, im = whole[:OUTER], whole[OUTER:]
        real.append(re * cosine + im * sine)
        imag.append(im * cosine - re * sine)
    for g in range(4):
        span = slice(g * 8, (g + 1) * 8)
        re = jnp.concatenate([part[span] for part in real], axis=0)
        im = jnp.concatenate([part[span] for part in imag], axis=0)
        both = jnp.concatenate([re, im], axis=1)
        final = dot((every[0, :128], every[1, :128]), halves(both), ((1,), (1,)))
        out[pl.ds(2 * g, 64, stride=8), :] = final[:64]
        out[pl.ds(2 * g + 1, 64, stride=8), :] = final[64:]


def columns_backward_kernel(info, data, mine, below, every, twist_cos, twist_sin, out):
    real, imag = [], []
    for g in range(4):
        span = slice(g * 8, (g + 1) * 8)
        both = jnp.concatenate(
            [data[pl.ds(2 * g, 64, stride=8), :], data[pl.ds(2 * g + 1, 64, stride=8), :]], axis=0
        )
        spread = dot(halves(both.T), (every[0, :128], every[1, :128]))
        re = spread[:, :128].reshape(SLAB, 8, 128)
        im = spread[:, 128:].reshape(SLAB, 8, 128)
        cosine, sine = twist_cos[span][None], twist_sin[span][None]
        real.append(re * cosine - im * sine)
        imag.append(im * cosine + re * sine)
    stacked = jnp.concatenate(
        [jnp.concatenate([part[s] for part in real + imag], axis=0) for s in range(SLAB)], axis=1
    )
    first = slice(128 + 2 * OUTER, 128 + 3 * OUTER)
    final = dot((every[0, first, : 2 * OUTER], every[1, first, : 2 * OUTER]), halves(stacked))
    for s in range(SLAB):
        part = final[:, s * 128 : (s + 1) * 128]
        out[pl.ds(s, OUTER, stride=BACK), :] = known(info, SLOPE) - part
    lane = lax.broadcasted_iota(jnp.int32, (SLAB, TILE_COLS), 1)
    late = (known(info, PLACE) == 0.0) & (lane % SLAB < SHIFT)
    for core in range(2):
        rows = pl.ds(3 * EDGE + core, SLAB, stride=2)
        start = core * SLAB * BACK + SLAB
        out[pl.ds(start, SLAB, stride=BACK), :] = jnp.where(late, below[rows, :], mine[rows, :])


def place_kernel(data, fields, columns, phase, heat, gradient):
    lane = lax.broadcasted_iota(jnp.int32, (SLAB, TILE_COLS), 1)
    row = lax.broadcasted_iota(jnp.int32, (SLAB, TILE_COLS), 0)
    own = (lane % SLAB == row) & (lane < 4 * SLAB)
    lane = lax.broadcasted_iota(jnp.int32, (TILE_ROWS, TILE_COLS), 1)
    outer = (lane < SHIFT) | (lane >= TILE_COLS - SHIFT)
    for f, out in enumerate((phase, heat)):
        start = f * SLAB * BACK
        values = data[pl.ds(start + SLAB, SLAB, stride=BACK), :]
        spread = jnp.concatenate(
            [jnp.where(own, values[x : x + 1], 0.0) for x in range(SLAB)], axis=0
        )
        high, rest = halves(spread)
        low = (spread - high.astype(jnp.float32) - rest.astype(jnp.float32)).astype(jnp.bfloat16)
        parts = [
            lax.dot_general(
                part, columns[...], (((1,), (0,)), ((), ())), preferred_element_type=jnp.float32
            )
            for part in (high, rest, low)
        ]
        edge = roll(parts[0] + (parts[1] + parts[2]), -SHIFT, 0)
        out[...] = jnp.where(outer, edge, fields[f])
        for s in range(SLAB):
            gradient[pl.ds(f * TILE_ROWS + s, SLAB, stride=SLAB), :] = data[
                pl.ds(start + s, SLAB, stride=BACK), :
            ]


def wave_numbers(info):
    shape = (CHIPS, 128)
    lane = lax.broadcasted_iota(jnp.int32, shape, 1)
    row_freq = lax.broadcasted_iota(jnp.int32, shape, 0) + CHIPS * (lane // 8)
    row_wave = jnp.where(row_freq >= ROWS // 2, row_freq - ROWS, row_freq).astype(jnp.float32)
    col_wave = 8.0 * known(info, CHIP) + (lane % 8).astype(jnp.float32)
    wave = jnp.where(known(info, CORE) == 0.0, row_wave, col_wave)
    return row_freq, row_wave, col_wave, wave


def rows_forward_kernel(info, data, first, second, twist_cos, twist_sin, out):
    real = data[pl.ds(0, CHIPS, stride=2), :]
    imag = data[pl.ds(1, CHIPS, stride=2), :]
    spread = dot((first[0], first[1]), halves(jnp.concatenate([real, imag], axis=1)))
    re = spread[:CHIPS, :128] + spread[CHIPS:, 128:]
    im = spread[:CHIPS, 128:] - spread[CHIPS:, :128]
    cosine, sine = twist_cos[...], twist_sin[...]
    turned = jnp.concatenate([re * cosine + im * sine, im * cosine - re * sine], axis=1)
    final = dot(halves(turned), (second[0], second[1]))
    wave = wave_numbers(info)[3]
    out[:CHIPS] = wave * final[:, :128]
    out[CHIPS:] = wave * final[:, 128:]


def rows_backward_kernel(info, mine, other, first, second, twist_cos, twist_sin, out):
    row_freq, row_wave, col_wave, wave = wave_numbers(info)
    valid = (
        (row_freq != ROWS // 2)
        & (col_wave != COLS // 2)
        & ((row_freq != 0) | (col_wave != 0.0))
    )
    denom = reference_conduct * jnp.maximum(row_wave * row_wave + col_wave * col_wave, 1.0)
    weight = jnp.where(col_wave == 0.0, 1.0, 2.0) / (ROWS * COLS)
    coef = jnp.where(valid, weight * wave / denom, 0.0)
    along = mine[...] + other[...]
    green = jnp.concatenate([coef * along[:CHIPS], coef * along[CHIPS:]], axis=1)
    spread = dot(halves(green), (second[0], second[1]))
    re, im = spread[:, :128], spread[:, 128:]
    cosine, sine = twist_cos[...], twist_sin[...]
    turned = jnp.concatenate([re * cosine - im * sine, im * cosine + re * sine], axis=1)
    final = dot((first[0], first[1]), halves(turned))
    out[pl.ds(0, CHIPS, stride=2), :] = final[:CHIPS, :128] - final[CHIPS:, 128:]
    out[pl.ds(1, CHIPS, stride=2), :] = final[:CHIPS, 128:] + final[CHIPS:, :128]


def exchange(array, axes, tile):
    blocks = array.reshape((array.size // tile // 128, tile, 128))
    return lax.all_to_all(blocks, axes, split_axis=0, concat_axis=0, tiled=True)


def shift(block, axes, count, step):
    return lax.ppermute(block, axes, [(i, (i + step) % count) for i in range(count)])


def bottom_strip(voxel, wetted, heat):
    bottom = [array[:, TILE_ROWS - EDGE :] for array in (voxel, wetted, heat)]
    parts = bottom[0].astype(jnp.float32), bottom[1].astype(jnp.float32), -bottom[2]
    which = lax.broadcasted_iota(jnp.int32, (3, EDGE, TILE_COLS), 0)
    return jnp.where(which == 0, parts[0], jnp.where(which == 1, parts[1], parts[2]))


def body(voxel, wetted, heat, slope):
    gx_size, gy_size = ROWS // TILE_ROWS, COLS // TILE_COLS
    indices = (GX_AXES, GY_AXES, CHIP_AXES, "core", ("x", "y_lo"))
    place = jnp.stack([lax.axis_index(axes) for axes in indices])
    (shared, order, columns), (row_to, row_back) = column_tables(), row_tables()
    tile = (TILE_ROWS, TILE_COLS)
    above = shift(bottom_strip(voxel, wetted, heat), GX_AXES, gx_size, 1)
    porous = voxel[0].astype(jnp.float32)
    phase = porous * wetted[0].astype(jnp.float32)
    heat = heat[0]
    (info,) = call(prepare_kernel, [(8, 128)], place.astype(jnp.int32), slope, smem=(0, 1))
    shapes = [(OUTER * BLOCK, 128), (2,) + tile]
    polar, fields = call(polar_kernel, shapes, info, porous, phase, heat)
    polar, fields = call(
        first_slab_kernel, shapes, info, porous, phase, heat, above, polar, fields
    )
    slab = exchange(polar, GY_AXES, 4).reshape(-1, 128)
    spec, parcel = call(
        columns_forward_kernel, [(2 * CHIPS, 128), (3 * EDGE + OUTER, 128)],
        info, slab, porous, phase, heat, order, *shared,
    )
    spec = exchange(spec, CHIP_AXES, 2).reshape(-1, 128)
    (mine,) = call(rows_forward_kernel, [(2 * CHIPS, 128)], info, spec, *row_to)
    other = lax.ppermute(mine, "core", [(0, 1), (1, 0)])
    (green,) = call(rows_backward_kernel, [(2 * CHIPS, 128)], info, mine, other, *row_back)
    green, parcel = lax.optimization_barrier((green, parcel))
    below = shift(parcel, GX_AXES, gx_size, -1)
    green = exchange(green, CHIP_AXES, 2).reshape(-1, 128)
    (fields,) = call(tail_kernel, [(2,) + tile], info, porous, phase, heat, fields, below)
    green, below, fields = lax.optimization_barrier((green, below, fields))
    (answer,) = call(
        columns_backward_kernel, [(OUTER * BACK, 128)], info, green, parcel, below, *shared
    )
    answer = exchange(answer, ("core", "x", "y_lo"), 1).reshape(-1, 128)
    phase, heat, gradient = call(
        place_kernel, [tile, tile, (2 * TILE_ROWS, TILE_COLS)], answer, fields, columns
    )
    return (phase[None], heat[None], gradient.reshape((2, 1) + tile))


def solution(mesh):
    fine = Mesh(mesh.devices.reshape(tuple(SIZES.values())), tuple(SIZES))
    in_specs = (P(None, GX_AXES, GY_AXES),) * 3 + (P(),)
    out_specs = (P(None, GX_AXES, GY_AXES),) * 2 + (P(None, None, GX_AXES, GY_AXES),)
    return jax.shard_map(body, mesh=fine, in_specs=in_specs, out_specs=out_specs, check_vma=False)
```

```python
import functools
import math

import jax
import jax.numpy as jnp
import numpy as np
from jax import lax
from jax.experimental import pallas as pl
from jax.experimental.pallas import tpu as pltpu
from jax.sharding import Mesh
from jax.sharding import PartitionSpec as P

solid_conduct = 1.7
gas_conduct = 0.026
liquid_conduct = 0.6
reference_conduct = 0.863
step_grad = 0.1
step_well = 0.3
step_drive = 0.2
step_heat = 0.12
latent_heat = 0.5
gradient_gain = 0.5

TILE_ROWS = 256
TILE_COLS = 128
EDGE = 8
SHIFT = 2
TALL = TILE_ROWS + EDGE
WIDE = 384
OUTER = 32
SLAB = 16
SPAN = 20
HALF = 64
BLOCK = SLAB + 4
BACK = SLAB + 1
CHIPS = 256
COLS = 4096
ROWS = 4096
CORE_MAJOR = np.arange(OUTER).reshape(-1, 2).T.reshape(-1)
SIZES = {"z": 8, "y_hi": 2, "x": 4, "y_lo": 4, "core": 2}
GX_AXES, GY_AXES = ("z", "y_hi"), ("x", "y_lo", "core")
CHIP_AXES = ("y_lo", "x", "y_hi", "z")
CHIP_ORDER = np.arange(CHIPS).reshape(8, 2, 4, 4).transpose(3, 2, 1, 0).reshape(-1)
VMEM = pl.BlockSpec(memory_space=pltpu.VMEM)
SMEM = pl.BlockSpec(memory_space=pltpu.SMEM)


def halves(array):
    high = array.astype(jnp.bfloat16)
    return high, (array - high.astype(jnp.float32)).astype(jnp.bfloat16)


def dot(left, right, contract=((1,), (0,))):
    def product(x, y):
        return lax.dot_general(x, y, (contract, ((), ())), preferred_element_type=jnp.float32)

    (left_high, left_low), (right_high, right_low) = left, right
    return product(left_high, right_high) + (
        product(left_high, right_low) + product(left_low, right_high)
    )


def call(kernel, outs, *args, smem=(), scratch=()):
    shapes = [jax.ShapeDtypeStruct(shape, jnp.float32) for shape in outs]
    spaces = [SMEM if i in smem else VMEM for i in range(len(args))]
    return pl.pallas_call(
        kernel,
        out_shape=shapes,
        in_specs=spaces,
        out_specs=[VMEM] * len(outs),
        scratch_shapes=list(scratch),
        compiler_params=pltpu.CompilerParams(vmem_limit_bytes=32 * 1024 * 1024),
    )(*args)


def angles(left, right, length):
    product = np.outer(np.arange(left), np.asarray(right)) % length
    return 2.0 * math.pi / length * product


def table(array):
    return jnp.asarray(np.asarray(array, dtype=np.float32))


def split_table(array):
    array = np.asarray(array, dtype=np.float32)
    high = array.astype(jnp.bfloat16)
    low = (array - high.astype(np.float32)).astype(jnp.bfloat16)
    return jnp.asarray(np.stack([high, low]))


def column_tables():
    first = angles(OUTER, range(OUTER), OUTER)
    cosine, sine = np.cos(first), np.sin(first)
    second = angles(64, range(128), 128)
    twist = angles(OUTER, range(128), COLS)
    mix = np.block([[np.cos(second), np.sin(second)], [-np.sin(second), np.cos(second)]])
    slot, s = np.divmod(np.arange(4 * SLAB), SLAB)
    order = np.zeros((128, 128))
    order[np.arange(4 * SLAB), EDGE * s + slot] = 1.0
    every = np.zeros((128 + 2 * OUTER + OUTER, 256))
    every[:128] = mix
    every[128 : 128 + 2 * OUTER, :OUTER] = np.concatenate([cosine, -sine], axis=0)
    every[128 + 2 * OUTER :, : 2 * OUTER] = np.concatenate([cosine, -sine], axis=1)[CORE_MAJOR]
    shared = [split_table(every), table(np.cos(twist)), table(np.sin(twist))]
    columns = np.zeros((128, 128))
    columns[np.arange(4 * SLAB), (slot - SHIFT) % TILE_COLS] = 1.0
    return shared, split_table(order), jnp.asarray(columns.astype(jnp.bfloat16))


def row_tables():
    first = angles(CHIPS, range(CHIPS), CHIPS)
    cosine, sine = np.cos(first)[:, CHIP_ORDER], np.sin(first)[:, CHIP_ORDER]
    starts = (np.concatenate([cosine, sine], axis=0), np.concatenate([cosine.T, sine.T], axis=0))
    tables = []
    for shift, sign, start in ((SHIFT, -1.0, starts[0]), (0, 1.0, starts[1])):
        inner = np.arange(SLAB) - shift
        second = angles(SLAB, inner, SLAB)
        twist = np.repeat(angles(CHIPS, inner, ROWS), 8, axis=1)
        cosine, sine = np.kron(np.cos(second), np.eye(8)), sign * np.kron(np.sin(second), np.eye(8))
        if shift:
            cosine, sine = cosine.T, sine.T
        mix = np.block([[cosine, sine], [-sine, cosine]])
        rest = [split_table(mix), table(np.cos(twist)), table(np.sin(twist))]
        tables.append([split_table(start)] + rest)
    return tables


GX, GY, CHIP, CORE, PLACE, SLOPE_X, SLOPE_Y, SLOPE = range(8)


def prepare_kernel(place, slope, info):
    values = [place[i].astype(jnp.float32) for i in range(5)] + [slope[0, 0], slope[0, 1]]
    values.append(jnp.where(place[3] == 0, slope[0, 0], slope[0, 1]))
    row = lax.broadcasted_iota(jnp.int32, info.shape, 0)
    filled = jnp.zeros(info.shape, jnp.float32)
    for i, value in enumerate(values):
        filled = jnp.where(row == i, value, filled)
    info[...] = filled


def known(info, i):
    return info[i : i + 1, :]


def with_above(above, porous, phase, heat):
    tops = (above[0], above[0] * above[1], -above[2])
    return [
        jnp.concatenate([top, field[...]], axis=0) for top, field in zip(tops, (porous, phase, heat))
    ]


def progress(phase, heat, porous, phase_lap, heat_lap):
    well = 2.0 * phase * (1.0 - phase) * (1.0 - 2.0 * phase)
    growth = 30.0 * phase * phase * (1.0 - phase) * (1.0 - phase)
    new_phase = porous * (
        phase + step_grad * phase_lap - step_well * well + step_drive * heat * growth
    )
    new_heat = heat + step_heat * heat_lap - latent_heat * (new_phase - phase)
    return new_phase, new_heat


def stencil(porous, phase, heat, neighbours):
    def laplace(around, field):
        return around[0] + around[1] + around[2] + around[3] - 6.0 * field

    phase_lap, heat_lap = laplace(neighbours(phase), phase), laplace(neighbours(heat), heat)
    phase, heat = progress(phase, heat, porous, phase_lap, heat_lap)
    around = neighbours(heat)
    phase_lap, heat_lap = laplace(neighbours(phase), phase), laplace(around, heat)
    phase, heat = progress(phase, heat, porous, phase_lap, heat_lap)
    return phase, heat, around[0] - around[1], around[2] - around[3]


def roll(field, step, axis):
    return pltpu.roll(field, step % field.shape[axis], axis)


def walled(wall, field):
    return field if wall is None else jnp.where(wall, 0.0, field)


def ring_neighbours(walls):
    def neighbours(field):
        moves = ((-1, 0), (1, 0), (-1, 1), (1, 1))
        return [walled(wall, roll(field, *move)) for move, wall in zip(moves, walls)]

    return neighbours


def conductivity_contrast(porous, phase):
    conduct = (
        porous * (gas_conduct + (liquid_conduct - gas_conduct) * phase)
        + (1.0 - porous) * solid_conduct
    )
    return conduct - reference_conduct


def shifted_rows(field):
    return roll(field, SHIFT - EDGE, 0)[: field.shape[0] - EDGE]


def row_walls(first, row):
    return first & (row == EDGE - 1), first & (row == EDGE)


def polar_blocks(info, talls, slabs, rows, out, fields):
    row = lax.broadcasted_iota(jnp.int32, talls[0].shape, 0)
    walls = row_walls(known(info, GX) == 0.0, row) + (None, None)
    phase_two, heat_two, along_rows, along_columns = stencil(*talls, ring_neighbours(walls))
    fields[0, :rows] = shifted_rows(phase_two)[:rows]
    fields[1, :rows] = shifted_rows(heat_two)[:rows]
    contrast = conductivity_contrast(talls[0], phase_two)
    polars = (
        shifted_rows(contrast * (known(info, SLOPE_X) + gradient_gain * along_rows)),
        shifted_rows(contrast * (known(info, SLOPE_Y) + gradient_gain * along_columns)),
    )
    tall = talls[0].shape[0]
    wide = WIDE if tall == TALL else TILE_COLS
    spare = jnp.zeros((wide - tall, TILE_COLS), jnp.float32)
    sublane = lax.broadcasted_iota(jnp.int32, (EDGE, wide), 0)
    lane = lax.broadcasted_iota(jnp.int32, (EDGE, TILE_COLS), 1)
    low = lax.broadcasted_iota(jnp.int32, (EDGE, TILE_COLS), 0) < 4
    edges = []
    for tall in talls:
        flipped = jnp.concatenate([tall, spare], axis=0).T
        edges.append(jnp.where(sublane < 4, flipped[:EDGE], flipped[TILE_COLS - EDGE :]))
    for x in slabs:
        first = EDGE - 2 * SHIFT + SLAB * x
        windows = [
            roll(edge, f * SPAN - first, 1)[:, :TILE_COLS] for f, edge in enumerate(edges)
        ]
        packed = jnp.where(
            lane < SPAN, windows[0], jnp.where(lane < 2 * SPAN, windows[1], windows[2])
        )
        swapped = roll(packed, 4, 0)
        lower, upper = jnp.where(low, packed, swapped), jnp.where(low, swapped, packed)
        both = jnp.where(lane < HALF, lower, roll(upper, HALF, 1))
        rows = slice(x * SLAB, (x + 1) * SLAB)
        start = 2 * x * BLOCK
        out[start : start + SLAB, :] = polars[0][rows]
        rest = roll(jnp.concatenate([both, polars[1][rows]], axis=0), -4, 0)
        out[start + SLAB : start + 2 * BLOCK, :] = rest


def polar_kernel(info, porous, phase, heat, out, fields):
    nothing = jnp.zeros((3, EDGE, TILE_COLS), jnp.float32)
    talls = with_above(nothing, porous, phase, heat)
    polar_blocks(info, talls, range(1, TILE_ROWS // SLAB), TILE_ROWS, out, fields)


def first_slab_kernel(info, porous, phase, heat, above, blocks, rows, out, fields):
    done = 2 * BLOCK
    out[done:, :] = blocks[done:, :]
    fields[:, EDGE:] = rows[:, EDGE:]
    talls = [tall[: 4 * EDGE] for tall in with_above(above, porous, phase, heat)]
    polar_blocks(info, talls, range(1), EDGE, out, fields)


def tail_kernel(info, porous, phase, heat, fields, parcel, out):
    ends = [
        jnp.concatenate([field[TILE_ROWS - 2 * EDGE :, :], roll(parcel[:EDGE, :], -f * SHIFT, 0)])
        for f, field in enumerate((porous, phase, heat))
    ]
    row = lax.broadcasted_iota(jnp.int32, ends[0].shape, 0)
    last = known(info, GX) == ROWS // TILE_ROWS - 1
    walls = (last & (row == 2 * EDGE - 1), last & (row == 2 * EDGE), None, None)
    late = lax.broadcasted_iota(jnp.int32, (EDGE, TILE_COLS), 0) >= EDGE - SHIFT
    for f, end in enumerate(stencil(*ends, ring_neighbours(walls))[:2]):
        whole = roll(fields[f], -SHIFT, 0)
        out[f, : TILE_ROWS - EDGE, :] = whole[: TILE_ROWS - EDGE]
        out[f, TILE_ROWS - EDGE :, :] = jnp.where(
            late, end[EDGE : 2 * EDGE], whole[TILE_ROWS - EDGE :]
        )


def edge_polar(info, data):
    raw = jnp.concatenate([data[pl.ds(SLAB + c, OUTER, stride=BLOCK), :] for c in range(4)], axis=0)
    fields = [raw] + [roll(raw, -f * SPAN, 1) for f in (1, 2)]
    lane = lax.broadcasted_iota(jnp.int32, raw.shape, 1)
    row = lane % HALF
    first = known(info, CHIP) == 0.0
    down_wall, up_wall = first & (row == 2 * SHIFT - 1), first & (row == 2 * SHIFT)
    tile = lax.broadcasted_iota(jnp.int32, (OUTER, TILE_COLS), 0)

    def neighbours(field):
        after = walled(tile == OUTER - 1, roll(roll(field[:OUTER], -1, 0), HALF, 1))
        before = walled(tile == 0, roll(roll(field[3 * OUTER :], 1, 0), HALF, 1))
        return (
            walled(down_wall, roll(field, -1, 1)),
            walled(up_wall, roll(field, 1, 1)),
            jnp.concatenate([field[OUTER:], after], axis=0),
            jnp.concatenate([before, field[: 3 * OUTER]], axis=0),
        )

    phase, heat, along_rows, along_columns = stencil(*fields, neighbours)
    first = known(info, CORE) == 0.0
    along = jnp.where(first, along_rows, along_columns)
    value = jnp.where(first, phase, heat)
    polar = conductivity_contrast(raw, phase) * (known(info, SLOPE) + gradient_gain * along)
    return [[array[c * OUTER : (c + 1) * OUTER] for c in range(4)] for array in (polar, value)]


def pack(columns):
    lane = lax.broadcasted_iota(jnp.int32, (OUTER, TILE_COLS), 1)
    packed = jnp.zeros((OUTER, TILE_COLS), jnp.float32)
    for slot, column in enumerate((2, 3, 0, 1)):
        start = SHIFT + (HALF if column >= 2 else 0)
        moved = roll(columns[column], SLAB * slot - start, 1)
        packed = jnp.where(lane // SLAB == slot, moved, packed)
    return packed


def columns_forward_kernel(
    info, data, porous, phase, heat, order, every, twist_cos, twist_sin, out, parcel
):
    polar, value = edge_polar(info, data)
    row = lax.broadcasted_iota(jnp.int32, (EDGE, TILE_COLS), 0)
    tops = [roll(field[:EDGE, :], f * SHIFT, 0) for f, field in enumerate((porous, phase, heat))]
    parcel[:EDGE, :] = jnp.where(row < SHIFT, tops[0], jnp.where(row < 2 * SHIFT, tops[1], tops[2]))
    parcel[EDGE:, :] = pack(value)
    packed = dot(halves(pack(polar)), (order[0], order[1]))
    lane = lax.broadcasted_iota(jnp.int32, (OUTER, TILE_COLS), 1)
    outer = (lane < SHIFT) | (lane >= TILE_COLS - SHIFT)
    parts = []
    for s in range(SLAB):
        parts.append(jnp.where(outer, 0.0, data[pl.ds(s, OUTER, stride=BLOCK), :]))
    rows = jnp.concatenate(parts, axis=1)
    first = slice(128, 128 + 2 * OUTER)
    starts = every[0, first, :OUTER], every[1, first, :OUTER]
    spread = dot(starts, halves(rows))
    edge = dot(starts, halves(packed))
    both_outer = jnp.concatenate([outer, outer], axis=0)
    cosine, sine = twist_cos[...], twist_sin[...]
    real, imag = [], []
    for s in range(SLAB):
        part = slice(s * 128, (s + 1) * 128)
        around = jnp.where(both_outer, roll(edge, -EDGE * s - SHIFT, 1), 0.0)
        whole = spread[:, part] + around
        re, im = whole[:OUTER], whole[OUTER:]
        real.append(re * cosine + im * sine)
        imag.append(im * cosine - re * sine)
    for g in range(4):
        span = slice(g * 8, (g + 1) * 8)
        re = jnp.concatenate([part[span] for part in real], axis=0)
        im = jnp.concatenate([part[span] for part in imag], axis=0)
        both = jnp.concatenate([re, im], axis=1)
        final = dot((every[0, :128], every[1, :128]), halves(both), ((1,), (1,)))
        out[pl.ds(2 * g, 64, stride=8), :] = final[:64]
        out[pl.ds(2 * g + 1, 64, stride=8), :] = final[64:]


def columns_backward_kernel(info, data, mine, below, every, twist_cos, twist_sin, out):
    real, imag = [], []
    for g in range(4):
        span = slice(g * 8, (g + 1) * 8)
        both = jnp.concatenate(
            [data[pl.ds(2 * g, 64, stride=8), :], data[pl.ds(2 * g + 1, 64, stride=8), :]], axis=0
        )
        spread = dot(halves(both.T), (every[0, :128], every[1, :128]))
        re = spread[:, :128].reshape(SLAB, 8, 128)
        im = spread[:, 128:].reshape(SLAB, 8, 128)
        cosine, sine = twist_cos[span][None], twist_sin[span][None]
        real.append(re * cosine - im * sine)
        imag.append(im * cosine + re * sine)
    stacked = jnp.concatenate(
        [jnp.concatenate([part[s] for part in real + imag], axis=0) for s in range(SLAB)], axis=1
    )
    first = slice(128 + 2 * OUTER, 128 + 3 * OUTER)
    final = dot((every[0, first, : 2 * OUTER], every[1, first, : 2 * OUTER]), halves(stacked))
    for s in range(SLAB):
        part = final[:, s * 128 : (s + 1) * 128]
        out[pl.ds(s, OUTER, stride=BACK), :] = known(info, SLOPE) - part
    lane = lax.broadcasted_iota(jnp.int32, (SLAB, TILE_COLS), 1)
    late = (known(info, PLACE) == 0.0) & (lane % SLAB < SHIFT)
    for core in range(2):
        rows = pl.ds(EDGE + core, SLAB, stride=2)
        start = core * SLAB * BACK + SLAB
        out[pl.ds(start, SLAB, stride=BACK), :] = jnp.where(late, below[rows, :], mine[rows, :])


def place_kernel(data, fields, columns, phase, heat, gradient):
    lane = lax.broadcasted_iota(jnp.int32, (SLAB, TILE_COLS), 1)
    row = lax.broadcasted_iota(jnp.int32, (SLAB, TILE_COLS), 0)
    own = (lane % SLAB == row) & (lane < 4 * SLAB)
    lane = lax.broadcasted_iota(jnp.int32, (TILE_ROWS, TILE_COLS), 1)
    outer = (lane < SHIFT) | (lane >= TILE_COLS - SHIFT)
    for f, out in enumerate((phase, heat)):
        start = f * SLAB * BACK
        values = data[pl.ds(start + SLAB, SLAB, stride=BACK), :]
        spread = jnp.concatenate(
            [jnp.where(own, values[x : x + 1], 0.0) for x in range(SLAB)], axis=0
        )
        high, rest = halves(spread)
        low = (spread - high.astype(jnp.float32) - rest.astype(jnp.float32)).astype(jnp.bfloat16)
        parts = [
            lax.dot_general(
                part, columns[...], (((1,), (0,)), ((), ())), preferred_element_type=jnp.float32
            )
            for part in (high, rest, low)
        ]
        edge = roll(parts[0] + (parts[1] + parts[2]), -SHIFT, 0)
        out[...] = jnp.where(outer, edge, fields[f])
        for s in range(SLAB):
            gradient[pl.ds(f * TILE_ROWS + s, SLAB, stride=SLAB), :] = data[
                pl.ds(start + s, SLAB, stride=BACK), :
            ]


def wave_numbers(info):
    shape = (CHIPS, 128)
    lane = lax.broadcasted_iota(jnp.int32, shape, 1)
    row_freq = lax.broadcasted_iota(jnp.int32, shape, 0) + CHIPS * (lane // 8)
    row_wave = jnp.where(row_freq >= ROWS // 2, row_freq - ROWS, row_freq).astype(jnp.float32)
    col_wave = 8.0 * known(info, CHIP) + (lane % 8).astype(jnp.float32)
    wave = jnp.where(known(info, CORE) == 0.0, row_wave, col_wave)
    return row_freq, row_wave, col_wave, wave


def rows_forward_kernel(info, data, first, second, twist_cos, twist_sin, out):
    real = data[pl.ds(0, CHIPS, stride=2), :]
    imag = data[pl.ds(1, CHIPS, stride=2), :]
    spread = dot((first[0], first[1]), halves(jnp.concatenate([real, imag], axis=1)))
    re = spread[:CHIPS, :128] + spread[CHIPS:, 128:]
    im = spread[:CHIPS, 128:] - spread[CHIPS:, :128]
    cosine, sine = twist_cos[...], twist_sin[...]
    turned = jnp.concatenate([re * cosine + im * sine, im * cosine - re * sine], axis=1)
    final = dot(halves(turned), (second[0], second[1]))
    wave = wave_numbers(info)[3]
    out[:CHIPS] = wave * final[:, :128]
    out[CHIPS:] = wave * final[:, 128:]


def rows_backward_kernel(info, mine, other, first, second, twist_cos, twist_sin, out):
    row_freq, row_wave, col_wave, wave = wave_numbers(info)
    valid = (
        (row_freq != ROWS // 2)
        & (col_wave != COLS // 2)
        & ((row_freq != 0) | (col_wave != 0.0))
    )
    denom = reference_conduct * jnp.maximum(row_wave * row_wave + col_wave * col_wave, 1.0)
    weight = jnp.where(col_wave == 0.0, 1.0, 2.0) / (ROWS * COLS)
    coef = jnp.where(valid, weight * wave / denom, 0.0)
    along = mine[...] + other[...]
    green = jnp.concatenate([coef * along[:CHIPS], coef * along[CHIPS:]], axis=1)
    spread = dot(halves(green), (second[0], second[1]))
    re, im = spread[:, :128], spread[:, 128:]
    cosine, sine = twist_cos[...], twist_sin[...]
    turned = jnp.concatenate([re * cosine - im * sine, im * cosine + re * sine], axis=1)
    final = dot((first[0], first[1]), halves(turned))
    out[pl.ds(0, CHIPS, stride=2), :] = final[:CHIPS, :128] - final[CHIPS:, 128:]
    out[pl.ds(1, CHIPS, stride=2), :] = final[:CHIPS, 128:] + final[CHIPS:, :128]


def exchange(array, axes, tile):
    blocks = array.reshape((array.size // tile // 128, tile, 128))
    return lax.all_to_all(blocks, axes, split_axis=0, concat_axis=0, tiled=True)


def shift(block, axes, count, step):
    return lax.ppermute(block, axes, [(i, (i + step) % count) for i in range(count)])


def bottom_strip(voxel, wetted, heat):
    bottom = [array[:, TILE_ROWS - EDGE :] for array in (voxel, wetted, heat)]
    parts = bottom[0].astype(jnp.float32), bottom[1].astype(jnp.float32), -bottom[2]
    which = lax.broadcasted_iota(jnp.int32, (3, EDGE, TILE_COLS), 0)
    return jnp.where(which == 0, parts[0], jnp.where(which == 1, parts[1], parts[2]))


def body(voxel, wetted, heat, slope):
    gx_size, gy_size = ROWS // TILE_ROWS, COLS // TILE_COLS
    indices = (GX_AXES, GY_AXES, CHIP_AXES, "core", ("x", "y_lo"))
    place = jnp.stack([lax.axis_index(axes) for axes in indices])
    (shared, order, columns), (row_to, row_back) = column_tables(), row_tables()
    tile = (TILE_ROWS, TILE_COLS)
    above = shift(bottom_strip(voxel, wetted, heat), GX_AXES, gx_size, 1)
    porous = voxel[0].astype(jnp.float32)
    phase = porous * wetted[0].astype(jnp.float32)
    heat = heat[0]
    (info,) = call(prepare_kernel, [(8, 128)], place.astype(jnp.int32), slope, smem=(0, 1))
    shapes = [(OUTER * BLOCK, 128), (2,) + tile]
    polar, fields = call(polar_kernel, shapes, info, porous, phase, heat)
    polar, fields = call(
        first_slab_kernel, shapes, info, porous, phase, heat, above, polar, fields
    )
    slab = exchange(polar, GY_AXES, 4).reshape(-1, 128)
    spec, parcel = call(
        columns_forward_kernel, [(2 * CHIPS, 128), (EDGE + OUTER, 128)],
        info, slab, porous, phase, heat, order, *shared,
    )
    spec = exchange(spec, CHIP_AXES, 2).reshape(-1, 128)
    (mine,) = call(rows_forward_kernel, [(2 * CHIPS, 128)], info, spec, *row_to)
    other = lax.ppermute(mine, "core", [(0, 1), (1, 0)])
    (green,) = call(rows_backward_kernel, [(2 * CHIPS, 128)], info, mine, other, *row_back)
    green, parcel = lax.optimization_barrier((green, parcel))
    below = shift(parcel, GX_AXES, gx_size, -1)
    green = exchange(green, CHIP_AXES, 2).reshape(-1, 128)
    (fields,) = call(tail_kernel, [(2,) + tile], info, porous, phase, heat, fields, below)
    green, below, fields = lax.optimization_barrier((green, below, fields))
    (answer,) = call(
        columns_backward_kernel, [(OUTER * BACK, 128)], info, green, parcel, below, *shared
    )
    answer = exchange(answer, ("core", "x", "y_lo"), 1).reshape(-1, 128)
    phase, heat, gradient = call(
        place_kernel, [tile, tile, (2 * TILE_ROWS, TILE_COLS)], answer, fields, columns
    )
    return (phase[None], heat[None], gradient.reshape((2, 1) + tile))


def solution(mesh):
    fine = Mesh(mesh.devices.reshape(tuple(SIZES.values())), tuple(SIZES))
    in_specs = (P(None, GX_AXES, GY_AXES),) * 3 + (P(),)
    out_specs = (P(None, GX_AXES, GY_AXES),) * 2 + (P(None, None, GX_AXES, GY_AXES),)
    return jax.shard_map(body, mesh=fine, in_specs=in_specs, out_specs=out_specs, check_vma=False)
```
